128 devices in a mesh: dp: 8 (over y_hi, x), ctx: 16 (over z, y_lo, core).
Axes of the slice: x: 4, y: 4 (y_hi: 2, y_lo: 2; y = y_hi * 2 + y_lo), z: 4, core: 2. Of those that a mesh axis runs over, the one named last changes fastest.
Arguments:
- patches: bfloat16 [16384, 1280], P(('dp', 'ctx')), may hold values from -45 to 45
- vision_gain: float32 [1280], replicated, may hold values from 0.25 to 1.75
- vision_bias: float32 [1280], replicated, may hold values from -1.75 to 1.75
- up_weight: bfloat16 [2560, 1280], P(('dp', 'ctx')), may hold values from -0.15625 to 0.15625
- down_weight: bfloat16 [2560, 1280], P(('dp', 'ctx')), may hold values from -0.125 to 0.125
- merge_gain: float32 [1280], replicated, may hold values from 0.25 to 1.75
- merge_bias: float32 [1280], replicated, may hold values from -1.75 to 1.75
- merge_weight: bfloat16 [5120, 8192], P(None, 'dp'), may hold values from -0.078125 to 0.078125
- attn_gain: float32 [8192], replicated, may hold values from 0.25 to 1.75
- query_weight: bfloat16 [8192, 4096], P(None, 'dp'), may hold values from -0.1875 to 0.1875
- kv_weight: bfloat16 [2, 8192, 1024], P(None, None, 'dp'), may hold values from -0.0625 to 0.0625
- text_query: bfloat16 [10240, 4096], P('ctx', 'dp'), may hold values from -120 to 120, as said below
- text_kv: bfloat16 [2, 10240, 1024], P(None, 'ctx', 'dp'), may hold values from -6 to 6, as said below
- doc_ids: int32 [10240], P('ctx'), may hold values from 0 to 3, never falling along the last dimension, each value on 1 to 5120 neighbouring positions
- image_sizes: int32 [128, 4], P(('dp', 'ctx')), may hold values from 1 to 16, as said below
- image_offsets: int32 [128, 4], P(('dp', 'ctx')), may hold values from 0 to 10239, as said below
Outputs:
- context: bfloat16 [10240, 4096], P('ctx', 'dp')
The draws below stay inside these ranges and needn't reach their ends.
Inputs may be any that keep to these rules, and one draw needn't show every extreme that they name: `image_sizes`: the 4 images of one device hold 32 merged rows together, and one of them holds exactly 16. `image_offsets`: images never intersect; each lies within the 640 positions of one index of ctx; the images of one index of ctx (over all of dp) put at most 32 rows into the positions of one index of ctx, and in every draw some index of ctx takes exactly 32 rows from every index. `text_query`: rows at image positions are not read. `text_kv`: rows at image positions are not read.
All inputs are finite; a program needn't handle non-finite values.
Results may differ from the reference program's by a relative error of at most 0.035.
Values may be sent and summed in bfloat16 or wider, within the bound.
No kernel may reach another device: no remote copies, remote signals or barrier semaphores. Data moves between devices by JAX's collectives and lax.ppermute only.
A program may use at most 128 MiB of HBM per device.

```python
import math
import jax
import jax.numpy as jnp
import numpy as np
from jax import lax

DV = 1280
VH = 2560
D = 8192
HEADS = 32
KV_HEADS = 8
HEAD_DIM = 128
MOST = 16
IMG_DEV = 4
TOK_DEV = 640
DOCS = 4
MW = 5120
MERGED_DEV = 32
PATCHES = 16384
TOKENS = 10240
DOC_MOST = 5120
N_DP = 8
N_CTX = 16


def paired_keys(key):
    key = jax.random.fold_in(key, 101)
    key_values = jnp.clip(jax.random.normal(key, (TOKENS, KV_HEADS * HEAD_DIM), jnp.float32), -4.0, 4.0)
    stride = TOKENS // 16
    row_ids = jnp.arange(TOKENS)
    strength = 10.0 + 20.0 * (row_ids // stride).astype(jnp.float32) / 15.0
    trailing = row_ids % stride == stride // 2 - 1
    following = jnp.roll(key_values, -1, axis=0)
    shrink = 1.0 - 2.0 / (jnp.roll(strength, -1) * math.sqrt(HEAD_DIM))
    paired = jnp.where(trailing[:, None], following * shrink[:, None], key_values)
    return paired


def image_layout(key):
    key = jax.random.fold_in(key, 202)
    streams = jax.random.split(key, 7)
    half = N_DP // 2
    slot_width = TOK_DEV // (2 * N_CTX)
    cut_low = jax.random.randint(streams[0], (N_DP, N_CTX), 1, MOST)
    cut_high = jax.random.randint(streams[1], (N_DP, N_CTX), 1, MOST - 1)
    cut_high = jnp.where(cut_high >= cut_low, cut_high + 1, cut_high)
    lower = jnp.minimum(cut_low, cut_high)
    upper = jnp.maximum(cut_low, cut_high)
    smaller = jnp.stack([lower, upper - lower, MOST - upper], axis=-1)
    big_pair = jax.random.randint(streams[2], (half, N_CTX), 0, IMG_DEV)
    big_slot = jnp.concatenate([big_pair, big_pair], axis=0)
    slot_ids = jnp.arange(IMG_DEV)
    other_index = jnp.clip(slot_ids - (slot_ids > big_slot[..., None]).astype(jnp.int32), 0, 2)
    sizes = jnp.where(slot_ids == big_slot[..., None], MOST, jnp.take_along_axis(smaller, other_index, axis=-1))
    pair_index = (jnp.arange(N_DP) % half)[:, None, None] * IMG_DEV + slot_ids[None, None, :]
    column_ids = jnp.arange(N_CTX)
    orders = jax.vmap(lambda single: jax.random.permutation(single, N_CTX))(jax.random.split(streams[3], N_CTX))
    crowded = jax.random.randint(streams[4], (), 0, N_CTX)
    moved = crowded - orders[column_ids, big_pair[0]]
    orders = (orders + moved[:, None]) % N_CTX
    owners = orders[column_ids[None, :, None], pair_index]
    places = jax.vmap(lambda single: jax.random.permutation(single, 2 * N_CTX))(jax.random.split(streams[5], N_CTX))
    side = (jnp.arange(N_DP) >= half).astype(jnp.int32)[:, None, None]
    sub_slot = places[owners, 2 * column_ids[None, :, None] + side]
    starts = jax.random.randint(streams[6], (N_DP, N_CTX, IMG_DEV), 0, slot_width - sizes + 1)
    offsets = owners * TOK_DEV + sub_slot * slot_width + starts
    return (sizes.reshape(N_DP * N_CTX, IMG_DEV).astype(jnp.int32), offsets.reshape(N_DP * N_CTX, IMG_DEV).astype(jnp.int32))


def draw_image_sizes(key, part):
    return image_layout(key)[0]


def draw_image_offsets(key, part):
    return image_layout(key)[1]


def draw_patches(key, part):
    key = jax.random.fold_in(key, 3)
    row_key, column_key, value_key = jax.random.split(key, 3)
    row_scale = jnp.exp(jax.random.uniform(row_key, (PATCHES, 1), jnp.float32, math.log(0.3), math.log(3.0)))
    column_scale = jnp.exp(jax.random.uniform(column_key, (1, DV), jnp.float32, math.log(0.3), math.log(3.0)))
    base = jnp.clip(jax.random.normal(value_key, (PATCHES, DV), jnp.float32), -5.0, 5.0)
    return (base * row_scale * column_scale).astype(jnp.bfloat16)


def draw_text_query(key, part):
    key = jax.random.fold_in(key, 5)
    query = 3.0 * jnp.clip(jax.random.normal(key, (TOKENS, HEADS * HEAD_DIM), jnp.float32), -4.0, 4.0)
    return query.astype(jnp.bfloat16)


def draw_text_kv(key, part):
    paired = paired_keys(key)
    key = jax.random.fold_in(key, 7)
    value_rows = 1.5 * jnp.clip(jax.random.normal(key, (TOKENS, KV_HEADS * HEAD_DIM), jnp.float32), -4.0, 4.0)
    return jnp.stack([paired, value_rows]).astype(jnp.bfloat16)


def block_scale(own_key, shape, cuts, smallest, top_value):
    gain, own = 1.0, jax.random.fold_in(own_key, 6)
    for axis_at, shards_of in cuts:
        draws = jnp.exp(jax.random.uniform(jax.random.fold_in(own, axis_at), (shards_of,), jnp.float32, smallest / len(cuts), top_value / len(cuts)))
        gain = gain * jnp.repeat(draws, shape[axis_at] // shards_of).reshape([-1 if axis == axis_at else 1 for axis in range(len(shape))])
    return gain


def profile(number_of, total, reach, slope):
    weights = [(1 << 20) // math.isqrt(grade ** slope) + 1 for grade in range(2, number_of + 1)]
    spare, counts = total - reach - (number_of - 1), [1] * (number_of - 1)
    while spare > 0:
        candidates = [i for i in range(number_of - 1) if counts[i] < reach]
        mass, budget = sum([weights[i] for i in candidates]), spare
        for i in candidates:
            more = min(reach - counts[i], max(1, budget * weights[i] // mass), spare)
            counts[i] = counts[i] + more
            spare = spare - more
    return np.array([reach] + counts)


def ragged_sizes(rng, count, total, limit, lean):
    if count == 2:
        one = jax.random.randint(rng, (), max(1, total - limit), min(limit, total - 1) + 1)
        return jnp.stack([one, total - one])
    lengths = jnp.asarray(profile(count, total, limit, lean), jnp.int32)
    twos = (count - 1) // 2
    donor, taker = lengths[1:1 + 2 * twos:2], lengths[2:2 + 2 * twos:2]
    margin = jnp.minimum(donor - 1, limit - taker)
    passed = jax.random.randint(jax.random.fold_in(rng, 1), (twos,), 0, 1 << 20) % (margin + 1)
    lengths = lengths.at[1:1 + 2 * twos:2].set(donor - passed).at[2:2 + 2 * twos:2].set(taker + passed)
    return lengths[jax.random.permutation(jax.random.fold_in(rng, 2), count)]


def noise(stream_key, extent, scale, reach, shards=(), held_as=jnp.bfloat16):
    entries = jax.random.normal(stream_key, extent, jnp.float32) * scale
    if len(shards) > 0:
        entries = block_scale(stream_key, extent, shards, -0.22, 0.18) * entries
    return jnp.clip(entries, min=-reach, max=reach).astype(held_as)


def setup_inputs(seed: int = 0) -> dict:
    seeds = jax.random.split(jax.random.key(seed), 17)
    patches = draw_patches(jax.random.fold_in(seeds[16], 71), 0)
    vision_gain = jnp.clip(1.0 + 0.15 * jax.random.normal(seeds[1], (DV,), jnp.float32), 0.25, 1.75)
    vision_bias = noise(seeds[2], (DV,), 0.3, 1.75, (), jnp.float32)
    up_weight = noise(seeds[3], (VH, DV), DV ** -0.5, 0.15625, ((0, 128),))
    down_weight = noise(seeds[4], (VH, DV), VH ** -0.5, 0.125, ((0, 128),))
    merge_gain = jnp.clip(1.0 + 0.15 * jax.random.normal(seeds[5], (DV,), jnp.float32), 0.25, 1.75)
    merge_bias = noise(seeds[6], (DV,), 0.3, 1.75, (), jnp.float32)
    merge_weight = noise(seeds[7], (MW, D), MW ** -0.5, 0.078125, ((1, 8),))
    attn_gain = jnp.clip(1.0 + 0.15 * jax.random.normal(seeds[8], (D,), jnp.float32), 0.25, 1.75)
    query_weight = noise(seeds[9], (D, HEADS * HEAD_DIM), (D // 9) ** -0.5, 0.1875, ((1, 8),))
    kv_weight = noise(seeds[10], (2, D, KV_HEADS * HEAD_DIM), D ** -0.5, 0.0625, ((2, 8),))
    text_query = draw_text_query(jax.random.fold_in(seeds[16], 71), 0)
    text_kv = draw_text_kv(jax.random.fold_in(seeds[16], 71), 0)
    doc_ids = jnp.searchsorted(jnp.cumsum(ragged_sizes(seeds[13], DOCS, TOKENS, DOC_MOST, 0)), jnp.arange(TOKENS), side="right").astype(jnp.int32)
    image_sizes = draw_image_sizes(jax.random.fold_in(seeds[16], 71), 0)
    image_offsets = draw_image_offsets(jax.random.fold_in(seeds[16], 71), 0)
    return {"patches": patches, "vision_gain": vision_gain, "vision_bias": vision_bias, "up_weight": up_weight, "down_weight": down_weight, "merge_gain": merge_gain, "merge_bias": merge_bias, "merge_weight": merge_weight, "attn_gain": attn_gain, "query_weight": query_weight, "kv_weight": kv_weight, "text_query": text_query, "text_kv": text_kv, "doc_ids": doc_ids, "image_sizes": image_sizes, "image_offsets": image_offsets}


MASKED_SCORE = -1e+30
EPSILON = 1e-06

def layer_norm(rows_in, norm_gain, norm_bias):
    values = rows_in.astype(jnp.float32)
    center = values - lax.optimization_barrier(jnp.mean(values, axis=-1, keepdims=True))
    spread = lax.optimization_barrier(jnp.mean(center * center, axis=-1, keepdims=True))
    return (center * lax.rsqrt(spread + EPSILON) * norm_gain + norm_bias).astype(jnp.bfloat16)

def quick_gelu(values):
    return values * jax.nn.sigmoid(1.702 * values)

def rms_scaled(rows_in, norm_gain):
    values = rows_in.astype(jnp.float32)
    mean_square = lax.optimization_barrier(jnp.mean(values * values, axis=-1, keepdims=True))
    return (values * lax.rsqrt(mean_square + EPSILON) * norm_gain).astype(jnp.bfloat16)

def row_positions(size_table, offset_table, row_count):
    image_ends = jnp.cumsum(size_table, axis=1, dtype=jnp.int32)
    image_starts = image_ends - size_table
    within = jnp.arange(row_count, dtype=jnp.int32)[None, :, None]
    inside = (within >= image_starts[:, None, :]) & (within < image_ends[:, None, :])
    placed = offset_table[:, None, :] - image_starts[:, None, :] + within
    return lax.optimization_barrier(jnp.sum(jnp.where(inside, placed, 0), axis=2, dtype=jnp.int32)).astype(jnp.int32)

def attend(running, queries, key_block, value_block, visible, score_scale):
    row_peak, row_total, accumulated = running
    scores = jnp.einsum('qkgd,tkd->qkgt', queries.astype(jnp.float32), key_block.astype(jnp.float32)) * score_scale
    visible_mask = visible[:, None, None, :]
    scores = jnp.where(visible_mask, scores, MASKED_SCORE)
    new_peak = jnp.maximum(row_peak, lax.optimization_barrier(jnp.max(scores, axis=-1)))
    weights = jnp.where(visible_mask, jnp.exp(scores - new_peak[..., None]), 0.0)
    rescale = jnp.exp(row_peak - new_peak)
    row_total = row_total * rescale + lax.optimization_barrier(jnp.sum(weights, axis=-1))
    weights_low = lax.optimization_barrier(weights.astype(jnp.bfloat16))
    blended = jnp.einsum('qkgt,tkd->qkgd', weights_low.astype(jnp.float32), value_block.astype(jnp.float32))
    return (new_peak, row_total, accumulated * rescale[..., None] + blended)

def reference(patches, vision_gain, vision_bias, up_weight, down_weight, merge_gain, merge_bias, merge_weight, attn_gain, query_weight, kv_weight, text_query, text_kv, doc_ids, image_sizes, image_offsets):
    vision_width = patches.shape[1]
    normed = layer_norm(patches, vision_gain, vision_bias)
    hidden = quick_gelu(lax.dot_general(normed, up_weight, (((1,), (1,)), ((), ())), preferred_element_type=jnp.float32)).astype(jnp.bfloat16)
    branch = jnp.dot(hidden, down_weight, preferred_element_type=jnp.float32)
    vision = (patches.astype(jnp.float32) + branch).astype(jnp.bfloat16)
    merged_in = layer_norm(vision, merge_gain, merge_bias).reshape(-1, 4 * vision_width)
    merged = jnp.dot(merged_in, merge_weight, preferred_element_type=jnp.float32).astype(jnp.bfloat16)
    ready_rows = rms_scaled(merged, attn_gain)
    image_query = jnp.dot(ready_rows, query_weight, preferred_element_type=jnp.float32).astype(jnp.bfloat16)
    image_key = jnp.dot(ready_rows, kv_weight[0], preferred_element_type=jnp.float32).astype(jnp.bfloat16)
    image_value = jnp.dot(ready_rows, kv_weight[1], preferred_element_type=jnp.float32).astype(jnp.bfloat16)
    positions = row_positions(image_sizes, image_offsets, MERGED_DEV).reshape(-1)
    queries = text_query.at[positions].set(image_query)
    key_rows = text_kv[0].at[positions].set(image_key)
    value_rows = text_kv[1].at[positions].set(image_value)
    group_size = HEADS // KV_HEADS
    score_scale = 1.0 / math.sqrt(HEAD_DIM)
    block_count = TOKENS // TOK_DEV
    query_blocks = queries.reshape(block_count, TOK_DEV, KV_HEADS, group_size, HEAD_DIM)
    key_blocks = key_rows.reshape(block_count, TOK_DEV, KV_HEADS, HEAD_DIM)
    value_blocks = value_rows.reshape(block_count, TOK_DEV, KV_HEADS, HEAD_DIM)
    doc_blocks = doc_ids.reshape(block_count, TOK_DEV)
    block_ids = jnp.arange(block_count, dtype=jnp.int32)
    offsets_in = jnp.arange(TOK_DEV, dtype=jnp.int32)

    def one_block(query_index):
        block_queries = query_blocks[query_index]
        query_doc = doc_blocks[query_index]
        query_place = query_index * TOK_DEV + offsets_in
        initial = (jnp.full((TOK_DEV, KV_HEADS, group_size), MASKED_SCORE, jnp.float32), jnp.zeros((TOK_DEV, KV_HEADS, group_size), jnp.float32), jnp.zeros((TOK_DEV, KV_HEADS, group_size, HEAD_DIM), jnp.float32))

        def key_step(running, inputs):
            key_block, value_block, key_doc, key_index = inputs
            key_place = key_index * TOK_DEV + offsets_in
            visible = (query_place[:, None] >= key_place[None, :]) & (query_doc[:, None] == key_doc[None, :])
            running = lax.cond(jnp.any(visible), lambda holding: attend(holding, block_queries, key_block, value_block, visible, score_scale), lambda holding: holding, running)
            return (running, None)
        running, unused = lax.scan(key_step, initial, (key_blocks, value_blocks, doc_blocks, block_ids))
        row_peak, row_total, accumulated = running
        return (accumulated / row_total[..., None]).reshape(TOK_DEV, HEADS * HEAD_DIM).astype(jnp.bfloat16)
    return lax.map(one_block, block_ids).reshape(TOKENS, HEADS * HEAD_DIM)
```

```python
import math

import jax
import jax.numpy as jnp
import numpy as np
from jax import lax
from jax.experimental import pallas as pl
from jax.experimental.pallas import tpu as pltpu
from jax.sharding import Mesh
from jax.sharding import PartitionSpec as P

HEAD_DIM = 128
MOST = 16
SEQ = 640
REACH = 8
WINDOW = SEQ * (REACH + 1)
KEY_BLOCK = 512
PADDED = -(-WINDOW // KEY_BLOCK) * KEY_BLOCK
QUERY_BLOCK = 128
GROUP = 4
IMAGES = 512
CAPACITY = 32

MASKED_SCORE = -1e30
LOWEST_PEAK = -1e29
EPSILON = 1e-06
DP = ("yh", "x")
CTX = ("z", "yl", "c")


def layer_norm(rows_in, norm_gain, norm_bias):
    values = rows_in.astype(jnp.float32)
    center = values - jnp.mean(values, axis=-1, keepdims=True)
    spread = jnp.mean(center * center, axis=-1, keepdims=True)
    return (center * lax.rsqrt(spread + EPSILON) * norm_gain + norm_bias).astype(jnp.bfloat16)


def quick_gelu(values):
    return values * jax.nn.sigmoid(1.702 * values)


def row_positions(size_table, offset_table, row_count):
    image_ends = jnp.cumsum(size_table, axis=1, dtype=jnp.int32)
    image_starts = image_ends - size_table
    within = jnp.arange(row_count, dtype=jnp.int32)[None, :, None]
    inside = (within >= image_starts[:, None, :]) & (within < image_ends[:, None, :])
    placed = offset_table[:, None, :] - image_starts[:, None, :] + within
    return jnp.sum(jnp.where(inside, placed, 0), axis=2, dtype=jnp.int32)


def gather_by_exchange(block, axes, count):
    return lax.all_to_all(
        jnp.broadcast_to(block[None], (count,) + block.shape), axes, split_axis=0, concat_axis=0
    )


def swap(rows, axis):
    return lax.ppermute(rows, axis, [(0, 1), (1, 0)])


def attention_kernel(
    info,
    image_src,
    image_dst,
    image_len,
    query_ref,
    low_ref,
    image_ref,
    text_ref,
    out_ref,
    text_held,
    key_wide,
    value_wide,
    image_key,
    image_value,
    key_held,
    value_held,
    sem,
):
    window_start = pl.multiple_of(info[0], SEQ)
    query_offset = info[1]
    copy = pltpu.make_async_copy(text_ref.at[pl.ds(window_start, WINDOW), :], text_held, sem)
    copy.start()

    def widen_image(step, unused):
        rows = pl.ds(pl.multiple_of(step * 256, 256), 256)
        image_key[rows, :] = image_ref[rows, :HEAD_DIM].astype(jnp.float32)
        image_value[rows, :] = image_ref[rows, HEAD_DIM:].astype(jnp.float32)
        return unused

    lax.fori_loop(0, 16, widen_image, 0)
    copy.wait()

    def widen_text(step, unused):
        rows = pl.ds(pl.multiple_of(step * 320, 320), 320)
        key_wide[rows, :] = text_held[rows, :HEAD_DIM].astype(jnp.float32)
        value_wide[rows, :] = text_held[rows, HEAD_DIM:].astype(jnp.float32)
        return unused

    lax.fori_loop(0, WINDOW // 320, widen_text, 0)
    row_in = lax.broadcasted_iota(jnp.int32, (MOST, HEAD_DIM), 0)

    def place(image, unused):
        target = image_dst[image]

        @pl.when((target >= 0) & (target < WINDOW))
        def _():
            origin = image_src[image]
            taken = row_in < image_len[image]
            rows = pl.ds(target, MOST)
            key_wide[rows, :] = jnp.where(taken, image_key[pl.ds(origin, MOST), :], key_wide[rows, :])
            value_wide[rows, :] = jnp.where(
                taken, image_value[pl.ds(origin, MOST), :], value_wide[rows, :]
            )

        return unused

    lax.fori_loop(0, IMAGES, place, 0)

    def narrow(step, unused):
        rows = pl.ds(pl.multiple_of(step * 320, 320), 320)
        key_held[rows, :] = key_wide[rows, :].astype(jnp.bfloat16)
        value_held[rows, :] = value_wide[rows, :].astype(jnp.bfloat16)
        return unused

    lax.fori_loop(0, WINDOW // 320, narrow, 0)
    if PADDED > WINDOW:
        key_held[WINDOW:, :] = jnp.zeros((PADDED - WINDOW, HEAD_DIM), jnp.bfloat16)
        value_held[WINDOW:, :] = jnp.zeros((PADDED - WINDOW, HEAD_DIM), jnp.bfloat16)

    tall = GROUP * QUERY_BLOCK
    to_power = math.log2(math.e) / math.sqrt(HEAD_DIM)
    row_at = lax.broadcasted_iota(jnp.int32, (QUERY_BLOCK, 1), 0)

    def query_step(block, unused):
        rows = pl.ds(pl.multiple_of(block * QUERY_BLOCK, QUERY_BLOCK), QUERY_BLOCK)
        first = query_offset + block * QUERY_BLOCK
        queries = jnp.concatenate(
            [query_ref[rows, h * HEAD_DIM : (h + 1) * HEAD_DIM] for h in range(GROUP)], axis=0
        )
        low_rows = jnp.concatenate([low_ref[rows, :]] * GROUP, axis=0)
        high_rows = jnp.concatenate([row_at + first] * GROUP, axis=0)
        low_first = info[2 + 2 * block]
        low_last = info[3 + 2 * block]
        begin = low_first // KEY_BLOCK
        end = (first + QUERY_BLOCK - 1) // KEY_BLOCK + 1
        clear_begin = jnp.minimum((low_last + KEY_BLOCK - 1) // KEY_BLOCK, end)
        clear_end = jnp.maximum((first + 1) // KEY_BLOCK, clear_begin)

        def key_step(at, running, masked):
            peak, total, gathered = running
            keys_at = pl.ds(pl.multiple_of(at * KEY_BLOCK, KEY_BLOCK), KEY_BLOCK)
            scores = lax.dot_general(
                queries,
                key_held[keys_at, :],
                (((1,), (1,)), ((), ())),
                preferred_element_type=jnp.float32,
            )
            if masked:
                place_at = at * KEY_BLOCK + lax.broadcasted_iota(jnp.int32, (1, KEY_BLOCK), 1)
                scores = jnp.where(
                    (place_at >= low_rows) & (place_at <= high_rows), scores, MASKED_SCORE
                )
            new_peak = jnp.maximum(peak, jnp.max(scores, axis=-1, keepdims=True))
            weights = jnp.exp2((scores - new_peak) * to_power)
            rescale = jnp.exp2((peak - new_peak) * to_power)
            total = total * rescale + jnp.sum(weights, axis=-1, keepdims=True)
            gathered = gathered * rescale + jnp.dot(
                weights.astype(jnp.bfloat16),
                value_held[keys_at, :],
                preferred_element_type=jnp.float32,
            )
            return new_peak, total, gathered

        running = (
            jnp.full((tall, 1), LOWEST_PEAK, jnp.float32),
            jnp.zeros((tall, 1), jnp.float32),
            jnp.zeros((tall, HEAD_DIM), jnp.float32),
        )
        running = lax.fori_loop(begin, clear_begin, lambda a, r: key_step(a, r, True), running)
        running = lax.fori_loop(clear_begin, clear_end, lambda a, r: key_step(a, r, False), running)
        peak, total, gathered = lax.fori_loop(
            clear_end, end, lambda a, r: key_step(a, r, True), running
        )
        context = (gathered / total).astype(jnp.bfloat16)
        for h in range(GROUP):
            out_ref[rows, h * HEAD_DIM : (h + 1) * HEAD_DIM] = context[
                h * QUERY_BLOCK : (h + 1) * QUERY_BLOCK
            ]
        return unused

    lax.fori_loop(0, SEQ // QUERY_BLOCK, query_step, 0)


def attention(info, image_src, image_dst, image_len, queries, low_rows, image_kv, text_kv):
    smem = pl.BlockSpec(memory_space=pltpu.SMEM)
    vmem = pl.BlockSpec(memory_space=pltpu.VMEM)
    image_rows = image_kv.shape[0]
    return pl.pallas_call(
        attention_kernel,
        out_shape=jax.ShapeDtypeStruct(queries.shape, jnp.bfloat16),
        in_specs=[smem] * 4 + [vmem] * 3 + [pl.BlockSpec(memory_space=pl.ANY)],
        out_specs=vmem,
        scratch_shapes=[
            pltpu.VMEM((WINDOW, 2 * HEAD_DIM), jnp.bfloat16),
            pltpu.VMEM((WINDOW + MOST, HEAD_DIM), jnp.float32),
            pltpu.VMEM((WINDOW + MOST, HEAD_DIM), jnp.float32),
            pltpu.VMEM((image_rows + MOST, HEAD_DIM), jnp.float32),
            pltpu.VMEM((image_rows + MOST, HEAD_DIM), jnp.float32),
            pltpu.VMEM((PADDED, HEAD_DIM), jnp.bfloat16),
            pltpu.VMEM((PADDED, HEAD_DIM), jnp.bfloat16),
            pltpu.SemaphoreType.DMA,
        ],
        compiler_params=pltpu.CompilerParams(vmem_limit_bytes=48 * 1024 * 1024),
        cost_estimate=pl.CostEstimate(
            flops=8_000_000_000, bytes_accessed=8_000_000, transcendentals=13_000_000
        ),
    )(info, image_src, image_dst, image_len, queries, low_rows, image_kv, text_kv)


def body(
    patches,
    vision_gain,
    vision_bias,
    up_weight,
    down_weight,
    merge_gain,
    merge_bias,
    merge_weight,
    attn_gain,
    query_weight,
    kv_weight,
    text_query,
    text_kv,
    doc_ids,
    image_sizes,
    image_offsets,
):
    z_at, yl_at, c_at = lax.axis_index("z"), lax.axis_index("yl"), lax.axis_index("c")
    ctx_index = lax.axis_index(CTX)
    width = patches.shape[1]
    own_rows = patches.shape[0]

    text_window = lax.all_gather(
        jnp.concatenate([text_kv[0], text_kv[1]], axis=1), CTX, axis=0, tiled=True
    )
    below = jnp.sum(
        (doc_ids[:, None] < jnp.arange(4, dtype=jnp.int32)[None, :]).astype(jnp.int32),
        axis=0,
        dtype=jnp.int32,
    )
    facts = lax.all_gather(
        jnp.concatenate([image_sizes, image_offsets, below[None, :]], axis=1), DP + CTX, axis=0
    ).reshape(8, 16, 12)

    normed = layer_norm(patches, vision_gain, vision_bias)
    spare = ((0, 24 - up_weight.shape[0]), (0, 0))
    units = gather_by_exchange(
        jnp.concatenate([jnp.pad(up_weight, spare), jnp.pad(down_weight, spare)], axis=0),
        DP + ("z",),
        32,
    )
    ups = units[:, :24].reshape(-1, width)
    downs = units[:, 24:].reshape(-1, width)
    pair = jnp.concatenate([normed, swap(normed, "yl")], axis=0)
    four = jnp.concatenate([pair, swap(pair, "c")], axis=0)
    hidden = quick_gelu(
        lax.dot_general(four, ups, (((1,), (1,)), ((), ())), preferred_element_type=jnp.float32)
    ).astype(jnp.bfloat16)
    partial = jnp.dot(hidden, downs, preferred_element_type=jnp.float32)
    half = partial[: 2 * own_rows] + swap(
        partial[2 * own_rows :].astype(jnp.bfloat16), "c"
    ).astype(jnp.float32)
    branch = half[:own_rows] + swap(half[own_rows:].astype(jnp.bfloat16), "yl").astype(jnp.float32)
    vision = (patches.astype(jnp.float32) + branch).astype(jnp.bfloat16)
    merged_in = layer_norm(vision, merge_gain, merge_bias).reshape(-1, 4 * width)

    column_in = gather_by_exchange(merged_in, DP, 8).reshape(-1, 4 * width)
    merged = jnp.dot(column_in, merge_weight, preferred_element_type=jnp.float32).astype(
        jnp.bfloat16
    )
    whole = gather_by_exchange(merged, DP, 8)
    wide = whole.astype(jnp.float32)
    part = merged.shape[1]
    mean_square = jnp.sum(wide * wide, axis=(0, 2), keepdims=True) / (8 * part)
    ready = (wide * lax.rsqrt(mean_square + EPSILON) * attn_gain.reshape(8, 1, part)).astype(
        jnp.bfloat16
    )
    ready = jnp.swapaxes(ready, 0, 1).reshape(merged.shape[0], 8 * part)
    image_kv = jnp.concatenate(
        [
            jnp.dot(ready, kv_weight[0], preferred_element_type=jnp.float32),
            jnp.dot(ready, kv_weight[1], preferred_element_type=jnp.float32),
        ],
        axis=1,
    ).astype(jnp.bfloat16)
    image_query = jnp.dot(ready, query_weight, preferred_element_type=jnp.float32).astype(
        jnp.bfloat16
    )

    sizes = jnp.swapaxes(facts[:, :, :4], 0, 1)
    offsets = jnp.swapaxes(facts[:, :, 4:8], 0, 1)
    starts = jnp.sum(facts[0, :, 8:], axis=0, dtype=jnp.int32)
    positions = row_positions(sizes.reshape(128, 4), offsets.reshape(128, 4), CAPACITY).reshape(
        16, 256
    )
    before = jnp.arange(256)[None, :] < jnp.arange(256)[:, None]
    own_owner = lax.dynamic_index_in_dim(positions, ctx_index, 0, False) // SEQ
    own_rank = jnp.sum(
        ((own_owner[None, :] == own_owner[:, None]) & before).astype(jnp.int32),
        axis=1,
        dtype=jnp.int32,
    )
    own_slot = own_owner * CAPACITY + own_rank
    spread_out = (jnp.arange(512, dtype=jnp.int32)[:, None] == own_slot[None, :]).astype(
        jnp.bfloat16
    )
    mine = positions // SEQ == ctx_index
    rank = jnp.sum((mine[:, None, :] & before[None]).astype(jnp.int32), axis=2, dtype=jnp.int32)
    slot_here = mine[:, :, None] & (
        rank[:, :, None] == jnp.arange(CAPACITY, dtype=jnp.int32)[None, None, :]
    )
    slot_place = jnp.sum(
        jnp.where(slot_here, positions[:, :, None] - ctx_index * SEQ + 1, 0),
        axis=1,
        dtype=jnp.int32,
    ).reshape(-1) - 1
    bring_in = jnp.arange(SEQ, dtype=jnp.int32)[:, None] == slot_place[None, :]
    is_image = jnp.any(bring_in, axis=1)

    blocks = [image_kv]
    for step in (1, 2, 3):
        blocks.append(lax.ppermute(image_kv, "z", [(i, (i + step) % 4) for i in range(4)]))
    plane = jnp.concatenate(blocks, axis=0)
    plane = jnp.concatenate([plane, swap(plane, "yl")], axis=0)
    every_kv = jnp.concatenate([plane, swap(plane, "c")], axis=0)

    sent = jnp.dot(spread_out, image_query, preferred_element_type=jnp.float32).astype(jnp.bfloat16)
    got = lax.all_to_all(
        sent.reshape(16, CAPACITY, -1), CTX, split_axis=0, concat_axis=0
    ).reshape(512, -1)
    placed_query = jnp.dot(
        bring_in.astype(jnp.bfloat16), got, preferred_element_type=jnp.float32
    ).astype(jnp.bfloat16)
    queries = jnp.where(is_image[:, None], placed_query, text_query)

    window_start = jnp.maximum(ctx_index - REACH, 0) * SEQ
    low_rows = (
        jnp.sum(
            jnp.where(
                doc_ids[:, None] == jnp.arange(4, dtype=jnp.int32)[None, :], starts[None, :], 0
            ),
            axis=1,
            dtype=jnp.int32,
        )
        - window_start
    )
    low_rows = jnp.maximum(low_rows, 0)
    edges = low_rows.reshape(-1, QUERY_BLOCK)
    info = jnp.concatenate(
        [
            jnp.stack([window_start, ctx_index * SEQ - window_start]).astype(jnp.int32),
            jnp.stack([edges[:, 0], edges[:, -1]], axis=1).reshape(-1),
        ]
    )
    source = jnp.arange(16, dtype=jnp.int32)
    source_block = (
        ((source % 2) ^ c_at) * 8 + (((source // 2) % 2) ^ yl_at) * 4 + (z_at - source // 4 + 4) % 4
    )
    within_device = jnp.cumsum(sizes, axis=2, dtype=jnp.int32) - sizes
    image_src = (
        source_block[:, None, None] * 256
        + jnp.arange(8, dtype=jnp.int32)[None, :, None] * CAPACITY
        + within_device
    )
    return attention(
        info,
        image_src.reshape(-1),
        (offsets - window_start).reshape(-1),
        sizes.reshape(-1),
        queries,
        low_rows[:, None],
        every_kv,
        text_window,
    )


def solution(mesh):
    fine = Mesh(mesh.devices.reshape(2, 4, 4, 2, 2), DP + CTX)
    every = DP + CTX
    return jax.shard_map(
        body,
        mesh=fine,
        in_specs=(
            P(every, None),
            P(),
            P(),
            P(every, None),
            P(every, None),
            P(),
            P(),
            P(None, DP),
            P(),
            P(None, DP),
            P(None, None, DP),
            P(CTX, DP),
            P(None, CTX, DP),
            P(CTX),
            P(every, None),
            P(every, None),
        ),
        out_specs=P(CTX, DP),
        check_vma=False,
    )
```

```python
import math

import jax
import jax.numpy as jnp
import numpy as np
from jax import lax
from jax.experimental import pallas as pl
from jax.experimental.pallas import tpu as pltpu
from jax.sharding import Mesh
from jax.sharding import PartitionSpec as P

HEAD_DIM = 128
MOST = 16
SEQ = 640
REACH = 8
WINDOW = SEQ * (REACH + 1)
KEY_BLOCK = 512
PADDED = -(-WINDOW // KEY_BLOCK) * KEY_BLOCK
QUERY_BLOCK = 128
GROUP = 4
IMAGES = 512
CAPACITY = 32
CHUNK = 16
CTX_COUNT = 16
DP_COUNT = 8

MASKED_SCORE = -1e30
LOWEST_PEAK = -1e29
EPSILON = 1e-06
DP = ("yh", "x")
CTX = ("z", "yl", "c")


def layer_norm(rows_in, norm_gain, norm_bias):
    values = rows_in.astype(jnp.float32)
    center = values - jnp.mean(values, axis=-1, keepdims=True)
    spread = jnp.mean(center * center, axis=-1, keepdims=True)
    return (center * lax.rsqrt(spread + EPSILON) * norm_gain + norm_bias).astype(jnp.bfloat16)


def quick_gelu(values):
    return values * jax.nn.sigmoid(1.702 * values)


def row_positions(size_table, offset_table, row_count):
    image_ends = jnp.cumsum(size_table, axis=1, dtype=jnp.int32)
    image_starts = image_ends - size_table
    within = jnp.arange(row_count, dtype=jnp.int32)[None, :, None]
    inside = (within >= image_starts[:, None, :]) & (within < image_ends[:, None, :])
    placed = offset_table[:, None, :] - image_starts[:, None, :] + within
    return jnp.sum(jnp.where(inside, placed, 0), axis=2, dtype=jnp.int32)


def gather_by_exchange(block, axes, count):
    return lax.all_to_all(
        jnp.broadcast_to(block[None], (count,) + block.shape), axes, split_axis=0, concat_axis=0
    )


def swap(rows, axis):
    return lax.ppermute(rows, axis, [(0, 1), (1, 0)])


def attention_kernel(
    info,
    image_src,
    image_dst,
    image_len,
    text_query_ref,
    bring_ref,
    low_ref,
    first_ref,
    last_ref,
    text_ref,
    out_ref,
    text_held,
    key_wide,
    value_wide,
    image_key,
    image_value,
    image_query,
    key_held,
    value_held,
    sem,
):
    window_start = pl.multiple_of(info[0], SEQ)
    query_offset = info[1]
    copy = pltpu.make_async_copy(text_ref.at[pl.ds(window_start, WINDOW), :], text_held, sem)
    copy.start()

    def widen_image(source, unused):
        for device in range(DP_COUNT):
            base = source * (DP_COUNT * CAPACITY) + device * CAPACITY
            rows = pl.ds(pl.multiple_of(base, CHUNK), CHUNK)
            block = first_ref[source, device * CHUNK : (device + 1) * CHUNK, :].astype(jnp.float32)
            image_key[rows, :] = block[:, :HEAD_DIM]
            image_value[rows, :] = block[:, HEAD_DIM:]
            rows = pl.ds(pl.multiple_of(base + CHUNK, CHUNK), CHUNK)
            at, side = device % 4 * CHUNK, device // 4 * 2 * HEAD_DIM
            block = last_ref[source, at : at + CHUNK, side : side + 2 * HEAD_DIM].astype(
                jnp.float32
            )
            image_key[rows, :] = block[:, :HEAD_DIM]
            image_value[rows, :] = block[:, HEAD_DIM:]
        rows = pl.ds(pl.multiple_of(source * CAPACITY, CAPACITY), CAPACITY)
        image_query[rows, :] = last_ref[source, 4 * CHUNK :, :]
        return unused

    lax.fori_loop(0, CTX_COUNT, widen_image, 0)
    copy.wait()

    def widen_text(step, unused):
        rows = pl.ds(pl.multiple_of(step * 320, 320), 320)
        key_wide[rows, :] = text_held[rows, :HEAD_DIM].astype(jnp.float32)
        value_wide[rows, :] = text_held[rows, HEAD_DIM:].astype(jnp.float32)
        return unused

    lax.fori_loop(0, WINDOW // 320, widen_text, 0)
    row_in = lax.broadcasted_iota(jnp.int32, (MOST, HEAD_DIM), 0)

    def place(image, unused):
        target = image_dst[image]

        @pl.when((target >= 0) & (target < WINDOW))
        def _():
            origin = image_src[image]
            taken = row_in < image_len[image]
            rows = pl.ds(target, MOST)
            key_wide[rows, :] = jnp.where(taken, image_key[pl.ds(origin, MOST), :], key_wide[rows, :])
            value_wide[rows, :] = jnp.where(
                taken, image_value[pl.ds(origin, MOST), :], value_wide[rows, :]
            )

        return unused

    lax.fori_loop(0, IMAGES, place, 0)

    def narrow(step, unused):
        rows = pl.ds(pl.multiple_of(step * 320, 320), 320)
        key_held[rows, :] = key_wide[rows, :].astype(jnp.bfloat16)
        value_held[rows, :] = value_wide[rows, :].astype(jnp.bfloat16)
        return unused

    lax.fori_loop(0, WINDOW // 320, narrow, 0)
    if PADDED > WINDOW:
        key_held[WINDOW:, :] = jnp.zeros((PADDED - WINDOW, HEAD_DIM), jnp.bfloat16)
        value_held[WINDOW:, :] = jnp.zeros((PADDED - WINDOW, HEAD_DIM), jnp.bfloat16)

    tall = GROUP * QUERY_BLOCK
    to_power = math.log2(math.e) / math.sqrt(HEAD_DIM)
    row_at = lax.broadcasted_iota(jnp.int32, (QUERY_BLOCK, 1), 0)

    def query_step(block, unused):
        rows = pl.ds(pl.multiple_of(block * QUERY_BLOCK, QUERY_BLOCK), QUERY_BLOCK)
        first = query_offset + block * QUERY_BLOCK
        bring = bring_ref[rows, :]
        is_image = jnp.max(bring.astype(jnp.float32), axis=-1, keepdims=True) > 0.5
        placed = jnp.where(
            is_image,
            jnp.dot(bring, image_query[...], preferred_element_type=jnp.float32),
            text_query_ref[rows, :].astype(jnp.float32),
        ).astype(jnp.bfloat16)
        queries = jnp.concatenate(
            [placed[:, h * HEAD_DIM : (h + 1) * HEAD_DIM] for h in range(GROUP)], axis=0
        )
        low_rows = jnp.concatenate([low_ref[rows, :]] * GROUP, axis=0)
        high_rows = jnp.concatenate([row_at + first] * GROUP, axis=0)
        low_first = info[2 + 2 * block]
        low_last = info[3 + 2 * block]
        begin = low_first // KEY_BLOCK
        end = (first + QUERY_BLOCK - 1) // KEY_BLOCK + 1
        clear_begin = jnp.minimum((low_last + KEY_BLOCK - 1) // KEY_BLOCK, end)
        clear_end = jnp.maximum((first + 1) // KEY_BLOCK, clear_begin)

        def key_step(at, running, masked):
            peak, total, gathered = running
            keys_at = pl.ds(pl.multiple_of(at * KEY_BLOCK, KEY_BLOCK), KEY_BLOCK)
            scores = lax.dot_general(
                queries,
                key_held[keys_at, :],
                (((1,), (1,)), ((), ())),
                preferred_element_type=jnp.float32,
            )
            if masked:
                place_at = at * KEY_BLOCK + lax.broadcasted_iota(jnp.int32, (1, KEY_BLOCK), 1)
                scores = jnp.where(
                    (place_at >= low_rows) & (place_at <= high_rows), scores, MASKED_SCORE
                )
            new_peak = jnp.maximum(peak, jnp.max(scores, axis=-1, keepdims=True))
            weights = jnp.exp2((scores - new_peak) * to_power)
            rescale = jnp.exp2((peak - new_peak) * to_power)
            total = total * rescale + jnp.sum(weights, axis=-1, keepdims=True)
            gathered = gathered * rescale + jnp.dot(
                weights.astype(jnp.bfloat16),
                value_held[keys_at, :],
                preferred_element_type=jnp.float32,
            )
            return new_peak, total, gathered

        running = (
            jnp.full((tall, 1), LOWEST_PEAK, jnp.float32),
            jnp.zeros((tall, 1), jnp.float32),
            jnp.zeros((tall, HEAD_DIM), jnp.float32),
        )
        running = lax.fori_loop(begin, clear_begin, lambda a, r: key_step(a, r, True), running)
        running = lax.fori_loop(clear_begin, clear_end, lambda a, r: key_step(a, r, False), running)
        peak, total, gathered = lax.fori_loop(
            clear_end, end, lambda a, r: key_step(a, r, True), running
        )
        context = (gathered / total).astype(jnp.bfloat16)
        for h in range(GROUP):
            out_ref[rows, h * HEAD_DIM : (h + 1) * HEAD_DIM] = context[
                h * QUERY_BLOCK : (h + 1) * QUERY_BLOCK
            ]
        return unused

    lax.fori_loop(0, SEQ // QUERY_BLOCK, query_step, 0)


def attention(info, image_src, image_dst, image_len, text_query, bring_in, low_rows, first, last, text):
    smem = pl.BlockSpec(memory_space=pltpu.SMEM)
    vmem = pl.BlockSpec(memory_space=pltpu.VMEM)
    image_rows = CTX_COUNT * DP_COUNT * CAPACITY
    return pl.pallas_call(
        attention_kernel,
        out_shape=jax.ShapeDtypeStruct(text_query.shape, jnp.bfloat16),
        in_specs=[smem] * 4 + [vmem] * 5 + [pl.BlockSpec(memory_space=pl.ANY)],
        out_specs=vmem,
        scratch_shapes=[
            pltpu.VMEM((WINDOW, 2 * HEAD_DIM), jnp.bfloat16),
            pltpu.VMEM((WINDOW + MOST, HEAD_DIM), jnp.float32),
            pltpu.VMEM((WINDOW + MOST, HEAD_DIM), jnp.float32),
            pltpu.VMEM((image_rows + MOST, HEAD_DIM), jnp.float32),
            pltpu.VMEM((image_rows + MOST, HEAD_DIM), jnp.float32),
            pltpu.VMEM((CTX_COUNT * CAPACITY, GROUP * HEAD_DIM), jnp.bfloat16),
            pltpu.VMEM((PADDED, HEAD_DIM), jnp.bfloat16),
            pltpu.VMEM((PADDED, HEAD_DIM), jnp.bfloat16),
            pltpu.SemaphoreType.DMA,
        ],
        compiler_params=pltpu.CompilerParams(vmem_limit_bytes=48 * 1024 * 1024),
        cost_estimate=pl.CostEstimate(
            flops=8_000_000_000, bytes_accessed=8_000_000, transcendentals=13_000_000
        ),
    )(info, image_src, image_dst, image_len, text_query, bring_in, low_rows, first, last, text)


def body(
    patches,
    vision_gain,
    vision_bias,
    up_weight,
    down_weight,
    merge_gain,
    merge_bias,
    merge_weight,
    attn_gain,
    query_weight,
    kv_weight,
    text_query,
    text_kv,
    doc_ids,
    image_sizes,
    image_offsets,
):
    ctx_index = lax.axis_index(CTX)
    width = patches.shape[1]
    own_rows = patches.shape[0]

    text_window = lax.all_gather(
        jnp.concatenate([text_kv[0], text_kv[1]], axis=1), CTX, axis=0, tiled=True
    )
    below = jnp.sum(
        (doc_ids[:, None] < jnp.arange(4, dtype=jnp.int32)[None, :]).astype(jnp.int32),
        axis=0,
        dtype=jnp.int32,
    )
    facts = gather_by_exchange(
        jnp.concatenate([image_sizes, image_offsets, below[None, :]], axis=1), DP + ("yl",), 16
    )
    facts = gather_by_exchange(facts.reshape(16, 12), ("z", "c"), 8)
    facts = facts.reshape(4, 2, 8, 2, 12).transpose(2, 0, 3, 1, 4).reshape(8, 16, 12)

    spare = ((0, 24 - up_weight.shape[0]), (0, 0))
    units = gather_by_exchange(
        jnp.concatenate([jnp.pad(up_weight, spare), jnp.pad(down_weight, spare)], axis=0),
        DP + ("yl",),
        16,
    )
    normed = layer_norm(patches, vision_gain, vision_bias)
    column = gather_by_exchange(normed, ("z",), 4).reshape(-1, width)
    near_rows = column.shape[0]
    near = jnp.concatenate([column, swap(column, "c")], axis=0)
    ups = units[:, :24].reshape(-1, width)
    downs = units[:, 24:].reshape(-1, width)
    hidden = quick_gelu(
        lax.dot_general(near, ups, (((1,), (1,)), ((), ())), preferred_element_type=jnp.float32)
    ).astype(jnp.bfloat16)
    away = jnp.dot(hidden[near_rows:], downs, preferred_element_type=jnp.float32).astype(
        jnp.bfloat16
    )
    here = jnp.dot(hidden[:near_rows], downs, preferred_element_type=jnp.float32)
    pair_sum = (here + swap(away, "c").astype(jnp.float32)).astype(jnp.bfloat16)
    terms = lax.all_to_all(
        pair_sum.reshape(4, own_rows, width), "z", split_axis=0, concat_axis=0
    )
    branch = jnp.sum(terms.astype(jnp.float32), axis=0)
    vision = (patches.astype(jnp.float32) + branch).astype(jnp.bfloat16)
    merged_in = layer_norm(vision, merge_gain, merge_bias).reshape(-1, 4 * width)

    columns = [
        gather_by_exchange(merged_in[at : at + CHUNK], DP, DP_COUNT).reshape(-1, 4 * width)
        for at in (0, CHUNK)
    ]
    wholes = []
    for column_in in columns:
        merged = jnp.dot(column_in, merge_weight, preferred_element_type=jnp.float32).astype(
            jnp.bfloat16
        )
        wholes.append(gather_by_exchange(merged, DP, DP_COUNT))
    image_kvs, image_queries = [], []
    for whole in wholes:
        wide = whole.astype(jnp.float32)
        part = whole.shape[2]
        mean_square = jnp.sum(wide * wide, axis=(0, 2), keepdims=True) / (DP_COUNT * part)
        ready = (wide * lax.rsqrt(mean_square + EPSILON) * attn_gain.reshape(8, 1, part)).astype(
            jnp.bfloat16
        )
        ready = jnp.swapaxes(ready, 0, 1).reshape(whole.shape[1], DP_COUNT * part)
        image_kvs.append(
            jnp.concatenate(
                [
                    jnp.dot(ready, kv_weight[0], preferred_element_type=jnp.float32),
                    jnp.dot(ready, kv_weight[1], preferred_element_type=jnp.float32),
                ],
                axis=1,
            ).astype(jnp.bfloat16)
        )
        image_queries.append(
            jnp.dot(ready, query_weight, preferred_element_type=jnp.float32).astype(jnp.bfloat16)
        )
    first = gather_by_exchange(image_kvs[0], CTX, CTX_COUNT)

    sizes = jnp.swapaxes(facts[:, :, :4], 0, 1)
    offsets = jnp.swapaxes(facts[:, :, 4:8], 0, 1)
    starts = jnp.sum(facts[0, :, 8:], axis=0, dtype=jnp.int32)
    positions = row_positions(sizes.reshape(128, 4), offsets.reshape(128, 4), CAPACITY).reshape(
        16, 256
    )
    before = jnp.arange(256)[None, :] < jnp.arange(256)[:, None]
    own_owner = lax.dynamic_index_in_dim(positions, ctx_index, 0, False) // SEQ
    own_rank = jnp.sum(
        ((own_owner[None, :] == own_owner[:, None]) & before).astype(jnp.int32),
        axis=1,
        dtype=jnp.int32,
    )
    own_slot = (own_owner * CAPACITY + own_rank).reshape(8, 2, CHUNK).swapaxes(0, 1).reshape(-1)
    spread_out = (jnp.arange(512, dtype=jnp.int32)[:, None] == own_slot[None, :]).astype(
        jnp.bfloat16
    )
    mine = positions // SEQ == ctx_index
    rank = jnp.sum((mine[:, None, :] & before[None]).astype(jnp.int32), axis=2, dtype=jnp.int32)
    slot_here = mine[:, :, None] & (
        rank[:, :, None] == jnp.arange(CAPACITY, dtype=jnp.int32)[None, None, :]
    )
    slot_place = jnp.sum(
        jnp.where(slot_here, positions[:, :, None] - ctx_index * SEQ + 1, 0),
        axis=1,
        dtype=jnp.int32,
    ).reshape(-1) - 1
    bring_in = jnp.arange(SEQ, dtype=jnp.int32)[:, None] == slot_place[None, :]

    chunk_rows = DP_COUNT * CHUNK
    sent = sum(
        jnp.dot(
            spread_out[:, k * chunk_rows : (k + 1) * chunk_rows],
            image_queries[k],
            preferred_element_type=jnp.float32,
        )
        for k in (0, 1)
    ).astype(jnp.bfloat16)
    half = chunk_rows // 2
    folded = jnp.concatenate([image_kvs[1][:half], image_kvs[1][half:]], axis=1)
    last = lax.all_to_all(
        jnp.concatenate(
            [
                jnp.broadcast_to(folded[None], (CTX_COUNT,) + folded.shape),
                sent.reshape(CTX_COUNT, CAPACITY, -1),
            ],
            axis=1,
        ),
        CTX,
        split_axis=0,
        concat_axis=0,
    )

    window_start = jnp.maximum(ctx_index - REACH, 0) * SEQ
    low_rows = (
        jnp.sum(
            jnp.where(
                doc_ids[:, None] == jnp.arange(4, dtype=jnp.int32)[None, :], starts[None, :], 0
            ),
            axis=1,
            dtype=jnp.int32,
        )
        - window_start
    )
    low_rows = jnp.maximum(low_rows, 0)
    edges = low_rows.reshape(-1, QUERY_BLOCK)
    info = jnp.concatenate(
        [
            jnp.stack([window_start, ctx_index * SEQ - window_start]).astype(jnp.int32),
            jnp.stack([edges[:, 0], edges[:, -1]], axis=1).reshape(-1),
        ]
    )
    within_device = jnp.cumsum(sizes, axis=2, dtype=jnp.int32) - sizes
    image_src = (
        jnp.arange(CTX_COUNT * DP_COUNT, dtype=jnp.int32).reshape(CTX_COUNT, DP_COUNT, 1) * CAPACITY
        + within_device
    )
    return attention(
        info,
        image_src.reshape(-1),
        (offsets - window_start).reshape(-1),
        sizes.reshape(-1),
        text_query,
        bring_in.astype(jnp.bfloat16),
        low_rows[:, None],
        first,
        last,
        text_window,
    )


def solution(mesh):
    fine = Mesh(mesh.devices.reshape(2, 4, 4, 2, 2), DP + CTX)
    every = DP + CTX
    return jax.shard_map(
        body,
        mesh=fine,
        in_specs=(
            P(every, None),
            P(),
            P(),
            P(every, None),
            P(every, None),
            P(),
            P(),
            P(None, DP),
            P(),
            P(None, DP),
            P(None, None, DP),
            P(CTX, DP),
            P(None, CTX, DP),
            P(CTX),
            P(every, None),
            P(every, None),
        ),
        out_specs=P(CTX, DP),
        check_vma=False,
    )
```

```python
import math

import jax
import jax.numpy as jnp
import numpy as np
from jax import lax
from jax.experimental import pallas as pl
from jax.experimental.pallas import tpu as pltpu
from jax.sharding import Mesh
from jax.sharding import PartitionSpec as P

HEAD_DIM = 128
MOST = 16
SEQ = 640
REACH = 8
WINDOW = SEQ * (REACH + 1)
KEY_BLOCK = 512
PADDED = -(-WINDOW // KEY_BLOCK) * KEY_BLOCK
QUERY_BLOCK = 128
GROUP = 4
IMAGES = 512
CAPACITY = 32
CHUNK = 16
UNITS = 24
CTX_COUNT = 16
DP_COUNT = 8

MASKED_SCORE = -1e30
LOWEST_PEAK = -1e29
EPSILON = 1e-06
DP = ("yh", "x")
CTX = ("z", "yl", "c")


def layer_norm(rows_in, norm_gain, norm_bias):
    values = rows_in.astype(jnp.float32)
    center = values - jnp.mean(values, axis=-1, keepdims=True)
    spread = jnp.mean(center * center, axis=-1, keepdims=True)
    return (center * lax.rsqrt(spread + EPSILON) * norm_gain + norm_bias).astype(jnp.bfloat16)


def quick_gelu(values):
    return values * jax.nn.sigmoid(1.702 * values)


def starts_within(sizes):
    count = sizes.shape[-1]
    earlier = jnp.arange(count)[None, :] < jnp.arange(count)[:, None]
    return jnp.sum(jnp.where(earlier, sizes[..., None, :], 0), axis=-1, dtype=jnp.int32)


def row_positions(size_table, offset_table, row_count):
    image_starts = starts_within(size_table)
    image_ends = image_starts + size_table
    within = jnp.arange(row_count, dtype=jnp.int32)[None, :, None]
    inside = (within >= image_starts[:, None, :]) & (within < image_ends[:, None, :])
    placed = offset_table[:, None, :] - image_starts[:, None, :] + within
    return jnp.sum(jnp.where(inside, placed, 0), axis=2, dtype=jnp.int32)


def gather_by_exchange(block, axes, count):
    return lax.all_to_all(
        jnp.broadcast_to(block[None], (count,) + block.shape), axes, split_axis=0, concat_axis=0
    )


def swap(rows, axis):
    return lax.ppermute(rows, axis, [(0, 1), (1, 0)])


def attention_kernel(
    info,
    image_src,
    image_dst,
    image_len,
    blocks_at,
    text_query_ref,
    bring_ref,
    low_ref,
    first_ref,
    last_ref,
    text_ref,
    out_ref,
    text_held,
    key_wide,
    value_wide,
    image_key,
    image_value,
    image_query,
    key_held,
    value_held,
    sems,
):
    query_offset = info[1]
    copies = []
    for shard in range(REACH + 1):
        copies.append(
            pltpu.make_async_copy(
                text_ref.at[blocks_at[CTX_COUNT + shard]],
                text_held.at[pl.ds(shard * SEQ, SEQ), :],
                sems.at[shard],
            )
        )
        copies[shard].start()

    def widen_image(source, unused):
        for device in range(DP_COUNT):
            base = source * (DP_COUNT * CAPACITY) + device * CAPACITY
            rows = pl.ds(pl.multiple_of(base, CHUNK), CHUNK)
            block = first_ref[blocks_at[source], device * CHUNK : (device + 1) * CHUNK, :].astype(jnp.float32)
            image_key[rows, :] = block[:, :HEAD_DIM]
            image_value[rows, :] = block[:, HEAD_DIM:]
            rows = pl.ds(pl.multiple_of(base + CHUNK, CHUNK), CHUNK)
            at, side = device % 4 * CHUNK, device // 4 * 2 * HEAD_DIM
            block = last_ref[source, at : at + CHUNK, side : side + 2 * HEAD_DIM].astype(
                jnp.float32
            )
            image_key[rows, :] = block[:, :HEAD_DIM]
            image_value[rows, :] = block[:, HEAD_DIM:]
        rows = pl.ds(pl.multiple_of(source * CAPACITY, CAPACITY), CAPACITY)
        image_query[rows, :] = last_ref[source, 4 * CHUNK :, :]
        return unused

    lax.fori_loop(0, CTX_COUNT, widen_image, 0)
    for copy in copies:
        copy.wait()

    def widen_text(step, unused):
        rows = pl.ds(pl.multiple_of(step * 320, 320), 320)
        key_wide[rows, :] = text_held[rows, :HEAD_DIM].astype(jnp.float32)
        value_wide[rows, :] = text_held[rows, HEAD_DIM:].astype(jnp.float32)
        return unused

    lax.fori_loop(0, WINDOW // 320, widen_text, 0)
    row_in = lax.broadcasted_iota(jnp.int32, (MOST, HEAD_DIM), 0)

    def place(image, unused):
        target = image_dst[image]

        @pl.when((target >= 0) & (target < WINDOW))
        def _():
            origin = image_src[image]
            taken = row_in < image_len[image]
            rows = pl.ds(target, MOST)
            key_wide[rows, :] = jnp.where(taken, image_key[pl.ds(origin, MOST), :], key_wide[rows, :])
            value_wide[rows, :] = jnp.where(
                taken, image_value[pl.ds(origin, MOST), :], value_wide[rows, :]
            )

        return unused

    lax.fori_loop(0, IMAGES, place, 0)

    def narrow(step, unused):
        rows = pl.ds(pl.multiple_of(step * 320, 320), 320)
        key_held[rows, :] = key_wide[rows, :].astype(jnp.bfloat16)
        value_held[rows, :] = value_wide[rows, :].astype(jnp.bfloat16)
        return unused

    lax.fori_loop(0, WINDOW // 320, narrow, 0)
    if PADDED > WINDOW:
        key_held[WINDOW:, :] = jnp.zeros((PADDED - WINDOW, HEAD_DIM), jnp.bfloat16)
        value_held[WINDOW:, :] = jnp.zeros((PADDED - WINDOW, HEAD_DIM), jnp.bfloat16)

    tall = GROUP * QUERY_BLOCK
    to_power = math.log2(math.e) / math.sqrt(HEAD_DIM)
    row_at = lax.broadcasted_iota(jnp.int32, (QUERY_BLOCK, 1), 0)

    def query_step(block, unused):
        rows = pl.ds(pl.multiple_of(block * QUERY_BLOCK, QUERY_BLOCK), QUERY_BLOCK)
        first = query_offset + block * QUERY_BLOCK
        bring = bring_ref[rows, :]
        is_image = jnp.max(bring.astype(jnp.float32), axis=-1, keepdims=True) > 0.5
        placed = jnp.where(
            is_image,
            jnp.dot(bring, image_query[...], preferred_element_type=jnp.float32),
            text_query_ref[rows, :].astype(jnp.float32),
        ).astype(jnp.bfloat16)
        queries = jnp.concatenate(
            [placed[:, h * HEAD_DIM : (h + 1) * HEAD_DIM] for h in range(GROUP)], axis=0
        )
        low_rows = jnp.concatenate([low_ref[rows, :]] * GROUP, axis=0)
        high_rows = jnp.concatenate([row_at + first] * GROUP, axis=0)
        low_first = info[2 + 2 * block]
        low_last = info[3 + 2 * block]
        begin = low_first // KEY_BLOCK
        end = (first + QUERY_BLOCK - 1) // KEY_BLOCK + 1
        clear_begin = jnp.minimum((low_last + KEY_BLOCK - 1) // KEY_BLOCK, end)
        clear_end = jnp.maximum((first + 1) // KEY_BLOCK, clear_begin)

        def key_step(at, running, masked):
            peak, total, gathered = running
            keys_at = pl.ds(pl.multiple_of(at * KEY_BLOCK, KEY_BLOCK), KEY_BLOCK)
            scores = lax.dot_general(
                queries,
                key_held[keys_at, :],
                (((1,), (1,)), ((), ())),
                preferred_element_type=jnp.float32,
            )
            if masked:
                place_at = at * KEY_BLOCK + lax.broadcasted_iota(jnp.int32, (1, KEY_BLOCK), 1)
                scores = jnp.where(
                    (place_at >= low_rows) & (place_at <= high_rows), scores, MASKED_SCORE
                )
            new_peak = jnp.maximum(peak, jnp.max(scores, axis=-1, keepdims=True))
            weights = jnp.exp2((scores - new_peak) * to_power)
            rescale = jnp.exp2((peak - new_peak) * to_power)
            total = total * rescale + jnp.sum(weights, axis=-1, keepdims=True)
            gathered = gathered * rescale + jnp.dot(
                weights.astype(jnp.bfloat16),
                value_held[keys_at, :],
                preferred_element_type=jnp.float32,
            )
            return new_peak, total, gathered

        running = (
            jnp.full((tall, 1), LOWEST_PEAK, jnp.float32),
            jnp.zeros((tall, 1), jnp.float32),
            jnp.zeros((tall, HEAD_DIM), jnp.float32),
        )
        running = lax.fori_loop(begin, clear_begin, lambda a, r: key_step(a, r, True), running)
        running = lax.fori_loop(clear_begin, clear_end, lambda a, r: key_step(a, r, False), running)
        peak, total, gathered = lax.fori_loop(
            clear_end, end, lambda a, r: key_step(a, r, True), running
        )
        context = (gathered / total).astype(jnp.bfloat16)
        for h in range(GROUP):
            out_ref[rows, h * HEAD_DIM : (h + 1) * HEAD_DIM] = context[
                h * QUERY_BLOCK : (h + 1) * QUERY_BLOCK
            ]
        return unused

    lax.fori_loop(0, SEQ // QUERY_BLOCK, query_step, 0)


def attention(
    info, image_src, image_dst, image_len, blocks_at, text_query, bring_in, low_rows, first, last, text
):
    smem = pl.BlockSpec(memory_space=pltpu.SMEM)
    vmem = pl.BlockSpec(memory_space=pltpu.VMEM)
    image_rows = CTX_COUNT * DP_COUNT * CAPACITY
    return pl.pallas_call(
        attention_kernel,
        out_shape=jax.ShapeDtypeStruct(text_query.shape, jnp.bfloat16),
        in_specs=[smem] * 5 + [vmem] * 5 + [pl.BlockSpec(memory_space=pl.ANY)],
        out_specs=vmem,
        scratch_shapes=[
            pltpu.VMEM((WINDOW, 2 * HEAD_DIM), jnp.bfloat16),
            pltpu.VMEM((WINDOW + MOST, HEAD_DIM), jnp.float32),
            pltpu.VMEM((WINDOW + MOST, HEAD_DIM), jnp.float32),
            pltpu.VMEM((image_rows + MOST, HEAD_DIM), jnp.float32),
            pltpu.VMEM((image_rows + MOST, HEAD_DIM), jnp.float32),
            pltpu.VMEM((CTX_COUNT * CAPACITY, GROUP * HEAD_DIM), jnp.bfloat16),
            pltpu.VMEM((PADDED, HEAD_DIM), jnp.bfloat16),
            pltpu.VMEM((PADDED, HEAD_DIM), jnp.bfloat16),
            pltpu.SemaphoreType.DMA((REACH + 1,)),
        ],
        compiler_params=pltpu.CompilerParams(vmem_limit_bytes=48 * 1024 * 1024),
        cost_estimate=pl.CostEstimate(
            flops=8_000_000_000, bytes_accessed=8_000_000, transcendentals=13_000_000
        ),
    )(info, image_src, image_dst, image_len, blocks_at, text_query, bring_in, low_rows, first, last, text)


def project_kernel(rows_ref, gain_ref, query_weight_ref, kv_weight_ref, query_ref, kv_ref, query_sum, kv_sum, squares):
    step = pl.program_id(0)

    @pl.when(step == 0)
    def _():
        query_sum[...] = jnp.zeros_like(query_sum)
        kv_sum[...] = jnp.zeros_like(kv_sum)
        squares[...] = jnp.zeros_like(squares)

    values = rows_ref[0].astype(jnp.float32)
    squares[...] += jnp.sum(values * values, axis=-1, keepdims=True)
    gained = (values * gain_ref[0]).astype(jnp.bfloat16)
    query_sum[...] += jnp.dot(gained, query_weight_ref[...], preferred_element_type=jnp.float32)
    kv_sum[:, :HEAD_DIM] += jnp.dot(gained, kv_weight_ref[0], preferred_element_type=jnp.float32)
    kv_sum[:, HEAD_DIM:] += jnp.dot(gained, kv_weight_ref[1], preferred_element_type=jnp.float32)

    @pl.when(step == DP_COUNT - 1)
    def _():
        scale = lax.rsqrt(squares[...] / (DP_COUNT * rows_ref.shape[2]) + EPSILON)
        query_ref[...] = (query_sum[...] * scale).astype(jnp.bfloat16)
        kv_ref[...] = (kv_sum[...] * scale).astype(jnp.bfloat16)


def project(whole, gain, query_weight, kv_weight):
    count, rows, part = whole.shape
    query_width, kv_width = query_weight.shape[1], kv_weight.shape[2]
    return pl.pallas_call(
        project_kernel,
        grid=(count,),
        out_shape=(
            jax.ShapeDtypeStruct((rows, query_width), jnp.bfloat16),
            jax.ShapeDtypeStruct((rows, 2 * kv_width), jnp.bfloat16),
        ),
        in_specs=[
            pl.BlockSpec((1, rows, part), lambda k: (k, 0, 0)),
            pl.BlockSpec((1, 1, part), lambda k: (k, 0, 0)),
            pl.BlockSpec((part, query_width), lambda k: (k, 0)),
            pl.BlockSpec((2, part, kv_width), lambda k: (0, k, 0)),
        ],
        out_specs=(
            pl.BlockSpec((rows, query_width), lambda k: (0, 0)),
            pl.BlockSpec((rows, 2 * kv_width), lambda k: (0, 0)),
        ),
        scratch_shapes=[
            pltpu.VMEM((rows, query_width), jnp.float32),
            pltpu.VMEM((rows, 2 * kv_width), jnp.float32),
            pltpu.VMEM((rows, 1), jnp.float32),
        ],
        compiler_params=pltpu.CompilerParams(vmem_limit_bytes=24 * 1024 * 1024),
        cost_estimate=pl.CostEstimate(
            flops=2 * rows * count * part * (query_width + 2 * kv_width),
            bytes_accessed=2 * count * part * (query_width + 2 * kv_width + rows),
            transcendentals=0,
        ),
    )(whole, gain, query_weight, kv_weight)


def body(
    patches,
    vision_gain,
    vision_bias,
    up_weight,
    down_weight,
    merge_gain,
    merge_bias,
    merge_weight,
    attn_gain,
    query_weight,
    kv_weight,
    text_query,
    text_kv,
    doc_ids,
    image_sizes,
    image_offsets,
):
    z_at, yl_at, c_at = lax.axis_index("z"), lax.axis_index("yl"), lax.axis_index("c")
    ctx_index = lax.axis_index(CTX)
    width = patches.shape[1]
    own_rows = patches.shape[0]
    units_own = up_weight.shape[0]

    below = jnp.sum(
        (doc_ids[:, None] < jnp.arange(4, dtype=jnp.int32)[None, :]).astype(jnp.int32),
        axis=0,
        dtype=jnp.int32,
    )
    facts = jnp.concatenate([image_sizes, image_offsets, below[None, :]], axis=1)
    facts = jnp.concatenate([facts // 128, facts % 128], axis=1).astype(jnp.bfloat16)
    fact_count = facts.shape[1]
    units = gather_by_exchange(
        jnp.concatenate(
            [
                jnp.pad(up_weight, ((0, UNITS - units_own), (0, 0))),
                down_weight,
                jnp.pad(facts, ((0, UNITS - units_own - 1), (0, width - fact_count))),
            ],
            axis=0,
        ),
        DP + ("yl",),
        16,
    )
    normed = layer_norm(patches, vision_gain, vision_bias)
    column = jnp.concatenate(
        [normed]
        + [
            lax.ppermute(normed, "z", [(i, (i + step) % 4) for i in range(4)])
            for step in (1, 2, 3)
        ],
        axis=0,
    )
    near_rows = column.shape[0]
    near = jnp.concatenate([column, swap(column, "c")], axis=0)
    ups = units[:, :UNITS].reshape(-1, width)
    downs = units[:, UNITS:].reshape(-1, width)
    facts = units[:, UNITS + units_own, :fact_count].reshape(1, -1)
    hidden = quick_gelu(
        lax.dot_general(near, ups, (((1,), (1,)), ((), ())), preferred_element_type=jnp.float32)
    ).astype(jnp.bfloat16)
    away = jnp.dot(hidden[near_rows:], downs, preferred_element_type=jnp.float32).astype(
        jnp.bfloat16
    )
    here = jnp.dot(hidden[:near_rows], downs, preferred_element_type=jnp.float32)
    came = swap(
        jnp.concatenate(
            [away, jnp.pad(facts, ((0, CHUNK - 1), (0, width - facts.shape[1])))], axis=0
        ),
        "c",
    )
    pair_sum = (here + came[:near_rows].astype(jnp.float32)).astype(jnp.bfloat16)
    other = came[near_rows : near_rows + 1, : facts.shape[1]]
    facts = jnp.concatenate(
        [jnp.where(c_at == 0, facts, other), jnp.where(c_at == 0, other, facts)], axis=1
    )
    tail = jnp.pad(facts, ((0, CHUNK - 1), (0, width - facts.shape[1])))
    by_z = pair_sum.reshape(4, own_rows, width)
    terms = lax.all_to_all(
        jnp.stack(
            [
                jnp.concatenate(
                    [lax.dynamic_index_in_dim(by_z, (z_at - j + 4) % 4, 0, False), tail], axis=0
                )
                for j in range(4)
            ]
        ),
        "z",
        split_axis=0,
        concat_axis=0,
    )
    branch = jnp.sum(terms[:, :own_rows].astype(jnp.float32), axis=0)
    facts = terms[:, own_rows, : facts.shape[1]].astype(jnp.int32)
    facts = facts.reshape(4, 2, 8, 2, fact_count).transpose(2, 0, 3, 1, 4)
    facts = facts.reshape(8, 16, 2, fact_count // 2)
    facts = facts[:, :, 0] * 128 + facts[:, :, 1]
    vision = (patches.astype(jnp.float32) + branch).astype(jnp.bfloat16)
    merged_in = layer_norm(vision, merge_gain, merge_bias).reshape(-1, 4 * width)

    text = jnp.concatenate([text_kv[0], text_kv[1]], axis=1)
    text, merged_in = lax.optimization_barrier((text, merged_in))
    text = jnp.concatenate(
        [
            text,
            lax.ppermute(text, "z", [(0, 1), (1, 2), (2, 3)]),
            lax.ppermute(text, "z", [(0, 2), (1, 3)]),
        ],
        axis=0,
    )
    text = jnp.concatenate([text, swap(text, "yl")], axis=0)
    text = jnp.concatenate([text, swap(text, "c")], axis=0).reshape(12, SEQ, -1)

    columns = [
        gather_by_exchange(merged_in[at : at + CHUNK], DP, DP_COUNT).reshape(-1, 4 * width)
        for at in (0, CHUNK)
    ]
    wholes = []
    for column_in in columns:
        merged = jnp.dot(column_in, merge_weight, preferred_element_type=jnp.float32).astype(
            jnp.bfloat16
        )
        wholes.append(gather_by_exchange(merged, DP, DP_COUNT))
    image_kvs, image_queries = [], []
    for whole in wholes:
        image_query, image_kv = project(
            whole, attn_gain.reshape(DP_COUNT, 1, -1), query_weight, kv_weight
        )
        image_queries.append(image_query)
        image_kvs.append(image_kv)
    first = jnp.concatenate(
        [image_kvs[0]]
        + [
            lax.ppermute(image_kvs[0], "z", [(i, (i + step) % 4) for i in range(4)])
            for step in (1, 2, 3)
        ],
        axis=0,
    )
    first = jnp.concatenate([first, swap(first, "yl")], axis=0)
    first = jnp.concatenate([first, swap(first, "c")], axis=0).reshape(
        (CTX_COUNT,) + image_kvs[0].shape
    )

    sizes = jnp.swapaxes(facts[:, :, :4], 0, 1)
    offsets = jnp.swapaxes(facts[:, :, 4:8], 0, 1)
    starts = jnp.sum(facts[0, :, 8:], axis=0, dtype=jnp.int32)
    positions = row_positions(sizes.reshape(128, 4), offsets.reshape(128, 4), CAPACITY).reshape(
        16, 256
    )
    before = jnp.arange(256)[None, :] < jnp.arange(256)[:, None]
    own_owner = lax.dynamic_index_in_dim(positions, ctx_index, 0, False) // SEQ
    own_rank = jnp.sum(
        ((own_owner[None, :] == own_owner[:, None]) & before).astype(jnp.int32),
        axis=1,
        dtype=jnp.int32,
    )
    own_slot = (own_owner * CAPACITY + own_rank).reshape(8, 2, CHUNK).swapaxes(0, 1).reshape(-1)
    spread_out = (jnp.arange(512, dtype=jnp.int32)[:, None] == own_slot[None, :]).astype(
        jnp.bfloat16
    )
    mine = positions // SEQ == ctx_index
    rank = jnp.sum((mine[:, None, :] & before[None]).astype(jnp.int32), axis=2, dtype=jnp.int32)
    slot_here = mine[:, :, None] & (
        rank[:, :, None] == jnp.arange(CAPACITY, dtype=jnp.int32)[None, None, :]
    )
    slot_place = jnp.sum(
        jnp.where(slot_here, positions[:, :, None] - ctx_index * SEQ + 1, 0),
        axis=1,
        dtype=jnp.int32,
    ).reshape(-1) - 1
    bring_in = jnp.arange(SEQ, dtype=jnp.int32)[:, None] == slot_place[None, :]

    chunk_rows = DP_COUNT * CHUNK
    sent = sum(
        jnp.dot(
            spread_out[:, k * chunk_rows : (k + 1) * chunk_rows],
            image_queries[k],
            preferred_element_type=jnp.float32,
        )
        for k in (0, 1)
    ).astype(jnp.bfloat16)
    half = chunk_rows // 2
    folded = jnp.concatenate([image_kvs[1][:half], image_kvs[1][half:]], axis=1)
    last = lax.all_to_all(
        jnp.concatenate(
            [
                jnp.broadcast_to(folded[None], (CTX_COUNT,) + folded.shape),
                sent.reshape(CTX_COUNT, CAPACITY, -1),
            ],
            axis=1,
        ),
        CTX,
        split_axis=0,
        concat_axis=0,
    )

    window_start = jnp.maximum(ctx_index - REACH, 0) * SEQ
    low_rows = (
        jnp.sum(
            jnp.where(
                doc_ids[:, None] == jnp.arange(4, dtype=jnp.int32)[None, :], starts[None, :], 0
            ),
            axis=1,
            dtype=jnp.int32,
        )
        - window_start
    )
    low_rows = jnp.maximum(low_rows, 0)
    edges = low_rows.reshape(-1, QUERY_BLOCK)
    info = jnp.concatenate(
        [
            jnp.stack([window_start, ctx_index * SEQ - window_start]).astype(jnp.int32),
            jnp.stack([edges[:, 0], edges[:, -1]], axis=1).reshape(-1),
        ]
    )
    within_device = starts_within(sizes)
    source = jnp.arange(CTX_COUNT, dtype=jnp.int32)
    first_at = (
        ((source % 2) ^ c_at) * 8 + ((source // 2 % 2) ^ yl_at) * 4 + (z_at - source // 4 + 4) % 4
    )
    shard = window_start // SEQ + jnp.arange(REACH + 1, dtype=jnp.int32)
    text_at = (
        ((shard % 2) ^ c_at) * 6
        + ((shard // 2 % 2) ^ yl_at) * 3
        + jnp.clip(z_at - shard // 4, 0, 2)
    )
    image_src = (
        jnp.arange(CTX_COUNT * DP_COUNT, dtype=jnp.int32).reshape(CTX_COUNT, DP_COUNT, 1) * CAPACITY
        + within_device
    )
    return attention(
        info,
        image_src.reshape(-1),
        (offsets - window_start).reshape(-1),
        sizes.reshape(-1),
        jnp.concatenate([first_at, text_at]).astype(jnp.int32),
        text_query,
        bring_in.astype(jnp.bfloat16),
        low_rows[:, None],
        first,
        last,
        text,
    )


def solution(mesh):
    fine = Mesh(mesh.devices.reshape(2, 4, 4, 2, 2), DP + CTX)
    every = DP + CTX
    return jax.shard_map(
        body,
        mesh=fine,
        in_specs=(
            P(every, None),
            P(),
            P(),
            P(every, None),
            P(every, None),
            P(),
            P(),
            P(None, DP),
            P(),
            P(None, DP),
            P(None, None, DP),
            P(CTX, DP),
            P(None, CTX, DP),
            P(CTX),
            P(every, None),
            P(every, None),
        ),
        out_specs=P(CTX, DP),
        check_vma=False,
    )
```

```python
import math

import jax
import jax.numpy as jnp
import numpy as np
from jax import lax
from jax.experimental import pallas as pl
from jax.experimental.pallas import tpu as pltpu
from jax.sharding import Mesh
from jax.sharding import PartitionSpec as P

HEAD_DIM = 128
MOST = 16
SEQ = 640
REACH = 8
WINDOW = SEQ * (REACH + 1)
KEY_BLOCK = 640
PADDED = -(-WINDOW // KEY_BLOCK) * KEY_BLOCK
QUERY_BLOCK = 640
GROUP = 4
IMAGES = 512
PLACE_UNROLL = 4
CAPACITY = 32
CHUNK = 16
UNITS = 24
CTX_COUNT = 16
DP_COUNT = 8

MASKED_SCORE = -1e30
LOWEST_PEAK = -1e29
EPSILON = 1e-06
DP = ("yh", "x")
CTX = ("z", "yl", "c")


def layer_norm(rows_in, norm_gain, norm_bias):
    values = rows_in.astype(jnp.float32)
    center = values - jnp.mean(values, axis=-1, keepdims=True)
    spread = jnp.mean(center * center, axis=-1, keepdims=True)
    return (center * lax.rsqrt(spread + EPSILON) * norm_gain + norm_bias).astype(jnp.bfloat16)


def quick_gelu(values):
    return values * jax.nn.sigmoid(1.702 * values)


def starts_within(sizes):
    count = sizes.shape[-1]
    earlier = jnp.arange(count)[None, :] < jnp.arange(count)[:, None]
    return jnp.sum(jnp.where(earlier, sizes[..., None, :], 0), axis=-1, dtype=jnp.int32)


def row_positions(size_table, offset_table, row_count):
    image_starts = starts_within(size_table)
    image_ends = image_starts + size_table
    within = jnp.arange(row_count, dtype=jnp.int32)[None, :, None]
    inside = (within >= image_starts[:, None, :]) & (within < image_ends[:, None, :])
    placed = offset_table[:, None, :] - image_starts[:, None, :] + within
    return jnp.sum(jnp.where(inside, placed, 0), axis=2, dtype=jnp.int32)


def gather_by_exchange(block, axes, count):
    return lax.all_to_all(
        jnp.broadcast_to(block[None], (count,) + block.shape), axes, split_axis=0, concat_axis=0
    )


def swap(rows, axis):
    return lax.ppermute(rows, axis, [(0, 1), (1, 0)])


def attention_kernel(
    info,
    image_src,
    image_dst,
    image_len,
    blocks_at,
    text_query_ref,
    bring_ref,
    low_ref,
    first_near_ref,
    first_far_ref,
    last_ref,
    text_near_ref,
    text_far_ref,
    out_ref,
    text_held,
    key_wide,
    value_wide,
    image_key,
    image_value,
    image_query,
    key_held,
    value_held,
    sems,
):
    query_offset = info[1]
    half = CTX_COUNT // 2
    near = text_near_ref.shape[0]
    copies = []
    for shard in range(REACH + 1):
        at = blocks_at[CTX_COUNT + shard]
        target = text_held.at[pl.ds(shard * SEQ, SEQ), :]

        @pl.when(at < near)
        def _(at=at, target=target, shard=shard):
            pltpu.make_async_copy(text_near_ref.at[at], target, sems.at[shard]).start()

        @pl.when(at >= near)
        def _(at=at, target=target, shard=shard):
            pltpu.make_async_copy(text_far_ref.at[at - near], target, sems.at[shard]).start()

        copies.append(pltpu.make_async_copy(text_near_ref.at[0], target, sems.at[shard]))

    for side, first_ref in enumerate((first_near_ref, first_far_ref)):

        def widen_first(block, unused, side=side, first_ref=first_ref):
            source = blocks_at[side * half + block]
            for device in range(DP_COUNT):
                base = source * (DP_COUNT * CAPACITY) + device * CAPACITY
                rows = pl.ds(pl.multiple_of(base, CHUNK), CHUNK)
                held = first_ref[block, device * CHUNK : (device + 1) * CHUNK, :].astype(
                    jnp.float32
                )
                image_key[rows, :] = held[:, :HEAD_DIM]
                image_value[rows, :] = held[:, HEAD_DIM:]
            return unused

        lax.fori_loop(0, half, widen_first, 0)

    def widen_last(source, unused):
        for device in range(DP_COUNT):
            base = source * (DP_COUNT * CAPACITY) + device * CAPACITY + CHUNK
            rows = pl.ds(pl.multiple_of(base, CHUNK), CHUNK)
            at, side = device % 4 * CHUNK, device // 4 * 2 * HEAD_DIM
            held = last_ref[source, at : at + CHUNK, side : side + 2 * HEAD_DIM].astype(jnp.float32)
            image_key[rows, :] = held[:, :HEAD_DIM]
            image_value[rows, :] = held[:, HEAD_DIM:]
        rows = pl.ds(pl.multiple_of(source * CAPACITY, CAPACITY), CAPACITY)
        image_query[rows, :] = last_ref[source, 4 * CHUNK :, :]
        return unused

    lax.fori_loop(0, CTX_COUNT, widen_last, 0)
    for shard in range(REACH + 1):
        copies[shard].wait()

    def widen_text(step, unused):
        rows = pl.ds(pl.multiple_of(step * 320, 320), 320)
        key_wide[rows, :] = text_held[rows, :HEAD_DIM].astype(jnp.float32)
        value_wide[rows, :] = text_held[rows, HEAD_DIM:].astype(jnp.float32)
        return unused

    lax.fori_loop(0, WINDOW // 320, widen_text, 0)
    row_in = lax.broadcasted_iota(jnp.int32, (MOST, HEAD_DIM), 0)

    def place(step, unused):
        for lane in range(PLACE_UNROLL):
            image = step * PLACE_UNROLL + lane
            target = image_dst[image]
            origin = image_src[image]
            taken = row_in < image_len[image]
            rows = pl.ds(target, MOST)
            pltpu.store(key_wide.at[rows, :], image_key[pl.ds(origin, MOST), :], mask=taken)
            pltpu.store(value_wide.at[rows, :], image_value[pl.ds(origin, MOST), :], mask=taken)
        return unused

    lax.fori_loop(0, IMAGES // PLACE_UNROLL, place, 0)

    def narrow(step, unused):
        rows = pl.ds(pl.multiple_of(step * HEAD_DIM, HEAD_DIM), HEAD_DIM)
        key_held[rows, :] = key_wide[rows, :].astype(jnp.bfloat16)
        value_held[:HEAD_DIM, rows] = value_wide[rows, :].T.astype(jnp.bfloat16)
        return unused

    lax.fori_loop(0, WINDOW // HEAD_DIM, narrow, 0)
    value_held[HEAD_DIM:, :] = jnp.ones((CHUNK, PADDED), jnp.bfloat16)
    if PADDED > WINDOW:
        key_held[WINDOW:, :] = jnp.zeros((PADDED - WINDOW, HEAD_DIM), jnp.bfloat16)
        value_held[:HEAD_DIM, WINDOW:] = jnp.zeros((HEAD_DIM, PADDED - WINDOW), jnp.bfloat16)

    across = GROUP * QUERY_BLOCK
    to_power = math.log2(math.e) / math.sqrt(HEAD_DIM)
    column_at = lax.broadcasted_iota(jnp.int32, (1, QUERY_BLOCK), 1)

    def query_step(block, unused):
        rows = pl.ds(pl.multiple_of(block * QUERY_BLOCK, QUERY_BLOCK), QUERY_BLOCK)
        first = query_offset + block * QUERY_BLOCK
        bring = bring_ref[rows, :]
        is_image = jnp.max(bring.astype(jnp.float32), axis=-1, keepdims=True) > 0.5
        placed = jnp.where(
            is_image,
            jnp.dot(bring, image_query[...], preferred_element_type=jnp.float32),
            text_query_ref[rows, :].astype(jnp.float32),
        )
        queries = jnp.concatenate(
            [placed[:, h * HEAD_DIM : (h + 1) * HEAD_DIM].T for h in range(GROUP)], axis=1
        ).astype(jnp.bfloat16)
        lows = jnp.concatenate([low_ref[:, rows]] * GROUP, axis=1)
        highs = jnp.concatenate([column_at + first] * GROUP, axis=1)
        low_first = info[2 + 2 * block]
        low_last = info[3 + 2 * block]
        begin = low_first // KEY_BLOCK
        end = (first + QUERY_BLOCK - 1) // KEY_BLOCK + 1
        clear_begin = jnp.minimum((low_last + KEY_BLOCK - 1) // KEY_BLOCK, end)
        clear_end = jnp.maximum((first + 1) // KEY_BLOCK, clear_begin)

        def key_step(at, running, masked):
            peak, gathered = running
            keys_at = pl.ds(pl.multiple_of(at * KEY_BLOCK, KEY_BLOCK), KEY_BLOCK)
            scores = jnp.dot(key_held[keys_at, :], queries, preferred_element_type=jnp.float32)
            if masked:
                place_at = at * KEY_BLOCK + lax.broadcasted_iota(jnp.int32, (KEY_BLOCK, 1), 0)
                scores = jnp.where((place_at >= lows) & (place_at <= highs), scores, MASKED_SCORE)
            new_peak = jnp.maximum(peak, jnp.max(scores, axis=0, keepdims=True))
            weights = jnp.exp2((scores - new_peak) * to_power).astype(jnp.bfloat16)
            rescale = jnp.exp2((peak - new_peak) * to_power)
            gathered = gathered * rescale + jnp.dot(
                value_held[:, keys_at], weights, preferred_element_type=jnp.float32
            )
            return new_peak, gathered

        running = (
            jnp.full((1, across), LOWEST_PEAK, jnp.float32),
            jnp.zeros((HEAD_DIM + CHUNK, across), jnp.float32),
        )
        running = lax.fori_loop(begin, clear_begin, lambda a, r: key_step(a, r, True), running)
        running = lax.fori_loop(clear_begin, clear_end, lambda a, r: key_step(a, r, False), running)
        peak, gathered = lax.fori_loop(clear_end, end, lambda a, r: key_step(a, r, True), running)
        context = gathered[:HEAD_DIM] / gathered[HEAD_DIM : HEAD_DIM + 1]
        for h in range(GROUP):
            out_ref[rows, h * HEAD_DIM : (h + 1) * HEAD_DIM] = context[
                :, h * QUERY_BLOCK : (h + 1) * QUERY_BLOCK
            ].T.astype(jnp.bfloat16)
        return unused

    lax.fori_loop(0, SEQ // QUERY_BLOCK, query_step, 0)


def attention(tables, text_query, bring_in, low_rows, first, last, text):
    smem = pl.BlockSpec(memory_space=pltpu.SMEM)
    vmem = pl.BlockSpec(memory_space=pltpu.VMEM)
    image_rows = CTX_COUNT * DP_COUNT * CAPACITY
    return pl.pallas_call(
        attention_kernel,
        out_shape=jax.ShapeDtypeStruct(text_query.shape, jnp.bfloat16),
        in_specs=[smem] * 5 + [vmem] * 6 + [pl.BlockSpec(memory_space=pl.ANY)] * 2,
        out_specs=vmem,
        scratch_shapes=[
            pltpu.VMEM((WINDOW, 2 * HEAD_DIM), jnp.bfloat16),
            pltpu.VMEM((WINDOW + MOST, HEAD_DIM), jnp.float32),
            pltpu.VMEM((WINDOW + MOST, HEAD_DIM), jnp.float32),
            pltpu.VMEM((image_rows + MOST, HEAD_DIM), jnp.float32),
            pltpu.VMEM((image_rows + MOST, HEAD_DIM), jnp.float32),
            pltpu.VMEM((CTX_COUNT * CAPACITY, GROUP * HEAD_DIM), jnp.bfloat16),
            pltpu.VMEM((PADDED, HEAD_DIM), jnp.bfloat16),
            pltpu.VMEM((HEAD_DIM + CHUNK, PADDED), jnp.bfloat16),
            pltpu.SemaphoreType.DMA((REACH + 1,)),
        ],
        compiler_params=pltpu.CompilerParams(vmem_limit_bytes=48 * 1024 * 1024),
        cost_estimate=pl.CostEstimate(
            flops=8_000_000_000, bytes_accessed=8_000_000, transcendentals=13_000_000
        ),
    )(*tables, text_query, bring_in, low_rows, *first, last, *text)


def project_kernel(rows_ref, gain_ref, query_weight_ref, kv_weight_ref, query_ref, kv_ref, query_sum, kv_sum, squares):
    step = pl.program_id(0)

    @pl.when(step == 0)
    def _():
        query_sum[...] = jnp.zeros_like(query_sum)
        kv_sum[...] = jnp.zeros_like(kv_sum)
        squares[...] = jnp.zeros_like(squares)

    values = rows_ref[0].astype(jnp.float32)
    squares[...] += jnp.sum(values * values, axis=-1, keepdims=True)
    gained = (values * gain_ref[0]).astype(jnp.bfloat16)
    query_sum[...] += jnp.dot(gained, query_weight_ref[...], preferred_element_type=jnp.float32)
    kv_sum[:, :HEAD_DIM] += jnp.dot(gained, kv_weight_ref[0], preferred_element_type=jnp.float32)
    kv_sum[:, HEAD_DIM:] += jnp.dot(gained, kv_weight_ref[1], preferred_element_type=jnp.float32)

    @pl.when(step == DP_COUNT - 1)
    def _():
        scale = lax.rsqrt(squares[...] / (DP_COUNT * rows_ref.shape[2]) + EPSILON)
        query_ref[...] = (query_sum[...] * scale).astype(jnp.bfloat16)
        kv_ref[...] = (kv_sum[...] * scale).astype(jnp.bfloat16)


def project(whole, gain, query_weight, kv_weight):
    count, rows, part = whole.shape
    query_width, kv_width = query_weight.shape[1], kv_weight.shape[2]
    return pl.pallas_call(
        project_kernel,
        grid=(count,),
        out_shape=(
            jax.ShapeDtypeStruct((rows, query_width), jnp.bfloat16),
            jax.ShapeDtypeStruct((rows, 2 * kv_width), jnp.bfloat16),
        ),
        in_specs=[
            pl.BlockSpec((1, rows, part), lambda k: (k, 0, 0)),
            pl.BlockSpec((1, 1, part), lambda k: (k, 0, 0)),
            pl.BlockSpec((part, query_width), lambda k: (k, 0)),
            pl.BlockSpec((2, part, kv_width), lambda k: (0, k, 0)),
        ],
        out_specs=(
            pl.BlockSpec((rows, query_width), lambda k: (0, 0)),
            pl.BlockSpec((rows, 2 * kv_width), lambda k: (0, 0)),
        ),
        scratch_shapes=[
            pltpu.VMEM((rows, query_width), jnp.float32),
            pltpu.VMEM((rows, 2 * kv_width), jnp.float32),
            pltpu.VMEM((rows, 1), jnp.float32),
        ],
        compiler_params=pltpu.CompilerParams(vmem_limit_bytes=24 * 1024 * 1024),
        cost_estimate=pl.CostEstimate(
            flops=2 * rows * count * part * (query_width + 2 * kv_width),
            bytes_accessed=2 * count * part * (query_width + 2 * kv_width + rows),
            transcendentals=0,
        ),
    )(whole, gain, query_weight, kv_weight)


def body(
    patches,
    vision_gain,
    vision_bias,
    up_weight,
    down_weight,
    merge_gain,
    merge_bias,
    merge_weight,
    attn_gain,
    query_weight,
    kv_weight,
    text_query,
    text_kv,
    doc_ids,
    image_sizes,
    image_offsets,
):
    z_at, yl_at, c_at = lax.axis_index("z"), lax.axis_index("yl"), lax.axis_index("c")
    ctx_index = lax.axis_index(CTX)
    width = patches.shape[1]
    own_rows = patches.shape[0]
    units_own = up_weight.shape[0]

    below = jnp.sum(
        (doc_ids[:, None] < jnp.arange(4, dtype=jnp.int32)[None, :]).astype(jnp.int32),
        axis=0,
        dtype=jnp.int32,
    )
    facts = jnp.concatenate([image_sizes, image_offsets, below[None, :]], axis=1)
    facts = jnp.concatenate([facts // 128, facts % 128], axis=1).astype(jnp.bfloat16)
    fact_count = facts.shape[1]
    block = jnp.concatenate(
        [
            jnp.pad(up_weight, ((0, UNITS - units_own), (0, 0))),
            down_weight,
            jnp.pad(facts, ((0, UNITS - units_own - 1), (0, width - fact_count))),
        ],
        axis=0,
    )
    block = jnp.broadcast_to(block[None], (16,) + block.shape)
    block, patches = lax.optimization_barrier((block, patches))
    units = lax.all_to_all(block, DP + ("yl",), split_axis=0, concat_axis=0)
    normed = layer_norm(patches, vision_gain, vision_bias)
    column = jnp.concatenate(
        [normed]
        + [
            lax.ppermute(normed, "z", [(i, (i + step) % 4) for i in range(4)])
            for step in (1, 2, 3)
        ],
        axis=0,
    )
    near_rows = column.shape[0]
    near = jnp.concatenate([column, swap(column, "c")], axis=0)
    ups = units[:, :UNITS].reshape(-1, width)
    downs = units[:, UNITS:].reshape(-1, width)
    facts = units[:, UNITS + units_own, :fact_count].reshape(1, -1)
    hidden = quick_gelu(
        lax.dot_general(near, ups, (((1,), (1,)), ((), ())), preferred_element_type=jnp.float32)
    ).astype(jnp.bfloat16)
    away = jnp.dot(hidden[near_rows:], downs, preferred_element_type=jnp.float32).astype(
        jnp.bfloat16
    )
    here = jnp.dot(hidden[:near_rows], downs, preferred_element_type=jnp.float32)
    came = swap(
        jnp.concatenate(
            [away, jnp.pad(facts, ((0, CHUNK - 1), (0, width - facts.shape[1])))], axis=0
        ),
        "c",
    )
    pair_sum = (here + came[:near_rows].astype(jnp.float32)).astype(jnp.bfloat16)
    other = came[near_rows : near_rows + 1, : facts.shape[1]]
    facts = jnp.concatenate(
        [jnp.where(c_at == 0, facts, other), jnp.where(c_at == 0, other, facts)], axis=1
    )
    tail = jnp.pad(facts, ((0, CHUNK - 1), (0, width - facts.shape[1])))
    by_z = pair_sum.reshape(4, own_rows, width)
    terms = lax.all_to_all(
        jnp.stack(
            [
                jnp.concatenate(
                    [lax.dynamic_index_in_dim(by_z, (z_at - j + 4) % 4, 0, False), tail], axis=0
                )
                for j in range(4)
            ]
        ),
        "z",
        split_axis=0,
        concat_axis=0,
    )
    branch = jnp.sum(terms[:, :own_rows].astype(jnp.float32), axis=0)
    facts = terms[:, own_rows, : facts.shape[1]].astype(jnp.int32)
    facts = facts.reshape(4, 2, 8, 2, fact_count).transpose(2, 0, 3, 1, 4)
    facts = facts.reshape(8, 16, 2, fact_count // 2)
    facts = facts[:, :, 0] * 128 + facts[:, :, 1]
    vision = (patches.astype(jnp.float32) + branch).astype(jnp.bfloat16)
    merged_in = layer_norm(vision, merge_gain, merge_bias).reshape(-1, 4 * width)

    text = jnp.concatenate([text_kv[0], text_kv[1]], axis=1)
    text, merged_in = lax.optimization_barrier((text, merged_in))
    text = jnp.concatenate(
        [
            text,
            lax.ppermute(text, "z", [(0, 1), (1, 2), (2, 3)]),
            lax.ppermute(text, "z", [(0, 2), (1, 3)]),
        ],
        axis=0,
    )
    columns = [
        gather_by_exchange(merged_in[at : at + CHUNK], DP, DP_COUNT).reshape(-1, 4 * width)
        for at in (0, CHUNK)
    ]
    text, columns[0] = lax.optimization_barrier((text, columns[0]))
    text = jnp.concatenate([text, swap(text, "yl")], axis=0)
    spread_rows = []
    for column_in in columns:
        merged = jnp.dot(column_in, merge_weight, preferred_element_type=jnp.float32).astype(
            jnp.bfloat16
        )
        spread_rows.append(jnp.broadcast_to(merged[None], (DP_COUNT,) + merged.shape))
    text, spread_rows[1] = lax.optimization_barrier((text, spread_rows[1]))
    wholes = [lax.all_to_all(rows, DP, split_axis=0, concat_axis=0) for rows in spread_rows]
    gains = attn_gain.reshape(DP_COUNT, 1, -1)
    image_queries, image_kvs = [None, None], [None, None]
    image_queries[0], image_kvs[0] = project(wholes[0], gains, query_weight, kv_weight)
    first = jnp.concatenate(
        [image_kvs[0]]
        + [
            lax.ppermute(image_kvs[0], "z", [(i, (i + step) % 4) for i in range(4)])
            for step in (1, 2, 3)
        ],
        axis=0,
    )
    first = jnp.concatenate([first, swap(first, "yl")], axis=0)
    first_far, text_far = swap(first, "c"), swap(text, "c")
    first_far, text_far, wholes[1] = lax.optimization_barrier((first_far, text_far, wholes[1]))
    first = [half.reshape((8,) + image_kvs[0].shape) for half in (first, first_far)]
    text = [half.reshape(6, SEQ, -1) for half in (text, text_far)]
    image_queries[1], image_kvs[1] = project(wholes[1], gains, query_weight, kv_weight)

    sizes = jnp.swapaxes(facts[:, :, :4], 0, 1)
    offsets = jnp.swapaxes(facts[:, :, 4:8], 0, 1)
    starts = jnp.sum(facts[0, :, 8:], axis=0, dtype=jnp.int32)
    positions = row_positions(sizes.reshape(128, 4), offsets.reshape(128, 4), CAPACITY).reshape(
        16, 256
    )
    before = jnp.arange(256)[None, :] < jnp.arange(256)[:, None]
    own_owner = lax.dynamic_index_in_dim(positions, ctx_index, 0, False) // SEQ
    own_rank = jnp.sum(
        ((own_owner[None, :] == own_owner[:, None]) & before).astype(jnp.int32),
        axis=1,
        dtype=jnp.int32,
    )
    own_slot = (own_owner * CAPACITY + own_rank).reshape(8, 2, CHUNK).swapaxes(0, 1).reshape(-1)
    spread_out = (jnp.arange(512, dtype=jnp.int32)[:, None] == own_slot[None, :]).astype(
        jnp.bfloat16
    )
    mine = positions // SEQ == ctx_index
    rank = jnp.sum((mine[:, None, :] & before[None]).astype(jnp.int32), axis=2, dtype=jnp.int32)
    slot_here = mine[:, :, None] & (
        rank[:, :, None] == jnp.arange(CAPACITY, dtype=jnp.int32)[None, None, :]
    )
    slot_place = jnp.sum(
        jnp.where(slot_here, positions[:, :, None] - ctx_index * SEQ + 1, 0),
        axis=1,
        dtype=jnp.int32,
    ).reshape(-1) - 1
    bring_in = jnp.arange(SEQ, dtype=jnp.int32)[:, None] == slot_place[None, :]

    chunk_rows = DP_COUNT * CHUNK
    sent = sum(
        jnp.dot(
            spread_out[:, k * chunk_rows : (k + 1) * chunk_rows],
            image_queries[k],
            preferred_element_type=jnp.float32,
        )
        for k in (0, 1)
    ).astype(jnp.bfloat16)
    half = chunk_rows // 2
    folded = jnp.concatenate([image_kvs[1][:half], image_kvs[1][half:]], axis=1)
    last = lax.all_to_all(
        jnp.concatenate(
            [
                jnp.broadcast_to(folded[None], (CTX_COUNT,) + folded.shape),
                sent.reshape(CTX_COUNT, CAPACITY, -1),
            ],
            axis=1,
        ),
        CTX,
        split_axis=0,
        concat_axis=0,
    )

    window_start = jnp.maximum(ctx_index - REACH, 0) * SEQ
    low_rows = (
        jnp.sum(
            jnp.where(
                doc_ids[:, None] == jnp.arange(4, dtype=jnp.int32)[None, :], starts[None, :], 0
            ),
            axis=1,
            dtype=jnp.int32,
        )
        - window_start
    )
    low_rows = jnp.maximum(low_rows, 0)
    edges = low_rows.reshape(-1, QUERY_BLOCK)
    info = jnp.concatenate(
        [
            jnp.stack([window_start, ctx_index * SEQ - window_start]).astype(jnp.int32),
            jnp.stack([edges[:, 0], edges[:, -1]], axis=1).reshape(-1),
        ]
    )
    within_device = starts_within(sizes)
    block = jnp.arange(CTX_COUNT, dtype=jnp.int32)
    first_from = (
        (z_at - block % 4 + 4) % 4 * 4 + ((block // 4 % 2) ^ yl_at) * 2 + ((block // 8) ^ c_at)
    )
    shard = window_start // SEQ + jnp.arange(REACH + 1, dtype=jnp.int32)
    text_at = (
        ((shard % 2) ^ c_at) * 6
        + ((shard // 2 % 2) ^ yl_at) * 3
        + jnp.clip(z_at - shard // 4, 0, 2)
    )
    image_src = (
        jnp.arange(CTX_COUNT * DP_COUNT, dtype=jnp.int32).reshape(CTX_COUNT, DP_COUNT, 1) * CAPACITY
        + within_device
    )
    targets = (offsets - window_start).reshape(-1)
    inside = (targets >= 0) & (targets < WINDOW)
    tables = (
        info,
        image_src.reshape(-1),
        jnp.where(inside, targets, 0),
        jnp.where(inside, sizes.reshape(-1), 0),
        jnp.concatenate([first_from, text_at]).astype(jnp.int32),
    )
    return attention(
        tables, text_query, bring_in.astype(jnp.bfloat16), low_rows[None, :], first, last, text
    )


def solution(mesh):
    fine = Mesh(mesh.devices.reshape(2, 4, 4, 2, 2), DP + CTX)
    every = DP + CTX
    return jax.shard_map(
        body,
        mesh=fine,
        in_specs=(
            P(every, None),
            P(),
            P(),
            P(every, None),
            P(every, None),
            P(),
            P(),
            P(None, DP),
            P(),
            P(None, DP),
            P(None, None, DP),
            P(CTX, DP),
            P(None, CTX, DP),
            P(CTX),
            P(every, None),
            P(every, None),
        ),
        out_specs=P(CTX, DP),
        check_vma=False,
    )
```

```python
import math

import jax
import jax.numpy as jnp
import numpy as np
from jax import lax
from jax.experimental import pallas as pl
from jax.experimental.pallas import tpu as pltpu
from jax.sharding import Mesh
from jax.sharding import PartitionSpec as P

HEAD_DIM = 128
MOST = 16
SEQ = 640
REACH = 8
WINDOW = SEQ * (REACH + 1)
KEY_BLOCK = 640
PADDED = -(-WINDOW // KEY_BLOCK) * KEY_BLOCK
QUERY_BLOCK = 640
GROUP = 4
IMAGES = 512
PLACE_UNROLL = 4
CAPACITY = 32
CHUNK = 16
UNITS = 24
CTX_COUNT = 16
DP_COUNT = 8

MASKED_SCORE = -1e30
LOWEST_PEAK = -1e29
EPSILON = 1e-06
DP = ("yh", "x")
CTX = ("z", "yl", "c")


def layer_norm(rows_in, norm_gain, norm_bias):
    values = rows_in.astype(jnp.float32)
    center = values - jnp.mean(values, axis=-1, keepdims=True)
    spread = jnp.mean(center * center, axis=-1, keepdims=True)
    return (center * lax.rsqrt(spread + EPSILON) * norm_gain + norm_bias).astype(jnp.bfloat16)


def quick_gelu(values):
    return values * jax.nn.sigmoid(1.702 * values)


def starts_within(sizes):
    count = sizes.shape[-1]
    earlier = jnp.arange(count)[None, :] < jnp.arange(count)[:, None]
    return jnp.sum(jnp.where(earlier, sizes[..., None, :], 0), axis=-1, dtype=jnp.int32)


def row_positions(size_table, offset_table, row_count):
    image_starts = starts_within(size_table)
    image_ends = image_starts + size_table
    within = jnp.arange(row_count, dtype=jnp.int32)[None, :, None]
    inside = (within >= image_starts[:, None, :]) & (within < image_ends[:, None, :])
    placed = offset_table[:, None, :] - image_starts[:, None, :] + within
    return jnp.sum(jnp.where(inside, placed, 0), axis=2, dtype=jnp.int32)


def gather_by_exchange(block, axes, count):
    return lax.all_to_all(
        jnp.broadcast_to(block[None], (count,) + block.shape), axes, split_axis=0, concat_axis=0
    )


def swap(rows, axis):
    return lax.ppermute(rows, axis, [(0, 1), (1, 0)])


def attention_kernel(
    info,
    image_src,
    image_dst,
    image_len,
    blocks_at,
    text_query_ref,
    bring_ref,
    low_ref,
    first_near_ref,
    first_far_ref,
    last_ref,
    text_near_ref,
    text_far_ref,
    out_ref,
    text_held,
    key_wide,
    value_wide,
    image_key,
    image_value,
    image_query,
    key_held,
    value_held,
    sems,
):
    query_offset = info[1]
    half = CTX_COUNT // 2
    near = text_near_ref.shape[0]
    copies = []
    for shard in range(REACH + 1):
        at = blocks_at[CTX_COUNT + shard]
        target = text_held.at[pl.ds(shard * SEQ, SEQ), :]

        @pl.when(at < near)
        def _(at=at, target=target, shard=shard):
            pltpu.make_async_copy(text_near_ref.at[at], target, sems.at[shard]).start()

        @pl.when(at >= near)
        def _(at=at, target=target, shard=shard):
            pltpu.make_async_copy(text_far_ref.at[at - near], target, sems.at[shard]).start()

        copies.append(pltpu.make_async_copy(text_near_ref.at[0], target, sems.at[shard]))

    for side, first_ref in enumerate((first_near_ref, first_far_ref)):

        def widen_first(block, unused, side=side, first_ref=first_ref):
            source = blocks_at[side * half + block]
            for device in range(DP_COUNT):
                base = source * (DP_COUNT * CAPACITY) + device * CAPACITY
                rows = pl.ds(pl.multiple_of(base, CHUNK), CHUNK)
                held = first_ref[block, device * CHUNK : (device + 1) * CHUNK, :].astype(
                    jnp.float32
                )
                image_key[rows, :] = held[:, :HEAD_DIM]
                image_value[rows, :] = held[:, HEAD_DIM:]
            return unused

        lax.fori_loop(0, half, widen_first, 0)

    def widen_last(source, unused):
        for device in range(DP_COUNT):
            base = source * (DP_COUNT * CAPACITY) + device * CAPACITY + CHUNK
            rows = pl.ds(pl.multiple_of(base, CHUNK), CHUNK)
            at, side = device % 4 * CHUNK, device // 4 * 2 * HEAD_DIM
            held = last_ref[source, at : at + CHUNK, side : side + 2 * HEAD_DIM].astype(jnp.float32)
            image_key[rows, :] = held[:, :HEAD_DIM]
            image_value[rows, :] = held[:, HEAD_DIM:]
        rows = pl.ds(pl.multiple_of(source * CAPACITY, CAPACITY), CAPACITY)
        image_query[rows, :] = last_ref[source, 4 * CHUNK :, :]
        return unused

    lax.fori_loop(0, CTX_COUNT, widen_last, 0)
    for shard in range(REACH + 1):
        copies[shard].wait()

    def widen_text(step, unused):
        rows = pl.ds(pl.multiple_of(step * 320, 320), 320)
        key_wide[rows, :] = text_held[rows, :HEAD_DIM].astype(jnp.float32)
        value_wide[rows, :] = text_held[rows, HEAD_DIM:].astype(jnp.float32)
        return unused

    lax.fori_loop(0, WINDOW // 320, widen_text, 0)
    row_in = lax.broadcasted_iota(jnp.int32, (MOST, HEAD_DIM), 0)

    def place(step, unused):
        for lane in range(PLACE_UNROLL):
            image = step * PLACE_UNROLL + lane
            target = image_dst[image]
            origin = image_src[image]
            taken = row_in < image_len[image]
            rows = pl.ds(target, MOST)
            pltpu.store(key_wide.at[rows, :], image_key[pl.ds(origin, MOST), :], mask=taken)
            pltpu.store(value_wide.at[rows, :], image_value[pl.ds(origin, MOST), :], mask=taken)
        return unused

    lax.fori_loop(0, IMAGES // PLACE_UNROLL, place, 0)

    def narrow(step, unused):
        rows = pl.ds(pl.multiple_of(step * HEAD_DIM, HEAD_DIM), HEAD_DIM)
        key_held[rows, :] = key_wide[rows, :].astype(jnp.bfloat16)
        value_held[:HEAD_DIM, rows] = value_wide[rows, :].T.astype(jnp.bfloat16)
        return unused

    lax.fori_loop(0, WINDOW // HEAD_DIM, narrow, 0)
    value_held[HEAD_DIM:, :] = jnp.ones((CHUNK, PADDED), jnp.bfloat16)
    if PADDED > WINDOW:
        key_held[WINDOW:, :] = jnp.zeros((PADDED - WINDOW, HEAD_DIM), jnp.bfloat16)
        value_held[:HEAD_DIM, WINDOW:] = jnp.zeros((HEAD_DIM, PADDED - WINDOW), jnp.bfloat16)

    across = GROUP * QUERY_BLOCK
    to_power = math.log2(math.e) / math.sqrt(HEAD_DIM)
    column_at = lax.broadcasted_iota(jnp.int32, (1, QUERY_BLOCK), 1)

    def query_step(block, unused):
        rows = pl.ds(pl.multiple_of(block * QUERY_BLOCK, QUERY_BLOCK), QUERY_BLOCK)
        first = query_offset + block * QUERY_BLOCK
        bring = bring_ref[rows, :]
        is_image = jnp.max(bring.astype(jnp.float32), axis=-1, keepdims=True) > 0.5
        placed = jnp.where(
            is_image,
            jnp.dot(bring, image_query[...], preferred_element_type=jnp.float32),
            text_query_ref[rows, :].astype(jnp.float32),
        )
        queries = jnp.concatenate(
            [placed[:, h * HEAD_DIM : (h + 1) * HEAD_DIM].T for h in range(GROUP)], axis=1
        ).astype(jnp.bfloat16)
        lows = jnp.concatenate([low_ref[:, rows]] * GROUP, axis=1)
        highs = jnp.concatenate([column_at + first] * GROUP, axis=1)
        low_first = info[2 + 2 * block]
        low_last = info[3 + 2 * block]
        begin = low_first // KEY_BLOCK
        end = (first + QUERY_BLOCK - 1) // KEY_BLOCK + 1
        clear_begin = jnp.minimum((low_last + KEY_BLOCK - 1) // KEY_BLOCK, end)
        clear_end = jnp.maximum((first + 1) // KEY_BLOCK, clear_begin)

        def key_step(at, running, masked):
            peak, gathered = running
            keys_at = pl.ds(pl.multiple_of(at * KEY_BLOCK, KEY_BLOCK), KEY_BLOCK)
            scores = jnp.dot(key_held[keys_at, :], queries, preferred_element_type=jnp.float32)
            if masked:
                place_at = at * KEY_BLOCK + lax.broadcasted_iota(jnp.int32, (KEY_BLOCK, 1), 0)
                scores = jnp.where((place_at >= lows) & (place_at <= highs), scores, MASKED_SCORE)
            new_peak = jnp.maximum(peak, jnp.max(scores, axis=0, keepdims=True))
            weights = jnp.exp2((scores - new_peak) * to_power).astype(jnp.bfloat16)
            rescale = jnp.exp2((peak - new_peak) * to_power)
            gathered = gathered * rescale + jnp.dot(
                value_held[:, keys_at], weights, preferred_element_type=jnp.float32
            )
            return new_peak, gathered

        running = (
            jnp.full((1, across), LOWEST_PEAK, jnp.float32),
            jnp.zeros((HEAD_DIM + CHUNK, across), jnp.float32),
        )
        running = lax.fori_loop(begin, clear_begin, lambda a, r: key_step(a, r, True), running)
        running = lax.fori_loop(clear_begin, clear_end, lambda a, r: key_step(a, r, False), running)
        peak, gathered = lax.fori_loop(clear_end, end, lambda a, r: key_step(a, r, True), running)
        context = gathered[:HEAD_DIM] / gathered[HEAD_DIM : HEAD_DIM + 1]
        for h in range(GROUP):
            out_ref[rows, h * HEAD_DIM : (h + 1) * HEAD_DIM] = context[
                :, h * QUERY_BLOCK : (h + 1) * QUERY_BLOCK
            ].T.astype(jnp.bfloat16)
        return unused

    lax.fori_loop(0, SEQ // QUERY_BLOCK, query_step, 0)


def attention(tables, text_query, bring_in, low_rows, first, last, text):
    smem = pl.BlockSpec(memory_space=pltpu.SMEM)
    vmem = pl.BlockSpec(memory_space=pltpu.VMEM)
    image_rows = CTX_COUNT * DP_COUNT * CAPACITY
    return pl.pallas_call(
        attention_kernel,
        out_shape=jax.ShapeDtypeStruct(text_query.shape, jnp.bfloat16),
        in_specs=[smem] * 5 + [vmem] * 6 + [pl.BlockSpec(memory_space=pl.ANY)] * 2,
        out_specs=vmem,
        scratch_shapes=[
            pltpu.VMEM((WINDOW, 2 * HEAD_DIM), jnp.bfloat16),
            pltpu.VMEM((WINDOW + MOST, HEAD_DIM), jnp.float32),
            pltpu.VMEM((WINDOW + MOST, HEAD_DIM), jnp.float32),
            pltpu.VMEM((image_rows + MOST, HEAD_DIM), jnp.float32),
            pltpu.VMEM((image_rows + MOST, HEAD_DIM), jnp.float32),
            pltpu.VMEM((CTX_COUNT * CAPACITY, GROUP * HEAD_DIM), jnp.bfloat16),
            pltpu.VMEM((PADDED, HEAD_DIM), jnp.bfloat16),
            pltpu.VMEM((HEAD_DIM + CHUNK, PADDED), jnp.bfloat16),
            pltpu.SemaphoreType.DMA((REACH + 1,)),
        ],
        compiler_params=pltpu.CompilerParams(vmem_limit_bytes=48 * 1024 * 1024),
        cost_estimate=pl.CostEstimate(
            flops=8_000_000_000, bytes_accessed=8_000_000, transcendentals=13_000_000
        ),
    )(*tables, text_query, bring_in, low_rows, *first, last, *text)


def project_kernel(rows_ref, gain_ref, query_weight_ref, kv_weight_ref, query_ref, kv_ref, query_sum, kv_sum, squares):
    step = pl.program_id(0)

    @pl.when(step == 0)
    def _():
        query_sum[...] = jnp.zeros_like(query_sum)
        kv_sum[...] = jnp.zeros_like(kv_sum)
        squares[...] = jnp.zeros_like(squares)

    values = rows_ref[0].astype(jnp.float32)
    squares[...] += jnp.sum(values * values, axis=-1, keepdims=True)
    gained = (values * gain_ref[0]).astype(jnp.bfloat16)
    query_sum[...] += jnp.dot(gained, query_weight_ref[...], preferred_element_type=jnp.float32)
    kv_sum[:, :HEAD_DIM] += jnp.dot(gained, kv_weight_ref[0], preferred_element_type=jnp.float32)
    kv_sum[:, HEAD_DIM:] += jnp.dot(gained, kv_weight_ref[1], preferred_element_type=jnp.float32)

    @pl.when(step == DP_COUNT - 1)
    def _():
        scale = lax.rsqrt(squares[...] / (DP_COUNT * rows_ref.shape[2]) + EPSILON)
        query_ref[...] = (query_sum[...] * scale).astype(jnp.bfloat16)
        kv_ref[...] = (kv_sum[...] * scale).astype(jnp.bfloat16)


def project(whole, gain, query_weight, kv_weight):
    count, rows, part = whole.shape
    query_width, kv_width = query_weight.shape[1], kv_weight.shape[2]
    return pl.pallas_call(
        project_kernel,
        grid=(count,),
        out_shape=(
            jax.ShapeDtypeStruct((rows, query_width), jnp.bfloat16),
            jax.ShapeDtypeStruct((rows, 2 * kv_width), jnp.bfloat16),
        ),
        in_specs=[
            pl.BlockSpec((1, rows, part), lambda k: (k, 0, 0)),
            pl.BlockSpec((1, 1, part), lambda k: (k, 0, 0)),
            pl.BlockSpec((part, query_width), lambda k: (k, 0)),
            pl.BlockSpec((2, part, kv_width), lambda k: (0, k, 0)),
        ],
        out_specs=(
            pl.BlockSpec((rows, query_width), lambda k: (0, 0)),
            pl.BlockSpec((rows, 2 * kv_width), lambda k: (0, 0)),
        ),
        scratch_shapes=[
            pltpu.VMEM((rows, query_width), jnp.float32),
            pltpu.VMEM((rows, 2 * kv_width), jnp.float32),
            pltpu.VMEM((rows, 1), jnp.float32),
        ],
        compiler_params=pltpu.CompilerParams(vmem_limit_bytes=24 * 1024 * 1024),
        cost_estimate=pl.CostEstimate(
            flops=2 * rows * count * part * (query_width + 2 * kv_width),
            bytes_accessed=2 * count * part * (query_width + 2 * kv_width + rows),
            transcendentals=0,
        ),
    )(whole, gain, query_weight, kv_weight)


def body(
    patches,
    vision_gain,
    vision_bias,
    up_weight,
    down_weight,
    merge_gain,
    merge_bias,
    merge_weight,
    attn_gain,
    query_weight,
    kv_weight,
    text_query,
    text_kv,
    doc_ids,
    image_sizes,
    image_offsets,
):
    z_at, yl_at, c_at = lax.axis_index("z"), lax.axis_index("yl"), lax.axis_index("c")
    ctx_index = lax.axis_index(CTX)
    width = patches.shape[1]
    own_rows = patches.shape[0]
    units_own = up_weight.shape[0]

    below = jnp.sum(
        (doc_ids[:, None] < jnp.arange(4, dtype=jnp.int32)[None, :]).astype(jnp.int32),
        axis=0,
        dtype=jnp.int32,
    )
    facts = jnp.concatenate([image_sizes, image_offsets, below[None, :]], axis=1)
    facts = jnp.concatenate([facts // 128, facts % 128], axis=1).astype(jnp.bfloat16)
    fact_count = facts.shape[1]
    block = jnp.concatenate(
        [
            jnp.pad(up_weight, ((0, UNITS - units_own), (0, 0))),
            down_weight,
            jnp.pad(facts, ((0, UNITS - units_own - 1), (0, width - fact_count))),
        ],
        axis=0,
    )
    block = jnp.broadcast_to(block[None], (16,) + block.shape)
    block, patches = lax.optimization_barrier((block, patches))
    units = lax.all_to_all(block, DP + ("yl",), split_axis=0, concat_axis=0)
    text = jnp.concatenate([text_kv[0], text_kv[1]], axis=1)
    text, units = lax.optimization_barrier((text, units))
    text = jnp.concatenate([text, swap(text, "yl")], axis=0)
    normed = layer_norm(patches, vision_gain, vision_bias)
    column = jnp.concatenate(
        [normed]
        + [
            lax.ppermute(normed, "z", [(i, (i + step) % 4) for i in range(4)])
            for step in (1, 2, 3)
        ],
        axis=0,
    )
    near_rows = column.shape[0]
    near = jnp.concatenate([column, swap(column, "c")], axis=0)
    ups = units[:, :UNITS].reshape(-1, width)
    downs = units[:, UNITS:].reshape(-1, width)
    facts = units[:, UNITS + units_own, :fact_count].reshape(1, -1)
    hidden = quick_gelu(
        lax.dot_general(near, ups, (((1,), (1,)), ((), ())), preferred_element_type=jnp.float32)
    ).astype(jnp.bfloat16)
    away = jnp.dot(hidden[near_rows:], downs, preferred_element_type=jnp.float32).astype(
        jnp.bfloat16
    )
    here = jnp.dot(hidden[:near_rows], downs, preferred_element_type=jnp.float32)
    came = swap(
        jnp.concatenate(
            [away, jnp.pad(facts, ((0, CHUNK - 1), (0, width - facts.shape[1])))], axis=0
        ),
        "c",
    )
    pair_sum = (here + came[:near_rows].astype(jnp.float32)).astype(jnp.bfloat16)
    other = came[near_rows : near_rows + 1, : facts.shape[1]]
    facts = jnp.concatenate(
        [jnp.where(c_at == 0, facts, other), jnp.where(c_at == 0, other, facts)], axis=1
    )
    tail = jnp.pad(facts, ((0, CHUNK - 1), (0, width - facts.shape[1])))
    by_z = pair_sum.reshape(4, own_rows, width)
    terms = lax.all_to_all(
        jnp.stack(
            [
                jnp.concatenate(
                    [lax.dynamic_index_in_dim(by_z, (z_at - j + 4) % 4, 0, False), tail], axis=0
                )
                for j in range(4)
            ]
        ),
        "z",
        split_axis=0,
        concat_axis=0,
    )
    branch = jnp.sum(terms[:, :own_rows].astype(jnp.float32), axis=0)
    facts = terms[:, own_rows, : facts.shape[1]].astype(jnp.int32)
    facts = facts.reshape(4, 2, 8, 2, fact_count).transpose(2, 0, 3, 1, 4)
    facts = facts.reshape(8, 16, 2, fact_count // 2)
    facts = facts[:, :, 0] * 128 + facts[:, :, 1]
    vision = (patches.astype(jnp.float32) + branch).astype(jnp.bfloat16)
    merged_in = layer_norm(vision, merge_gain, merge_bias).reshape(-1, 4 * width)

    text, merged_in = lax.optimization_barrier((text, merged_in))
    text = jnp.concatenate(
        [
            text,
            lax.ppermute(text, "z", [(0, 1), (1, 2), (2, 3)]),
            lax.ppermute(text, "z", [(0, 2), (1, 3)]),
        ],
        axis=0,
    )
    columns = [
        gather_by_exchange(merged_in[at : at + CHUNK], DP, DP_COUNT).reshape(-1, 4 * width)
        for at in (0, CHUNK)
    ]
    spread_rows = []
    for column_in in columns:
        merged = jnp.dot(column_in, merge_weight, preferred_element_type=jnp.float32).astype(
            jnp.bfloat16
        )
        spread_rows.append(jnp.broadcast_to(merged[None], (DP_COUNT,) + merged.shape))
    text, spread_rows[1] = lax.optimization_barrier((text, spread_rows[1]))
    wholes = [lax.all_to_all(rows, DP, split_axis=0, concat_axis=0) for rows in spread_rows]
    gains = attn_gain.reshape(DP_COUNT, 1, -1)
    image_queries, image_kvs = [None, None], [None, None]
    image_queries[0], image_kvs[0] = project(wholes[0], gains, query_weight, kv_weight)
    first = jnp.concatenate(
        [image_kvs[0]]
        + [
            lax.ppermute(image_kvs[0], "z", [(i, (i + step) % 4) for i in range(4)])
            for step in (1, 2, 3)
        ],
        axis=0,
    )
    first = jnp.concatenate([first, swap(first, "yl")], axis=0)
    first_far, text_far = swap(first, "c"), swap(text, "c")
    first_far, text_far, wholes[1] = lax.optimization_barrier((first_far, text_far, wholes[1]))
    first = [half.reshape((8,) + image_kvs[0].shape) for half in (first, first_far)]
    text = [half.reshape(6, SEQ, -1) for half in (text, text_far)]
    image_queries[1], image_kvs[1] = project(wholes[1], gains, query_weight, kv_weight)

    sizes = jnp.swapaxes(facts[:, :, :4], 0, 1)
    offsets = jnp.swapaxes(facts[:, :, 4:8], 0, 1)
    starts = jnp.sum(facts[0, :, 8:], axis=0, dtype=jnp.int32)
    positions = row_positions(sizes.reshape(128, 4), offsets.reshape(128, 4), CAPACITY).reshape(
        16, 256
    )
    before = jnp.arange(256)[None, :] < jnp.arange(256)[:, None]
    own_owner = lax.dynamic_index_in_dim(positions, ctx_index, 0, False) // SEQ
    own_rank = jnp.sum(
        ((own_owner[None, :] == own_owner[:, None]) & before).astype(jnp.int32),
        axis=1,
        dtype=jnp.int32,
    )
    own_slot = (own_owner * CAPACITY + own_rank).reshape(8, 2, CHUNK).swapaxes(0, 1).reshape(-1)
    spread_out = (jnp.arange(512, dtype=jnp.int32)[:, None] == own_slot[None, :]).astype(
        jnp.bfloat16
    )
    mine = positions // SEQ == ctx_index
    rank = jnp.sum((mine[:, None, :] & before[None]).astype(jnp.int32), axis=2, dtype=jnp.int32)
    slot_here = mine[:, :, None] & (
        rank[:, :, None] == jnp.arange(CAPACITY, dtype=jnp.int32)[None, None, :]
    )
    slot_place = jnp.sum(
        jnp.where(slot_here, positions[:, :, None] - ctx_index * SEQ + 1, 0),
        axis=1,
        dtype=jnp.int32,
    ).reshape(-1) - 1
    bring_in = jnp.arange(SEQ, dtype=jnp.int32)[:, None] == slot_place[None, :]

    chunk_rows = DP_COUNT * CHUNK
    sent = sum(
        jnp.dot(
            spread_out[:, k * chunk_rows : (k + 1) * chunk_rows],
            image_queries[k],
            preferred_element_type=jnp.float32,
        )
        for k in (0, 1)
    ).astype(jnp.bfloat16)
    half = chunk_rows // 2
    folded = jnp.concatenate([image_kvs[1][:half], image_kvs[1][half:]], axis=1)
    last = lax.all_to_all(
        jnp.concatenate(
            [
                jnp.broadcast_to(folded[None], (CTX_COUNT,) + folded.shape),
                sent.reshape(CTX_COUNT, CAPACITY, -1),
            ],
            axis=1,
        ),
        CTX,
        split_axis=0,
        concat_axis=0,
    )

    window_start = jnp.maximum(ctx_index - REACH, 0) * SEQ
    low_rows = (
        jnp.sum(
            jnp.where(
                doc_ids[:, None] == jnp.arange(4, dtype=jnp.int32)[None, :], starts[None, :], 0
            ),
            axis=1,
            dtype=jnp.int32,
        )
        - window_start
    )
    low_rows = jnp.maximum(low_rows, 0)
    edges = low_rows.reshape(-1, QUERY_BLOCK)
    info = jnp.concatenate(
        [
            jnp.stack([window_start, ctx_index * SEQ - window_start]).astype(jnp.int32),
            jnp.stack([edges[:, 0], edges[:, -1]], axis=1).reshape(-1),
        ]
    )
    within_device = starts_within(sizes)
    block = jnp.arange(CTX_COUNT, dtype=jnp.int32)
    first_from = (
        (z_at - block % 4 + 4) % 4 * 4 + ((block // 4 % 2) ^ yl_at) * 2 + ((block // 8) ^ c_at)
    )
    shard = window_start // SEQ + jnp.arange(REACH + 1, dtype=jnp.int32)
    text_at = (
        ((shard % 2) ^ c_at) * 6
        + jnp.clip(z_at - shard // 4, 0, 2) * 2
        + ((shard // 2 % 2) ^ yl_at)
    )
    image_src = (
        jnp.arange(CTX_COUNT * DP_COUNT, dtype=jnp.int32).reshape(CTX_COUNT, DP_COUNT, 1) * CAPACITY
        + within_device
    )
    targets = (offsets - window_start).reshape(-1)
    inside = (targets >= 0) & (targets < WINDOW)
    tables = (
        info,
        image_src.reshape(-1),
        jnp.where(inside, targets, 0),
        jnp.where(inside, sizes.reshape(-1), 0),
        jnp.concatenate([first_from, text_at]).astype(jnp.int32),
    )
    return attention(
        tables, text_query, bring_in.astype(jnp.bfloat16), low_rows[None, :], first, last, text
    )


def solution(mesh):
    fine = Mesh(mesh.devices.reshape(2, 4, 4, 2, 2), DP + CTX)
    every = DP + CTX
    return jax.shard_map(
        body,
        mesh=fine,
        in_specs=(
            P(every, None),
            P(),
            P(),
            P(every, None),
            P(every, None),
            P(),
            P(),
            P(None, DP),
            P(),
            P(None, DP),
            P(None, None, DP),
            P(CTX, DP),
            P(None, CTX, DP),
            P(CTX),
            P(every, None),
            P(every, None),
        ),
        out_specs=P(CTX, DP),
        check_vma=False,
    )
```

```python
import math

import jax
import jax.numpy as jnp
import numpy as np
from jax import lax
from jax.experimental import pallas as pl
from jax.experimental.pallas import tpu as pltpu
from jax.sharding import Mesh
from jax.sharding import PartitionSpec as P

HEAD_DIM = 128
MOST = 16
SEQ = 640
REACH = 8
WINDOW = SEQ * (REACH + 1)
KEY_BLOCK = 640
PADDED = -(-WINDOW // KEY_BLOCK) * KEY_BLOCK
QUERY_BLOCK = 640
GROUP = 4
IMAGES = 512
PLACE_UNROLL = 4
CAPACITY = 32
CHUNK = 16
UNITS = 24
CTX_COUNT = 16
DP_COUNT = 8

MASKED_SCORE = -1e30
LOWEST_PEAK = -1e29
EPSILON = 1e-06
DP = ("yh", "x")
CTX = ("z", "yl", "c")


def layer_norm(rows_in, norm_gain, norm_bias):
    values = rows_in.astype(jnp.float32)
    center = values - jnp.mean(values, axis=-1, keepdims=True)
    spread = jnp.mean(center * center, axis=-1, keepdims=True)
    return (center * lax.rsqrt(spread + EPSILON) * norm_gain + norm_bias).astype(jnp.bfloat16)


def quick_gelu(values):
    return values * jax.nn.sigmoid(1.702 * values)


def starts_within(sizes):
    count = sizes.shape[-1]
    earlier = jnp.arange(count)[None, :] < jnp.arange(count)[:, None]
    return jnp.sum(jnp.where(earlier, sizes[..., None, :], 0), axis=-1, dtype=jnp.int32)


def row_positions(size_table, offset_table, row_count):
    image_starts = starts_within(size_table)
    image_ends = image_starts + size_table
    within = jnp.arange(row_count, dtype=jnp.int32)[None, :, None]
    inside = (within >= image_starts[:, None, :]) & (within < image_ends[:, None, :])
    placed = offset_table[:, None, :] - image_starts[:, None, :] + within
    return jnp.sum(jnp.where(inside, placed, 0), axis=2, dtype=jnp.int32)


def gather_by_exchange(block, axes, count):
    return lax.all_to_all(
        jnp.broadcast_to(block[None], (count,) + block.shape), axes, split_axis=0, concat_axis=0
    )


def swap(rows, axis):
    return lax.ppermute(rows, axis, [(0, 1), (1, 0)])


def turn(rows, axis, by):
    return lax.ppermute(rows, axis, [(i, (i + by) % 4) for i in range(4)])


def gather_by_ring(block):
    pair = jnp.stack([block, swap(block, "yh")])
    left, right = turn(pair, "x", 1), turn(pair, "x", -1)
    across = jnp.stack([turn(left[0], "x", 1), turn(right[1], "x", -1)])
    return jnp.concatenate([pair, left, right, across], axis=0)


def attention_kernel(
    info,
    image_src,
    image_dst,
    image_len,
    blocks_at,
    text_query_ref,
    bring_ref,
    low_ref,
    first_ref,
    last_ref,
    text_near_ref,
    text_far_ref,
    out_ref,
    text_held,
    key_wide,
    value_wide,
    image_key,
    image_value,
    image_query,
    key_held,
    value_held,
    sems,
):
    query_offset = info[1]
    near = text_near_ref.shape[0]
    copies = []
    for shard in range(REACH + 1):
        at = blocks_at[shard]
        target = text_held.at[pl.ds(shard * SEQ, SEQ), :]

        @pl.when(at < near)
        def _(at=at, target=target, shard=shard):
            pltpu.make_async_copy(text_near_ref.at[at], target, sems.at[shard]).start()

        @pl.when(at >= near)
        def _(at=at, target=target, shard=shard):
            pltpu.make_async_copy(text_far_ref.at[at - near], target, sems.at[shard]).start()

        copies.append(pltpu.make_async_copy(text_near_ref.at[0], target, sems.at[shard]))

    def widen_first(source, unused):
        for device in range(DP_COUNT):
            base = source * (DP_COUNT * CAPACITY) + device * CAPACITY
            rows = pl.ds(pl.multiple_of(base, CHUNK), CHUNK)
            held = first_ref[source, device * CHUNK : (device + 1) * CHUNK, :].astype(jnp.float32)
            image_key[rows, :] = held[:, :HEAD_DIM]
            image_value[rows, :] = held[:, HEAD_DIM:]
        return unused

    lax.fori_loop(0, CTX_COUNT, widen_first, 0)

    def widen_last(source, unused):
        for device in range(DP_COUNT):
            base = source * (DP_COUNT * CAPACITY) + device * CAPACITY + CHUNK
            rows = pl.ds(pl.multiple_of(base, CHUNK), CHUNK)
            at, side = device % 4 * CHUNK, device // 4 * 2 * HEAD_DIM
            held = last_ref[source, at : at + CHUNK, side : side + 2 * HEAD_DIM].astype(jnp.float32)
            image_key[rows, :] = held[:, :HEAD_DIM]
            image_value[rows, :] = held[:, HEAD_DIM:]
        rows = pl.ds(pl.multiple_of(source * CAPACITY, CAPACITY), CAPACITY)
        image_query[rows, :] = last_ref[source, 4 * CHUNK :, :]
        return unused

    lax.fori_loop(0, CTX_COUNT, widen_last, 0)
    for shard in range(REACH + 1):
        copies[shard].wait()

    def widen_text(step, unused):
        rows = pl.ds(pl.multiple_of(step * 320, 320), 320)
        key_wide[rows, :] = text_held[rows, :HEAD_DIM].astype(jnp.float32)
        value_wide[rows, :] = text_held[rows, HEAD_DIM:].astype(jnp.float32)
        return unused

    lax.fori_loop(0, WINDOW // 320, widen_text, 0)
    row_in = lax.broadcasted_iota(jnp.int32, (MOST, HEAD_DIM), 0)

    def place(step, unused):
        for lane in range(PLACE_UNROLL):
            image = step * PLACE_UNROLL + lane
            target = image_dst[image]
            origin = image_src[image]
            taken = row_in < image_len[image]
            rows = pl.ds(target, MOST)
            pltpu.store(key_wide.at[rows, :], image_key[pl.ds(origin, MOST), :], mask=taken)
            pltpu.store(value_wide.at[rows, :], image_value[pl.ds(origin, MOST), :], mask=taken)
        return unused

    lax.fori_loop(0, IMAGES // PLACE_UNROLL, place, 0)

    def narrow(step, unused):
        rows = pl.ds(pl.multiple_of(step * HEAD_DIM, HEAD_DIM), HEAD_DIM)
        key_held[rows, :] = key_wide[rows, :].astype(jnp.bfloat16)
        value_held[:HEAD_DIM, rows] = value_wide[rows, :].T.astype(jnp.bfloat16)
        return unused

    lax.fori_loop(0, WINDOW // HEAD_DIM, narrow, 0)
    value_held[HEAD_DIM:, :] = jnp.ones((CHUNK, PADDED), jnp.bfloat16)
    if PADDED > WINDOW:
        key_held[WINDOW:, :] = jnp.zeros((PADDED - WINDOW, HEAD_DIM), jnp.bfloat16)
        value_held[:HEAD_DIM, WINDOW:] = jnp.zeros((HEAD_DIM, PADDED - WINDOW), jnp.bfloat16)

    across = GROUP * QUERY_BLOCK
    to_power = math.log2(math.e) / math.sqrt(HEAD_DIM)
    column_at = lax.broadcasted_iota(jnp.int32, (1, QUERY_BLOCK), 1)

    def query_step(block, unused):
        rows = pl.ds(pl.multiple_of(block * QUERY_BLOCK, QUERY_BLOCK), QUERY_BLOCK)
        first = query_offset + block * QUERY_BLOCK
        bring = bring_ref[rows, :]
        is_image = jnp.max(bring.astype(jnp.float32), axis=-1, keepdims=True) > 0.5
        placed = jnp.where(
            is_image,
            jnp.dot(bring, image_query[...], preferred_element_type=jnp.float32),
            text_query_ref[rows, :].astype(jnp.float32),
        )
        queries = jnp.concatenate(
            [placed[:, h * HEAD_DIM : (h + 1) * HEAD_DIM].T for h in range(GROUP)], axis=1
        ).astype(jnp.bfloat16)
        lows = jnp.concatenate([low_ref[:, rows]] * GROUP, axis=1)
        highs = jnp.concatenate([column_at + first] * GROUP, axis=1)
        low_first = info[2 + 2 * block]
        low_last = info[3 + 2 * block]
        begin = low_first // KEY_BLOCK
        end = (first + QUERY_BLOCK - 1) // KEY_BLOCK + 1
        clear_begin = jnp.minimum((low_last + KEY_BLOCK - 1) // KEY_BLOCK, end)
        clear_end = jnp.maximum((first + 1) // KEY_BLOCK, clear_begin)

        def key_step(at, running, masked):
            peak, gathered = running
            keys_at = pl.ds(pl.multiple_of(at * KEY_BLOCK, KEY_BLOCK), KEY_BLOCK)
            scores = jnp.dot(key_held[keys_at, :], queries, preferred_element_type=jnp.float32)
            if masked:
                place_at = at * KEY_BLOCK + lax.broadcasted_iota(jnp.int32, (KEY_BLOCK, 1), 0)
                scores = jnp.where((place_at >= lows) & (place_at <= highs), scores, MASKED_SCORE)
            new_peak = jnp.maximum(peak, jnp.max(scores, axis=0, keepdims=True))
            weights = jnp.exp2((scores - new_peak) * to_power).astype(jnp.bfloat16)
            rescale = jnp.exp2((peak - new_peak) * to_power)
            gathered = gathered * rescale + jnp.dot(
                value_held[:, keys_at], weights, preferred_element_type=jnp.float32
            )
            return new_peak, gathered

        running = (
            jnp.full((1, across), LOWEST_PEAK, jnp.float32),
            jnp.zeros((HEAD_DIM + CHUNK, across), jnp.float32),
        )
        running = lax.fori_loop(begin, clear_begin, lambda a, r: key_step(a, r, True), running)
        running = lax.fori_loop(clear_begin, clear_end, lambda a, r: key_step(a, r, False), running)
        peak, gathered = lax.fori_loop(clear_end, end, lambda a, r: key_step(a, r, True), running)
        context = gathered[:HEAD_DIM] / gathered[HEAD_DIM : HEAD_DIM + 1]
        for h in range(GROUP):
            out_ref[rows, h * HEAD_DIM : (h + 1) * HEAD_DIM] = context[
                :, h * QUERY_BLOCK : (h + 1) * QUERY_BLOCK
            ].T.astype(jnp.bfloat16)
        return unused

    lax.fori_loop(0, SEQ // QUERY_BLOCK, query_step, 0)


def attention(tables, text_query, bring_in, low_rows, first, last, text):
    smem = pl.BlockSpec(memory_space=pltpu.SMEM)
    vmem = pl.BlockSpec(memory_space=pltpu.VMEM)
    image_rows = CTX_COUNT * DP_COUNT * CAPACITY
    return pl.pallas_call(
        attention_kernel,
        out_shape=jax.ShapeDtypeStruct(text_query.shape, jnp.bfloat16),
        in_specs=[smem] * 5 + [vmem] * 5 + [pl.BlockSpec(memory_space=pl.ANY)] * 2,
        out_specs=vmem,
        scratch_shapes=[
            pltpu.VMEM((WINDOW, 2 * HEAD_DIM), jnp.bfloat16),
            pltpu.VMEM((WINDOW + MOST, HEAD_DIM), jnp.float32),
            pltpu.VMEM((WINDOW + MOST, HEAD_DIM), jnp.float32),
            pltpu.VMEM((image_rows + MOST, HEAD_DIM), jnp.float32),
            pltpu.VMEM((image_rows + MOST, HEAD_DIM), jnp.float32),
            pltpu.VMEM((CTX_COUNT * CAPACITY, GROUP * HEAD_DIM), jnp.bfloat16),
            pltpu.VMEM((PADDED, HEAD_DIM), jnp.bfloat16),
            pltpu.VMEM((HEAD_DIM + CHUNK, PADDED), jnp.bfloat16),
            pltpu.SemaphoreType.DMA((REACH + 1,)),
        ],
        compiler_params=pltpu.CompilerParams(vmem_limit_bytes=48 * 1024 * 1024),
        cost_estimate=pl.CostEstimate(
            flops=8_000_000_000, bytes_accessed=8_000_000, transcendentals=13_000_000
        ),
    )(*tables, text_query, bring_in, low_rows, first, last, *text)


def project_kernel(order_ref, rows_ref, gain_ref, query_weight_ref, kv_weight_ref, query_ref, kv_ref, query_sum, kv_sum, squares):
    step = pl.program_id(0)

    @pl.when(step == 0)
    def _():
        query_sum[...] = jnp.zeros_like(query_sum)
        kv_sum[...] = jnp.zeros_like(kv_sum)
        squares[...] = jnp.zeros_like(squares)

    values = rows_ref[0].astype(jnp.float32)
    squares[...] += jnp.sum(values * values, axis=-1, keepdims=True)
    gained = (values * gain_ref[0]).astype(jnp.bfloat16)
    query_sum[...] += jnp.dot(gained, query_weight_ref[...], preferred_element_type=jnp.float32)
    kv_sum[:, :HEAD_DIM] += jnp.dot(gained, kv_weight_ref[0], preferred_element_type=jnp.float32)
    kv_sum[:, HEAD_DIM:] += jnp.dot(gained, kv_weight_ref[1], preferred_element_type=jnp.float32)

    @pl.when(step == DP_COUNT - 1)
    def _():
        scale = lax.rsqrt(squares[...] / (DP_COUNT * rows_ref.shape[2]) + EPSILON)
        query_ref[...] = (query_sum[...] * scale).astype(jnp.bfloat16)
        kv_ref[...] = (kv_sum[...] * scale).astype(jnp.bfloat16)


def project(order, whole, gain, query_weight, kv_weight):
    count, rows, part = whole.shape
    query_width, kv_width = query_weight.shape[1], kv_weight.shape[2]
    return pl.pallas_call(
        project_kernel,
        grid_spec=pltpu.PrefetchScalarGridSpec(
            num_scalar_prefetch=1,
            grid=(count,),
            in_specs=[
                pl.BlockSpec((1, rows, part), lambda k, order: (k, 0, 0)),
                pl.BlockSpec((1, 1, part), lambda k, order: (order[k], 0, 0)),
                pl.BlockSpec((part, query_width), lambda k, order: (order[k], 0)),
                pl.BlockSpec((2, part, kv_width), lambda k, order: (0, order[k], 0)),
            ],
            out_specs=(
                pl.BlockSpec((rows, query_width), lambda k, order: (0, 0)),
                pl.BlockSpec((rows, 2 * kv_width), lambda k, order: (0, 0)),
            ),
            scratch_shapes=[
                pltpu.VMEM((rows, query_width), jnp.float32),
                pltpu.VMEM((rows, 2 * kv_width), jnp.float32),
                pltpu.VMEM((rows, 1), jnp.float32),
            ],
        ),
        out_shape=(
            jax.ShapeDtypeStruct((rows, query_width), jnp.bfloat16),
            jax.ShapeDtypeStruct((rows, 2 * kv_width), jnp.bfloat16),
        ),
        compiler_params=pltpu.CompilerParams(vmem_limit_bytes=52 * 1024 * 1024),
        cost_estimate=pl.CostEstimate(
            flops=2 * rows * count * part * (query_width + 2 * kv_width),
            bytes_accessed=2 * count * part * (query_width + 2 * kv_width + rows),
            transcendentals=0,
        ),
    )(order, whole, gain, query_weight, kv_weight)


def body(
    patches,
    vision_gain,
    vision_bias,
    up_weight,
    down_weight,
    merge_gain,
    merge_bias,
    merge_weight,
    attn_gain,
    query_weight,
    kv_weight,
    text_query,
    text_kv,
    doc_ids,
    image_sizes,
    image_offsets,
):
    z_at, yl_at, c_at = lax.axis_index("z"), lax.axis_index("yl"), lax.axis_index("c")
    ctx_index = lax.axis_index(CTX)
    width = patches.shape[1]
    own_rows = patches.shape[0]
    units_own = up_weight.shape[0]

    below = jnp.sum(
        (doc_ids[:, None] < jnp.arange(4, dtype=jnp.int32)[None, :]).astype(jnp.int32),
        axis=0,
        dtype=jnp.int32,
    )
    facts = jnp.concatenate([image_sizes, image_offsets, below[None, :]], axis=1)
    facts = jnp.concatenate([facts // 128, facts % 128], axis=1).astype(jnp.bfloat16)
    fact_count = facts.shape[1]
    block = jnp.concatenate(
        [
            jnp.pad(up_weight, ((0, UNITS - units_own), (0, 0))),
            down_weight,
            jnp.pad(facts, ((0, UNITS - units_own - 1), (0, width - fact_count))),
        ],
        axis=0,
    )
    block = jnp.broadcast_to(block[None], (16,) + block.shape)
    block, patches = lax.optimization_barrier((block, patches))
    units = lax.all_to_all(block, DP + ("yl",), split_axis=0, concat_axis=0)
    text = jnp.concatenate([text_kv[0], text_kv[1]], axis=1)
    text, units = lax.optimization_barrier((text, units))
    text = jnp.concatenate([text, swap(text, "yl")], axis=0)
    normed = layer_norm(patches, vision_gain, vision_bias)
    column = jnp.concatenate(
        [normed]
        + [
            lax.ppermute(normed, "z", [(i, (i + step) % 4) for i in range(4)])
            for step in (1, 2, 3)
        ],
        axis=0,
    )
    near_rows = column.shape[0]
    near = jnp.concatenate([column, swap(column, "c")], axis=0)
    ups = units[:, :UNITS].reshape(-1, width)
    downs = units[:, UNITS:].reshape(-1, width)
    facts = units[:, UNITS + units_own, :fact_count].reshape(1, -1)
    hidden = quick_gelu(
        lax.dot_general(near, ups, (((1,), (1,)), ((), ())), preferred_element_type=jnp.float32)
    ).astype(jnp.bfloat16)
    away = jnp.dot(hidden[near_rows:], downs, preferred_element_type=jnp.float32).astype(
        jnp.bfloat16
    )
    here = jnp.dot(hidden[:near_rows], downs, preferred_element_type=jnp.float32)
    came = swap(
        jnp.concatenate(
            [away, jnp.pad(facts, ((0, CHUNK - 1), (0, width - facts.shape[1])))], axis=0
        ),
        "c",
    )
    pair_sum = (here + came[:near_rows].astype(jnp.float32)).astype(jnp.bfloat16)
    other = came[near_rows : near_rows + 1, : facts.shape[1]]
    facts = jnp.concatenate(
        [jnp.where(c_at == 0, facts, other), jnp.where(c_at == 0, other, facts)], axis=1
    )
    tail = jnp.pad(facts, ((0, CHUNK - 1), (0, width - facts.shape[1])))
    by_z = pair_sum.reshape(4, own_rows, width)
    terms = lax.all_to_all(
        jnp.stack(
            [
                jnp.concatenate(
                    [lax.dynamic_index_in_dim(by_z, (z_at - j + 4) % 4, 0, False), tail], axis=0
                )
                for j in range(4)
            ]
        ),
        "z",
        split_axis=0,
        concat_axis=0,
    )
    branch = jnp.sum(terms[:, :own_rows].astype(jnp.float32), axis=0)
    facts = terms[:, own_rows, : facts.shape[1]].astype(jnp.int32)
    facts = facts.reshape(4, 2, 8, 2, fact_count).transpose(2, 0, 3, 1, 4)
    facts = facts.reshape(8, 16, 2, fact_count // 2)
    facts = facts[:, :, 0] * 128 + facts[:, :, 1]
    vision = (patches.astype(jnp.float32) + branch).astype(jnp.bfloat16)
    merged_in = layer_norm(vision, merge_gain, merge_bias).reshape(-1, 4 * width)

    text, merged_in = lax.optimization_barrier((text, merged_in))
    text = jnp.concatenate(
        [
            text,
            lax.ppermute(text, "z", [(0, 1), (1, 2), (2, 3)]),
            lax.ppermute(text, "z", [(0, 2), (1, 3)]),
        ],
        axis=0,
    )
    yh_at, x_at = lax.axis_index("yh"), lax.axis_index("x")
    step = jnp.array([0, 0, 3, 3, 1, 1, 2, 2], jnp.int32)
    order = (yh_at ^ (jnp.arange(8, dtype=jnp.int32) % 2)) * 4 + (x_at + step) % 4
    member = jnp.arange(8, dtype=jnp.int32)
    slot_of = jnp.sum(
        jnp.where(member[:, None] == order[None, :], member[None, :], 0), axis=1, dtype=jnp.int32
    )
    columns = [
        gather_by_ring(merged_in[at : at + CHUNK]).reshape(-1, 4 * width) for at in (0, CHUNK)
    ]
    spread_rows = []
    for column_in in columns:
        merged = jnp.dot(column_in, merge_weight, preferred_element_type=jnp.float32).astype(
            jnp.bfloat16
        )
        by_member = merged.reshape(DP_COUNT, CHUNK, -1)
        spread_rows.append(
            jnp.concatenate(
                [lax.dynamic_index_in_dim(by_member, slot_of[d], 0, False) for d in range(8)],
                axis=0,
            )
        )
    text, spread_rows[1] = lax.optimization_barrier((text, spread_rows[1]))
    wholes = [gather_by_ring(rows) for rows in spread_rows]
    gains = attn_gain.reshape(DP_COUNT, 1, -1)
    image_queries, image_kvs = [None, None], [None, None]
    image_queries[0], image_kvs[0] = project(order, wholes[0], gains, query_weight, kv_weight)
    first = gather_by_exchange(image_kvs[0], CTX, CTX_COUNT)
    text_far = swap(text, "c")
    first, text_far, wholes[1] = lax.optimization_barrier((first, text_far, wholes[1]))
    text = [half.reshape(6, SEQ, -1) for half in (text, text_far)]
    image_queries[1], image_kvs[1] = project(order, wholes[1], gains, query_weight, kv_weight)

    sizes = jnp.swapaxes(facts[:, :, :4], 0, 1)
    offsets = jnp.swapaxes(facts[:, :, 4:8], 0, 1)
    starts = jnp.sum(facts[0, :, 8:], axis=0, dtype=jnp.int32)
    positions = row_positions(sizes.reshape(128, 4), offsets.reshape(128, 4), CAPACITY).reshape(
        16, 256
    )
    before = jnp.arange(256)[None, :] < jnp.arange(256)[:, None]
    own_owner = lax.dynamic_index_in_dim(positions, ctx_index, 0, False) // SEQ
    own_rank = jnp.sum(
        ((own_owner[None, :] == own_owner[:, None]) & before).astype(jnp.int32),
        axis=1,
        dtype=jnp.int32,
    )
    own_slot = (own_owner * CAPACITY + own_rank).reshape(8, 2, CHUNK).swapaxes(0, 1).reshape(-1)
    spread_out = (jnp.arange(512, dtype=jnp.int32)[:, None] == own_slot[None, :]).astype(
        jnp.bfloat16
    )
    mine = positions // SEQ == ctx_index
    rank = jnp.sum((mine[:, None, :] & before[None]).astype(jnp.int32), axis=2, dtype=jnp.int32)
    slot_here = mine[:, :, None] & (
        rank[:, :, None] == jnp.arange(CAPACITY, dtype=jnp.int32)[None, None, :]
    )
    slot_place = jnp.sum(
        jnp.where(slot_here, positions[:, :, None] - ctx_index * SEQ + 1, 0),
        axis=1,
        dtype=jnp.int32,
    ).reshape(-1) - 1
    bring_in = jnp.arange(SEQ, dtype=jnp.int32)[:, None] == slot_place[None, :]

    chunk_rows = DP_COUNT * CHUNK
    sent = sum(
        jnp.dot(
            spread_out[:, k * chunk_rows : (k + 1) * chunk_rows],
            image_queries[k],
            preferred_element_type=jnp.float32,
        )
        for k in (0, 1)
    ).astype(jnp.bfloat16)
    half = chunk_rows // 2
    folded = jnp.concatenate([image_kvs[1][:half], image_kvs[1][half:]], axis=1)
    last = lax.all_to_all(
        jnp.concatenate(
            [
                jnp.broadcast_to(folded[None], (CTX_COUNT,) + folded.shape),
                sent.reshape(CTX_COUNT, CAPACITY, -1),
            ],
            axis=1,
        ),
        CTX,
        split_axis=0,
        concat_axis=0,
    )

    window_start = jnp.maximum(ctx_index - REACH, 0) * SEQ
    low_rows = (
        jnp.sum(
            jnp.where(
                doc_ids[:, None] == jnp.arange(4, dtype=jnp.int32)[None, :], starts[None, :], 0
            ),
            axis=1,
            dtype=jnp.int32,
        )
        - window_start
    )
    low_rows = jnp.maximum(low_rows, 0)
    edges = low_rows.reshape(-1, QUERY_BLOCK)
    info = jnp.concatenate(
        [
            jnp.stack([window_start, ctx_index * SEQ - window_start]).astype(jnp.int32),
            jnp.stack([edges[:, 0], edges[:, -1]], axis=1).reshape(-1),
        ]
    )
    within_device = starts_within(sizes)
    shard = window_start // SEQ + jnp.arange(REACH + 1, dtype=jnp.int32)
    text_at = (
        ((shard % 2) ^ c_at) * 6
        + jnp.clip(z_at - shard // 4, 0, 2) * 2
        + ((shard // 2 % 2) ^ yl_at)
    )
    image_src = (
        jnp.arange(CTX_COUNT * DP_COUNT, dtype=jnp.int32).reshape(CTX_COUNT, DP_COUNT, 1) * CAPACITY
        + within_device
    )
    targets = (offsets - window_start).reshape(-1)
    inside = (targets >= 0) & (targets < WINDOW)
    tables = (
        info,
        image_src.reshape(-1),
        jnp.where(inside, targets, 0),
        jnp.where(inside, sizes.reshape(-1), 0),
        text_at.astype(jnp.int32),
    )
    return attention(
        tables, text_query, bring_in.astype(jnp.bfloat16), low_rows[None, :], first, last, text
    )


def solution(mesh):
    fine = Mesh(mesh.devices.reshape(2, 4, 4, 2, 2), DP + CTX)
    every = DP + CTX
    return jax.shard_map(
        body,
        mesh=fine,
        in_specs=(
            P(every, None),
            P(),
            P(),
            P(every, None),
            P(every, None),
            P(),
            P(),
            P(None, DP),
            P(),
            P(None, DP),
            P(None, None, DP),
            P(CTX, DP),
            P(None, CTX, DP),
            P(CTX),
            P(every, None),
            P(every, None),
        ),
        out_specs=P(CTX, DP),
        check_vma=False,
    )
```

```python
import math

import jax
import jax.numpy as jnp
import numpy as np
from jax import lax
from jax.experimental import pallas as pl
from jax.experimental.pallas import tpu as pltpu
from jax.sharding import Mesh
from jax.sharding import PartitionSpec as P

HEAD_DIM = 128
MOST = 16
SEQ = 640
REACH = 8
WINDOW = SEQ * (REACH + 1)
KEY_BLOCK = 640
PADDED = -(-WINDOW // KEY_BLOCK) * KEY_BLOCK
QUERY_BLOCK = 640
GROUP = 4
IMAGES = 512
PLACE_UNROLL = 4
CAPACITY = 32
CHUNK = 16
UNITS = 24
CTX_COUNT = 16
DP_COUNT = 8

MASKED_SCORE = -1e30
LOWEST_PEAK = -1e29
EPSILON = 1e-06
DP = ("yh", "x")
CTX = ("z", "yl", "c")


def layer_norm(rows_in, norm_gain, norm_bias):
    values = rows_in.astype(jnp.float32)
    center = values - jnp.mean(values, axis=-1, keepdims=True)
    spread = jnp.mean(center * center, axis=-1, keepdims=True)
    return (center * lax.rsqrt(spread + EPSILON) * norm_gain + norm_bias).astype(jnp.bfloat16)


def quick_gelu(values):
    return values * jax.nn.sigmoid(1.702 * values)


def starts_within(sizes):
    count = sizes.shape[-1]
    earlier = jnp.arange(count)[None, :] < jnp.arange(count)[:, None]
    return jnp.sum(jnp.where(earlier, sizes[..., None, :], 0), axis=-1, dtype=jnp.int32)


def row_positions(size_table, offset_table, row_count):
    image_starts = starts_within(size_table)
    image_ends = image_starts + size_table
    within = jnp.arange(row_count, dtype=jnp.int32)[None, :, None]
    inside = (within >= image_starts[:, None, :]) & (within < image_ends[:, None, :])
    placed = offset_table[:, None, :] - image_starts[:, None, :] + within
    return jnp.sum(jnp.where(inside, placed, 0), axis=2, dtype=jnp.int32)


def gather_by_exchange(block, axes, count):
    return lax.all_to_all(
        jnp.broadcast_to(block[None], (count,) + block.shape), axes, split_axis=0, concat_axis=0
    )


def swap(rows, axis):
    return lax.ppermute(rows, axis, [(0, 1), (1, 0)])


def turn(rows, axis, by):
    return lax.ppermute(rows, axis, [(i, (i + by) % 4) for i in range(4)])


def gather_by_ring(block):
    pair = jnp.stack([block, swap(block, "yh")])
    left, right = turn(pair, "x", 1), turn(pair, "x", -1)
    across = jnp.stack([turn(left[0], "x", 1), turn(right[1], "x", -1)])
    return jnp.concatenate([pair, left, right, across], axis=0)


def attention_kernel(
    info,
    image_src,
    image_dst,
    image_len,
    blocks_at,
    text_query_ref,
    bring_ref,
    low_ref,
    last_ref,
    text_near_ref,
    text_far_ref,
    out_ref,
    text_held,
    key_wide,
    value_wide,
    image_key,
    image_value,
    image_query,
    key_held,
    value_held,
    sems,
):
    query_offset = info[1]
    near = text_near_ref.shape[0]
    copies = []
    for shard in range(REACH + 1):
        at = blocks_at[shard]
        target = text_held.at[pl.ds(shard * SEQ, SEQ), :]

        @pl.when(at < near)
        def _(at=at, target=target, shard=shard):
            pltpu.make_async_copy(text_near_ref.at[at], target, sems.at[shard]).start()

        @pl.when(at >= near)
        def _(at=at, target=target, shard=shard):
            pltpu.make_async_copy(text_far_ref.at[at - near], target, sems.at[shard]).start()

        copies.append(pltpu.make_async_copy(text_near_ref.at[0], target, sems.at[shard]))

    def widen_image(source, unused):
        for device in range(DP_COUNT):
            base = source * (DP_COUNT * CAPACITY) + device * CAPACITY
            held = last_ref[source, device * CHUNK : (device + 1) * CHUNK, :].astype(jnp.float32)
            for part in range(2):
                rows = pl.ds(pl.multiple_of(base + part * CHUNK, CHUNK), CHUNK)
                side = part * 2 * HEAD_DIM
                image_key[rows, :] = held[:, side : side + HEAD_DIM]
                image_value[rows, :] = held[:, side + HEAD_DIM : side + 2 * HEAD_DIM]
        rows = pl.ds(pl.multiple_of(source * CAPACITY, CAPACITY), CAPACITY)
        image_query[rows, :] = last_ref[source, DP_COUNT * CHUNK :, :]
        return unused

    lax.fori_loop(0, CTX_COUNT, widen_image, 0)
    for shard in range(REACH + 1):
        copies[shard].wait()

    def widen_text(step, unused):
        rows = pl.ds(pl.multiple_of(step * 320, 320), 320)
        key_wide[rows, :] = text_held[rows, :HEAD_DIM].astype(jnp.float32)
        value_wide[rows, :] = text_held[rows, HEAD_DIM:].astype(jnp.float32)
        return unused

    lax.fori_loop(0, WINDOW // 320, widen_text, 0)
    row_in = lax.broadcasted_iota(jnp.int32, (MOST, HEAD_DIM), 0)

    def place(step, unused):
        for lane in range(PLACE_UNROLL):
            image = step * PLACE_UNROLL + lane
            target = image_dst[image]
            origin = image_src[image]
            taken = row_in < image_len[image]
            rows = pl.ds(target, MOST)
            pltpu.store(key_wide.at[rows, :], image_key[pl.ds(origin, MOST), :], mask=taken)
            pltpu.store(value_wide.at[rows, :], image_value[pl.ds(origin, MOST), :], mask=taken)
        return unused

    lax.fori_loop(0, IMAGES // PLACE_UNROLL, place, 0)

    def narrow(step, unused):
        rows = pl.ds(pl.multiple_of(step * HEAD_DIM, HEAD_DIM), HEAD_DIM)
        key_held[rows, :] = key_wide[rows, :].astype(jnp.bfloat16)
        value_held[:HEAD_DIM, rows] = value_wide[rows, :].T.astype(jnp.bfloat16)
        return unused

    lax.fori_loop(0, WINDOW // HEAD_DIM, narrow, 0)
    value_held[HEAD_DIM:, :] = jnp.ones((CHUNK, PADDED), jnp.bfloat16)
    if PADDED > WINDOW:
        key_held[WINDOW:, :] = jnp.zeros((PADDED - WINDOW, HEAD_DIM), jnp.bfloat16)
        value_held[:HEAD_DIM, WINDOW:] = jnp.zeros((HEAD_DIM, PADDED - WINDOW), jnp.bfloat16)

    across = GROUP * QUERY_BLOCK
    to_power = math.log2(math.e) / math.sqrt(HEAD_DIM)
    column_at = lax.broadcasted_iota(jnp.int32, (1, QUERY_BLOCK), 1)

    def query_step(block, unused):
        rows = pl.ds(pl.multiple_of(block * QUERY_BLOCK, QUERY_BLOCK), QUERY_BLOCK)
        first = query_offset + block * QUERY_BLOCK
        bring = bring_ref[rows, :]
        is_image = jnp.max(bring.astype(jnp.float32), axis=-1, keepdims=True) > 0.5
        placed = jnp.where(
            is_image,
            jnp.dot(bring, image_query[...], preferred_element_type=jnp.float32),
            text_query_ref[rows, :].astype(jnp.float32),
        )
        queries = jnp.concatenate(
            [placed[:, h * HEAD_DIM : (h + 1) * HEAD_DIM].T for h in range(GROUP)], axis=1
        ).astype(jnp.bfloat16)
        lows = jnp.concatenate([low_ref[:, rows]] * GROUP, axis=1)
        highs = jnp.concatenate([column_at + first] * GROUP, axis=1)
        low_first = info[2 + 2 * block]
        low_last = info[3 + 2 * block]
        begin = low_first // KEY_BLOCK
        end = (first + QUERY_BLOCK - 1) // KEY_BLOCK + 1
        clear_begin = jnp.minimum((low_last + KEY_BLOCK - 1) // KEY_BLOCK, end)
        clear_end = jnp.maximum((first + 1) // KEY_BLOCK, clear_begin)

        def key_step(at, running, masked):
            peak, gathered = running
            keys_at = pl.ds(pl.multiple_of(at * KEY_BLOCK, KEY_BLOCK), KEY_BLOCK)
            scores = jnp.dot(key_held[keys_at, :], queries, preferred_element_type=jnp.float32)
            if masked:
                place_at = at * KEY_BLOCK + lax.broadcasted_iota(jnp.int32, (KEY_BLOCK, 1), 0)
                scores = jnp.where((place_at >= lows) & (place_at <= highs), scores, MASKED_SCORE)
            new_peak = jnp.maximum(peak, jnp.max(scores, axis=0, keepdims=True))
            weights = jnp.exp2((scores - new_peak) * to_power).astype(jnp.bfloat16)
            rescale = jnp.exp2((peak - new_peak) * to_power)
            gathered = gathered * rescale + jnp.dot(
                value_held[:, keys_at], weights, preferred_element_type=jnp.float32
            )
            return new_peak, gathered

        running = (
            jnp.full((1, across), LOWEST_PEAK, jnp.float32),
            jnp.zeros((HEAD_DIM + CHUNK, across), jnp.float32),
        )
        running = lax.fori_loop(begin, clear_begin, lambda a, r: key_step(a, r, True), running)
        running = lax.fori_loop(clear_begin, clear_end, lambda a, r: key_step(a, r, False), running)
        peak, gathered = lax.fori_loop(clear_end, end, lambda a, r: key_step(a, r, True), running)
        context = gathered[:HEAD_DIM] / gathered[HEAD_DIM : HEAD_DIM + 1]
        for h in range(GROUP):
            out_ref[rows, h * HEAD_DIM : (h + 1) * HEAD_DIM] = context[
                :, h * QUERY_BLOCK : (h + 1) * QUERY_BLOCK
            ].T.astype(jnp.bfloat16)
        return unused

    lax.fori_loop(0, SEQ // QUERY_BLOCK, query_step, 0)


def attention(tables, text_query, bring_in, low_rows, last, text):
    smem = pl.BlockSpec(memory_space=pltpu.SMEM)
    vmem = pl.BlockSpec(memory_space=pltpu.VMEM)
    image_rows = CTX_COUNT * DP_COUNT * CAPACITY
    return pl.pallas_call(
        attention_kernel,
        out_shape=jax.ShapeDtypeStruct(text_query.shape, jnp.bfloat16),
        in_specs=[smem] * 5 + [vmem] * 4 + [pl.BlockSpec(memory_space=pl.ANY)] * 2,
        out_specs=vmem,
        scratch_shapes=[
            pltpu.VMEM((WINDOW, 2 * HEAD_DIM), jnp.bfloat16),
            pltpu.VMEM((WINDOW + MOST, HEAD_DIM), jnp.float32),
            pltpu.VMEM((WINDOW + MOST, HEAD_DIM), jnp.float32),
            pltpu.VMEM((image_rows + MOST, HEAD_DIM), jnp.float32),
            pltpu.VMEM((image_rows + MOST, HEAD_DIM), jnp.float32),
            pltpu.VMEM((CTX_COUNT * CAPACITY, GROUP * HEAD_DIM), jnp.bfloat16),
            pltpu.VMEM((PADDED, HEAD_DIM), jnp.bfloat16),
            pltpu.VMEM((HEAD_DIM + CHUNK, PADDED), jnp.bfloat16),
            pltpu.SemaphoreType.DMA((REACH + 1,)),
        ],
        compiler_params=pltpu.CompilerParams(vmem_limit_bytes=48 * 1024 * 1024),
        cost_estimate=pl.CostEstimate(
            flops=8_000_000_000, bytes_accessed=8_000_000, transcendentals=13_000_000
        ),
    )(*tables, text_query, bring_in, low_rows, last, *text)


def project_kernel(
    order_ref,
    first_ref,
    second_ref,
    gain_ref,
    query_weight_ref,
    kv_weight_ref,
    query_ref,
    kv_ref,
    query_sum,
    kv_sum,
    squares,
):
    step = pl.program_id(0)

    @pl.when(step == 0)
    def _():
        query_sum[...] = jnp.zeros_like(query_sum)
        kv_sum[...] = jnp.zeros_like(kv_sum)
        squares[...] = jnp.zeros_like(squares)

    values = jnp.concatenate([first_ref[0], second_ref[0]], axis=0).astype(jnp.float32)
    squares[...] += jnp.sum(values * values, axis=-1, keepdims=True)
    gained = (values * gain_ref[0]).astype(jnp.bfloat16)
    query_sum[...] += jnp.dot(gained, query_weight_ref[...], preferred_element_type=jnp.float32)
    kv_sum[:, :HEAD_DIM] += jnp.dot(gained, kv_weight_ref[0], preferred_element_type=jnp.float32)
    kv_sum[:, HEAD_DIM:] += jnp.dot(gained, kv_weight_ref[1], preferred_element_type=jnp.float32)

    @pl.when(step == DP_COUNT - 1)
    def _():
        scale = lax.rsqrt(squares[...] / (DP_COUNT * first_ref.shape[2]) + EPSILON)
        query_ref[...] = (query_sum[...] * scale).astype(jnp.bfloat16)
        kv = (kv_sum[...] * scale).astype(jnp.bfloat16)
        half = first_ref.shape[1]
        kv_ref[:, : 2 * HEAD_DIM] = kv[:half]
        kv_ref[:, 2 * HEAD_DIM :] = kv[half:]


def project(order, wholes, gain, query_weight, kv_weight):
    count, rows, part = wholes[0].shape
    query_width, kv_width = query_weight.shape[1], kv_weight.shape[2]
    rows_spec = pl.BlockSpec((1, rows, part), lambda k, order: (k, 0, 0))
    return pl.pallas_call(
        project_kernel,
        grid_spec=pltpu.PrefetchScalarGridSpec(
            num_scalar_prefetch=1,
            grid=(count,),
            in_specs=[
                rows_spec,
                rows_spec,
                pl.BlockSpec((1, 1, part), lambda k, order: (order[k], 0, 0)),
                pl.BlockSpec((part, query_width), lambda k, order: (order[k], 0)),
                pl.BlockSpec((2, part, kv_width), lambda k, order: (0, order[k], 0)),
            ],
            out_specs=(
                pl.BlockSpec((2 * rows, query_width), lambda k, order: (0, 0)),
                pl.BlockSpec((rows, 4 * kv_width), lambda k, order: (0, 0)),
            ),
            scratch_shapes=[
                pltpu.VMEM((2 * rows, query_width), jnp.float32),
                pltpu.VMEM((2 * rows, 2 * kv_width), jnp.float32),
                pltpu.VMEM((2 * rows, 1), jnp.float32),
            ],
        ),
        out_shape=(
            jax.ShapeDtypeStruct((2 * rows, query_width), jnp.bfloat16),
            jax.ShapeDtypeStruct((rows, 4 * kv_width), jnp.bfloat16),
        ),
        compiler_params=pltpu.CompilerParams(vmem_limit_bytes=20 * 1024 * 1024),
        cost_estimate=pl.CostEstimate(
            flops=4 * rows * count * part * (query_width + 2 * kv_width),
            bytes_accessed=2 * count * part * (query_width + 2 * kv_width + 2 * rows),
            transcendentals=0,
        ),
    )(order, *wholes, gain, query_weight, kv_weight)


def body(
    patches,
    vision_gain,
    vision_bias,
    up_weight,
    down_weight,
    merge_gain,
    merge_bias,
    merge_weight,
    attn_gain,
    query_weight,
    kv_weight,
    text_query,
    text_kv,
    doc_ids,
    image_sizes,
    image_offsets,
):
    z_at, yl_at, c_at = lax.axis_index("z"), lax.axis_index("yl"), lax.axis_index("c")
    ctx_index = lax.axis_index(CTX)
    width = patches.shape[1]
    own_rows = patches.shape[0]
    units_own = up_weight.shape[0]

    below = jnp.sum(
        (doc_ids[:, None] < jnp.arange(4, dtype=jnp.int32)[None, :]).astype(jnp.int32),
        axis=0,
        dtype=jnp.int32,
    )
    facts = jnp.concatenate([image_sizes, image_offsets, below[None, :]], axis=1)
    facts = jnp.concatenate([facts // 128, facts % 128], axis=1).astype(jnp.bfloat16)
    fact_count = facts.shape[1]
    block = jnp.concatenate(
        [
            jnp.pad(up_weight, ((0, UNITS - units_own), (0, 0))),
            down_weight,
            jnp.pad(facts, ((0, UNITS - units_own - 1), (0, width - fact_count))),
        ],
        axis=0,
    )
    block = jnp.broadcast_to(block[None], (16,) + block.shape)
    text = jnp.concatenate([text_kv[0], text_kv[1]], axis=1)
    block, patches, text = lax.optimization_barrier((block, patches, text))
    units = lax.all_to_all(block, DP + ("yl",), split_axis=0, concat_axis=0)
    text = jnp.concatenate([text, swap(text, "yl")], axis=0)
    text, units = lax.optimization_barrier((text, units))
    normed = layer_norm(patches, vision_gain, vision_bias)
    column = jnp.concatenate(
        [normed]
        + [
            lax.ppermute(normed, "z", [(i, (i + step) % 4) for i in range(4)])
            for step in (1, 2, 3)
        ],
        axis=0,
    )
    near_rows = column.shape[0]
    near = jnp.concatenate([column, swap(column, "c")], axis=0)
    ups = units[:, :UNITS].reshape(-1, width)
    downs = units[:, UNITS:].reshape(-1, width)
    facts = units[:, UNITS + units_own, :fact_count].reshape(1, -1)
    hidden = quick_gelu(
        lax.dot_general(near, ups, (((1,), (1,)), ((), ())), preferred_element_type=jnp.float32)
    ).astype(jnp.bfloat16)
    away = jnp.dot(hidden[near_rows:], downs, preferred_element_type=jnp.float32).astype(
        jnp.bfloat16
    )
    here = jnp.dot(hidden[:near_rows], downs, preferred_element_type=jnp.float32)
    came = swap(
        jnp.concatenate(
            [away, jnp.pad(facts, ((0, CHUNK - 1), (0, width - facts.shape[1])))], axis=0
        ),
        "c",
    )
    pair_sum = (here + came[:near_rows].astype(jnp.float32)).astype(jnp.bfloat16)
    other = came[near_rows : near_rows + 1, : facts.shape[1]]
    facts = jnp.concatenate(
        [jnp.where(c_at == 0, facts, other), jnp.where(c_at == 0, other, facts)], axis=1
    )
    tail = jnp.pad(facts, ((0, CHUNK - 1), (0, width - facts.shape[1])))
    by_z = pair_sum.reshape(4, own_rows, width)
    terms = lax.all_to_all(
        jnp.stack(
            [
                jnp.concatenate(
                    [lax.dynamic_index_in_dim(by_z, (z_at - j + 4) % 4, 0, False), tail], axis=0
                )
                for j in range(4)
            ]
        ),
        "z",
        split_axis=0,
        concat_axis=0,
    )
    branch = jnp.sum(terms[:, :own_rows].astype(jnp.float32), axis=0)
    facts = terms[:, own_rows, : facts.shape[1]].astype(jnp.int32)
    facts = facts.reshape(4, 2, 8, 2, fact_count).transpose(2, 0, 3, 1, 4)
    facts = facts.reshape(8, 16, 2, fact_count // 2)
    facts = facts[:, :, 0] * 128 + facts[:, :, 1]
    vision = (patches.astype(jnp.float32) + branch).astype(jnp.bfloat16)
    merged_in = layer_norm(vision, merge_gain, merge_bias).reshape(-1, 4 * width)

    text, merged_in = lax.optimization_barrier((text, merged_in))
    text = jnp.concatenate(
        [
            text,
            lax.ppermute(text, "z", [(0, 1), (1, 2), (2, 3)]),
            lax.ppermute(text, "z", [(0, 2), (1, 3)]),
        ],
        axis=0,
    )
    yh_at, x_at = lax.axis_index("yh"), lax.axis_index("x")
    step = jnp.array([0, 0, 3, 3, 1, 1, 2, 2], jnp.int32)
    order = (yh_at ^ (jnp.arange(8, dtype=jnp.int32) % 2)) * 4 + (x_at + step) % 4
    member = jnp.arange(8, dtype=jnp.int32)
    slot_of = jnp.sum(
        jnp.where(member[:, None] == order[None, :], member[None, :], 0), axis=1, dtype=jnp.int32
    )
    columns = [
        gather_by_ring(merged_in[at : at + CHUNK]).reshape(-1, 4 * width) for at in (0, CHUNK)
    ]
    spread_rows = []
    for column_in in columns:
        merged = jnp.dot(column_in, merge_weight, preferred_element_type=jnp.float32).astype(
            jnp.bfloat16
        )
        by_member = merged.reshape(DP_COUNT, CHUNK, -1)
        spread_rows.append(
            jnp.concatenate(
                [lax.dynamic_index_in_dim(by_member, slot_of[d], 0, False) for d in range(8)],
                axis=0,
            )
        )
    text, spread_rows[1] = lax.optimization_barrier((text, spread_rows[1]))
    wholes = [gather_by_ring(rows) for rows in spread_rows]
    gains = attn_gain.reshape(DP_COUNT, 1, -1)
    image_query, image_kv = project(order, wholes, gains, query_weight, kv_weight)
    text = [half.reshape(6, SEQ, -1) for half in (text, swap(text, "c"))]

    sizes = jnp.swapaxes(facts[:, :, :4], 0, 1)
    offsets = jnp.swapaxes(facts[:, :, 4:8], 0, 1)
    starts = jnp.sum(facts[0, :, 8:], axis=0, dtype=jnp.int32)
    positions = row_positions(sizes.reshape(128, 4), offsets.reshape(128, 4), CAPACITY).reshape(
        16, 256
    )
    before = jnp.arange(256)[None, :] < jnp.arange(256)[:, None]
    own_owner = lax.dynamic_index_in_dim(positions, ctx_index, 0, False) // SEQ
    own_rank = jnp.sum(
        ((own_owner[None, :] == own_owner[:, None]) & before).astype(jnp.int32),
        axis=1,
        dtype=jnp.int32,
    )
    own_slot = (own_owner * CAPACITY + own_rank).reshape(8, 2, CHUNK).swapaxes(0, 1).reshape(-1)
    spread_out = (jnp.arange(512, dtype=jnp.int32)[:, None] == own_slot[None, :]).astype(
        jnp.bfloat16
    )
    mine = positions // SEQ == ctx_index
    rank = jnp.sum((mine[:, None, :] & before[None]).astype(jnp.int32), axis=2, dtype=jnp.int32)
    slot_here = mine[:, :, None] & (
        rank[:, :, None] == jnp.arange(CAPACITY, dtype=jnp.int32)[None, None, :]
    )
    slot_place = jnp.sum(
        jnp.where(slot_here, positions[:, :, None] - ctx_index * SEQ + 1, 0),
        axis=1,
        dtype=jnp.int32,
    ).reshape(-1) - 1
    bring_in = jnp.arange(SEQ, dtype=jnp.int32)[:, None] == slot_place[None, :]

    sent = jnp.dot(spread_out, image_query, preferred_element_type=jnp.float32).astype(jnp.bfloat16)
    last = lax.all_to_all(
        jnp.concatenate(
            [
                jnp.broadcast_to(image_kv[None], (CTX_COUNT,) + image_kv.shape),
                sent.reshape(CTX_COUNT, CAPACITY, -1),
            ],
            axis=1,
        ),
        CTX,
        split_axis=0,
        concat_axis=0,
    )

    window_start = jnp.maximum(ctx_index - REACH, 0) * SEQ
    low_rows = (
        jnp.sum(
            jnp.where(
                doc_ids[:, None] == jnp.arange(4, dtype=jnp.int32)[None, :], starts[None, :], 0
            ),
            axis=1,
            dtype=jnp.int32,
        )
        - window_start
    )
    low_rows = jnp.maximum(low_rows, 0)
    edges = low_rows.reshape(-1, QUERY_BLOCK)
    info = jnp.concatenate(
        [
            jnp.stack([window_start, ctx_index * SEQ - window_start]).astype(jnp.int32),
            jnp.stack([edges[:, 0], edges[:, -1]], axis=1).reshape(-1),
        ]
    )
    within_device = starts_within(sizes)
    shard = window_start // SEQ + jnp.arange(REACH + 1, dtype=jnp.int32)
    text_at = (
        ((shard % 2) ^ c_at) * 6
        + jnp.clip(z_at - shard // 4, 0, 2) * 2
        + ((shard // 2 % 2) ^ yl_at)
    )
    image_src = (
        jnp.arange(CTX_COUNT * DP_COUNT, dtype=jnp.int32).reshape(CTX_COUNT, DP_COUNT, 1) * CAPACITY
        + within_device
    )
    targets = (offsets - window_start).reshape(-1)
    inside = (targets >= 0) & (targets < WINDOW)
    tables = (
        info,
        image_src.reshape(-1),
        jnp.where(inside, targets, 0),
        jnp.where(inside, sizes.reshape(-1), 0),
        text_at.astype(jnp.int32),
    )
    return attention(
        tables, text_query, bring_in.astype(jnp.bfloat16), low_rows[None, :], last, text
    )


def solution(mesh):
    fine = Mesh(mesh.devices.reshape(2, 4, 4, 2, 2), DP + CTX)
    every = DP + CTX
    return jax.shard_map(
        body,
        mesh=fine,
        in_specs=(
            P(every, None),
            P(),
            P(),
            P(every, None),
            P(every, None),
            P(),
            P(),
            P(None, DP),
            P(),
            P(None, DP),
            P(None, None, DP),
            P(CTX, DP),
            P(None, CTX, DP),
            P(CTX),
            P(every, None),
            P(every, None),
        ),
        out_specs=P(CTX, DP),
        check_vma=False,
    )
```

```python
import math

import jax
import jax.numpy as jnp
import numpy as np
from jax import lax
from jax.experimental import pallas as pl
from jax.experimental.pallas import tpu as pltpu
from jax.sharding import Mesh
from jax.sharding import PartitionSpec as P

HEAD_DIM = 128
MOST = 16
SEQ = 640
REACH = 8
WINDOW = SEQ * (REACH + 1)
KEY_BLOCK = 640
QUERY_BLOCK = 640
GROUP = 4
IMAGES = 512
PLACE_UNROLL = 4
CAPACITY = 32
CHUNK = 16
UNITS = 24
CTX_COUNT = 16
DP_COUNT = 8

MASKED_SCORE = -1e30
LOWEST_PEAK = -1e29
EPSILON = 1e-06
DP = ("yh", "x")
CTX = ("z", "yl", "c")


def layer_norm(rows_in, norm_gain, norm_bias):
    values = rows_in.astype(jnp.float32)
    center = values - jnp.mean(values, axis=-1, keepdims=True)
    spread = jnp.mean(center * center, axis=-1, keepdims=True)
    return (center * lax.rsqrt(spread + EPSILON) * norm_gain + norm_bias).astype(jnp.bfloat16)


def quick_gelu(values):
    return values * jax.nn.sigmoid(1.702 * values)


def starts_within(sizes):
    count = sizes.shape[-1]
    earlier = jnp.arange(count)[None, :] < jnp.arange(count)[:, None]
    return jnp.sum(jnp.where(earlier, sizes[..., None, :], 0), axis=-1, dtype=jnp.int32)


def row_positions(size_table, offset_table, row_count):
    image_starts = starts_within(size_table)
    image_ends = image_starts + size_table
    within = jnp.arange(row_count, dtype=jnp.int32)[None, :, None]
    inside = (within >= image_starts[:, None, :]) & (within < image_ends[:, None, :])
    placed = offset_table[:, None, :] - image_starts[:, None, :] + within
    return jnp.sum(jnp.where(inside, placed, 0), axis=2, dtype=jnp.int32)


def gather_by_exchange(block, axes, count):
    return lax.all_to_all(
        jnp.broadcast_to(block[None], (count,) + block.shape), axes, split_axis=0, concat_axis=0
    )


def swap(rows, axis):
    return lax.ppermute(rows, axis, [(0, 1), (1, 0)])


def turn(rows, axis, by):
    return lax.ppermute(rows, axis, [(i, (i + by) % 4) for i in range(4)])


def gather_by_ring(block):
    pair = jnp.stack([block, swap(block, "yh")])
    left, right = turn(pair, "x", 1), turn(pair, "x", -1)
    across = jnp.stack([turn(left[0], "x", 1), turn(right[1], "x", -1)])
    return jnp.concatenate([pair, left, right, across], axis=0)


def attention_kernel(
    info,
    image_src,
    image_dst,
    image_len,
    blocks_at,
    text_query_ref,
    bring_ref,
    low_ref,
    last_ref,
    text_near_ref,
    text_far_ref,
    out_ref,
    text_held,
    key_wide,
    value_wide,
    image_key,
    image_value,
    image_query,
    sems,
):
    query_offset = info[1]
    near = text_near_ref.shape[0]
    copies = []
    for shard in range(REACH + 1):
        at = blocks_at[shard]
        target = text_held.at[pl.ds(shard * SEQ, SEQ), :]

        @pl.when(at < near)
        def _(at=at, target=target, shard=shard):
            pltpu.make_async_copy(text_near_ref.at[at], target, sems.at[shard]).start()

        @pl.when(at >= near)
        def _(at=at, target=target, shard=shard):
            pltpu.make_async_copy(text_far_ref.at[at - near], target, sems.at[shard]).start()

        copies.append(pltpu.make_async_copy(text_near_ref.at[0], target, sems.at[shard]))

    def widen_image(source, unused):
        for device in range(DP_COUNT):
            base = source * (DP_COUNT * CAPACITY) + device * CAPACITY
            held = last_ref[source, device * CHUNK : (device + 1) * CHUNK, :].astype(jnp.float32)
            for part in range(2):
                rows = pl.ds(pl.multiple_of(base + part * CHUNK, CHUNK), CHUNK)
                side = part * 2 * HEAD_DIM
                image_key[rows, :] = held[:, side : side + HEAD_DIM]
                image_value[rows, :] = held[:, side + HEAD_DIM : side + 2 * HEAD_DIM]
        rows = pl.ds(pl.multiple_of(source * CAPACITY, CAPACITY), CAPACITY)
        image_query[rows, :] = last_ref[source, DP_COUNT * CHUNK :, :]
        return unused

    lax.fori_loop(0, CTX_COUNT, widen_image, 0)
    for shard in range(REACH + 1):
        copies[shard].wait()

    def widen_text(step, unused):
        rows = pl.ds(pl.multiple_of(step * 320, 320), 320)
        key_wide[rows, :] = text_held[rows, :HEAD_DIM].astype(jnp.float32)
        value_wide[rows, :] = text_held[rows, HEAD_DIM:].astype(jnp.float32)
        return unused

    lax.fori_loop(0, WINDOW // 320, widen_text, 0)
    row_in = lax.broadcasted_iota(jnp.int32, (MOST, HEAD_DIM), 0)

    def place(step, unused):
        for lane in range(PLACE_UNROLL):
            image = step * PLACE_UNROLL + lane
            target = image_dst[image]
            origin = image_src[image]
            taken = row_in < image_len[image]
            rows = pl.ds(target, MOST)
            pltpu.store(key_wide.at[rows, :], image_key[pl.ds(origin, MOST), :], mask=taken)
            pltpu.store(value_wide.at[rows, :], image_value[pl.ds(origin, MOST), :], mask=taken)
        return unused

    lax.fori_loop(0, IMAGES // PLACE_UNROLL, place, 0)

    ones = jnp.ones((CHUNK, KEY_BLOCK), jnp.bfloat16)
    across = GROUP * QUERY_BLOCK
    to_power = math.log2(math.e) / math.sqrt(HEAD_DIM)
    column_at = lax.broadcasted_iota(jnp.int32, (1, QUERY_BLOCK), 1)

    def query_step(block, unused):
        rows = pl.ds(pl.multiple_of(block * QUERY_BLOCK, QUERY_BLOCK), QUERY_BLOCK)
        first = query_offset + block * QUERY_BLOCK
        bring = bring_ref[rows, :]
        is_image = jnp.max(bring.astype(jnp.float32), axis=-1, keepdims=True) > 0.5
        placed = jnp.where(
            is_image,
            jnp.dot(bring, image_query[...], preferred_element_type=jnp.float32),
            text_query_ref[rows, :].astype(jnp.float32),
        )
        queries = jnp.concatenate(
            [placed[:, h * HEAD_DIM : (h + 1) * HEAD_DIM].T for h in range(GROUP)], axis=1
        ).astype(jnp.bfloat16)
        lows = jnp.concatenate([low_ref[:, rows]] * GROUP, axis=1)
        highs = jnp.concatenate([column_at + first] * GROUP, axis=1)
        low_first = info[2 + 2 * block]
        low_last = info[3 + 2 * block]
        begin = low_first // KEY_BLOCK
        end = (first + QUERY_BLOCK - 1) // KEY_BLOCK + 1
        clear_begin = jnp.minimum((low_last + KEY_BLOCK - 1) // KEY_BLOCK, end)
        clear_end = jnp.maximum((first + 1) // KEY_BLOCK, clear_begin)

        def key_step(at, running, masked):
            peak, gathered = running
            keys_at = pl.ds(pl.multiple_of(at * KEY_BLOCK, KEY_BLOCK), KEY_BLOCK)
            scores = jnp.dot(
                key_wide[keys_at, :].astype(jnp.bfloat16),
                queries,
                preferred_element_type=jnp.float32,
            )
            values = jnp.concatenate(
                [value_wide[keys_at, :].T.astype(jnp.bfloat16), ones], axis=0
            )
            if masked:
                place_at = at * KEY_BLOCK + lax.broadcasted_iota(jnp.int32, (KEY_BLOCK, 1), 0)
                scores = jnp.where((place_at >= lows) & (place_at <= highs), scores, MASKED_SCORE)
            new_peak = jnp.maximum(peak, jnp.max(scores, axis=0, keepdims=True))
            weights = jnp.exp2((scores - new_peak) * to_power).astype(jnp.bfloat16)
            rescale = jnp.exp2((peak - new_peak) * to_power)
            gathered = gathered * rescale + jnp.dot(
                values, weights, preferred_element_type=jnp.float32
            )
            return new_peak, gathered

        running = (
            jnp.full((1, across), LOWEST_PEAK, jnp.float32),
            jnp.zeros((HEAD_DIM + CHUNK, across), jnp.float32),
        )
        running = lax.fori_loop(begin, clear_begin, lambda a, r: key_step(a, r, True), running)
        running = lax.fori_loop(clear_begin, clear_end, lambda a, r: key_step(a, r, False), running)
        peak, gathered = lax.fori_loop(clear_end, end, lambda a, r: key_step(a, r, True), running)
        context = gathered[:HEAD_DIM] / gathered[HEAD_DIM : HEAD_DIM + 1]
        for h in range(GROUP):
            out_ref[rows, h * HEAD_DIM : (h + 1) * HEAD_DIM] = context[
                :, h * QUERY_BLOCK : (h + 1) * QUERY_BLOCK
            ].T.astype(jnp.bfloat16)
        return unused

    lax.fori_loop(0, SEQ // QUERY_BLOCK, query_step, 0)


def attention(tables, text_query, bring_in, low_rows, last, text):
    smem = pl.BlockSpec(memory_space=pltpu.SMEM)
    vmem = pl.BlockSpec(memory_space=pltpu.VMEM)
    image_rows = CTX_COUNT * DP_COUNT * CAPACITY
    return pl.pallas_call(
        attention_kernel,
        out_shape=jax.ShapeDtypeStruct(text_query.shape, jnp.bfloat16),
        in_specs=[smem] * 5 + [vmem] * 4 + [pl.BlockSpec(memory_space=pl.ANY)] * 2,
        out_specs=vmem,
        scratch_shapes=[
            pltpu.VMEM((WINDOW, 2 * HEAD_DIM), jnp.bfloat16),
            pltpu.VMEM((WINDOW + MOST, HEAD_DIM), jnp.float32),
            pltpu.VMEM((WINDOW + MOST, HEAD_DIM), jnp.float32),
            pltpu.VMEM((image_rows + MOST, HEAD_DIM), jnp.float32),
            pltpu.VMEM((image_rows + MOST, HEAD_DIM), jnp.float32),
            pltpu.VMEM((CTX_COUNT * CAPACITY, GROUP * HEAD_DIM), jnp.bfloat16),
            pltpu.SemaphoreType.DMA((REACH + 1,)),
        ],
        compiler_params=pltpu.CompilerParams(vmem_limit_bytes=48 * 1024 * 1024),
        cost_estimate=pl.CostEstimate(
            flops=8_000_000_000, bytes_accessed=8_000_000, transcendentals=13_000_000
        ),
    )(*tables, text_query, bring_in, low_rows, last, *text)


def project_kernel(
    order_ref,
    first_ref,
    second_ref,
    gain_ref,
    query_weight_ref,
    kv_weight_ref,
    query_ref,
    kv_ref,
    query_sum,
    kv_sum,
    squares,
):
    step = pl.program_id(0)

    @pl.when(step == 0)
    def _():
        query_sum[...] = jnp.zeros_like(query_sum)
        kv_sum[...] = jnp.zeros_like(kv_sum)
        squares[...] = jnp.zeros_like(squares)

    values = jnp.concatenate([first_ref[0], second_ref[0]], axis=0).astype(jnp.float32)
    squares[...] += jnp.sum(values * values, axis=-1, keepdims=True)
    gained = (values * gain_ref[0]).astype(jnp.bfloat16)
    query_sum[...] += jnp.dot(gained, query_weight_ref[...], preferred_element_type=jnp.float32)
    kv_sum[:, :HEAD_DIM] += jnp.dot(gained, kv_weight_ref[0], preferred_element_type=jnp.float32)
    kv_sum[:, HEAD_DIM:] += jnp.dot(gained, kv_weight_ref[1], preferred_element_type=jnp.float32)

    @pl.when(step == DP_COUNT - 1)
    def _():
        scale = lax.rsqrt(squares[...] / (DP_COUNT * first_ref.shape[2]) + EPSILON)
        query_ref[...] = (query_sum[...] * scale).astype(jnp.bfloat16)
        kv = (kv_sum[...] * scale).astype(jnp.bfloat16)
        half = first_ref.shape[1]
        kv_ref[:, : 2 * HEAD_DIM] = kv[:half]
        kv_ref[:, 2 * HEAD_DIM :] = kv[half:]


def project(order, wholes, gain, query_weight, kv_weight):
    count, rows, part = wholes[0].shape
    query_width, kv_width = query_weight.shape[1], kv_weight.shape[2]
    rows_spec = pl.BlockSpec((1, rows, part), lambda k, order: (k, 0, 0))
    return pl.pallas_call(
        project_kernel,
        grid_spec=pltpu.PrefetchScalarGridSpec(
            num_scalar_prefetch=1,
            grid=(count,),
            in_specs=[
                rows_spec,
                rows_spec,
                pl.BlockSpec((1, 1, part), lambda k, order: (order[k], 0, 0)),
                pl.BlockSpec((part, query_width), lambda k, order: (order[k], 0)),
                pl.BlockSpec((2, part, kv_width), lambda k, order: (0, order[k], 0)),
            ],
            out_specs=(
                pl.BlockSpec((2 * rows, query_width), lambda k, order: (0, 0)),
                pl.BlockSpec((rows, 4 * kv_width), lambda k, order: (0, 0)),
            ),
            scratch_shapes=[
                pltpu.VMEM((2 * rows, query_width), jnp.float32),
                pltpu.VMEM((2 * rows, 2 * kv_width), jnp.float32),
                pltpu.VMEM((2 * rows, 1), jnp.float32),
            ],
        ),
        out_shape=(
            jax.ShapeDtypeStruct((2 * rows, query_width), jnp.bfloat16),
            jax.ShapeDtypeStruct((rows, 4 * kv_width), jnp.bfloat16),
        ),
        compiler_params=pltpu.CompilerParams(vmem_limit_bytes=20 * 1024 * 1024),
        cost_estimate=pl.CostEstimate(
            flops=4 * rows * count * part * (query_width + 2 * kv_width),
            bytes_accessed=2 * count * part * (query_width + 2 * kv_width + 2 * rows),
            transcendentals=0,
        ),
    )(order, *wholes, gain, query_weight, kv_weight)


def body(
    patches,
    vision_gain,
    vision_bias,
    up_weight,
    down_weight,
    merge_gain,
    merge_bias,
    merge_weight,
    attn_gain,
    query_weight,
    kv_weight,
    text_query,
    text_kv,
    doc_ids,
    image_sizes,
    image_offsets,
):
    z_at, yl_at, c_at = lax.axis_index("z"), lax.axis_index("yl"), lax.axis_index("c")
    ctx_index = lax.axis_index(CTX)
    width = patches.shape[1]
    own_rows = patches.shape[0]
    units_own = up_weight.shape[0]

    below = jnp.sum(
        (doc_ids[:, None] < jnp.arange(4, dtype=jnp.int32)[None, :]).astype(jnp.int32),
        axis=0,
        dtype=jnp.int32,
    )
    facts = jnp.concatenate([image_sizes, image_offsets, below[None, :]], axis=1)
    facts = jnp.concatenate([facts // 128, facts % 128], axis=1).astype(jnp.bfloat16)
    fact_count = facts.shape[1]
    block = jnp.concatenate(
        [
            jnp.pad(up_weight, ((0, UNITS - units_own), (0, 0))),
            down_weight,
            jnp.pad(facts, ((0, UNITS - units_own - 1), (0, width - fact_count))),
        ],
        axis=0,
    )
    block = jnp.broadcast_to(block[None], (16,) + block.shape)
    block, patches = lax.optimization_barrier((block, patches))
    units = lax.all_to_all(block, DP + ("yl",), split_axis=0, concat_axis=0)
    text = jnp.concatenate([text_kv[0], text_kv[1]], axis=1)
    text, units = lax.optimization_barrier((text, units))
    text_beside = swap(text, "yl")
    normed = layer_norm(patches, vision_gain, vision_bias)
    column = jnp.concatenate(
        [normed]
        + [
            lax.ppermute(normed, "z", [(i, (i + step) % 4) for i in range(4)])
            for step in (1, 2, 3)
        ],
        axis=0,
    )
    near_rows = column.shape[0]
    near = jnp.concatenate([column, swap(column, "c")], axis=0)
    ups = units[:, :UNITS].reshape(-1, width)
    downs = units[:, UNITS:].reshape(-1, width)
    facts = units[:, UNITS + units_own, :fact_count].reshape(1, -1)
    hidden = quick_gelu(
        lax.dot_general(near, ups, (((1,), (1,)), ((), ())), preferred_element_type=jnp.float32)
    ).astype(jnp.bfloat16)
    away = jnp.dot(hidden[near_rows:], downs, preferred_element_type=jnp.float32).astype(
        jnp.bfloat16
    )
    here = jnp.dot(hidden[:near_rows], downs, preferred_element_type=jnp.float32)
    came = swap(
        jnp.concatenate(
            [away, jnp.pad(facts, ((0, CHUNK - 1), (0, width - facts.shape[1])))], axis=0
        ),
        "c",
    )
    text_beside, came = lax.optimization_barrier((text_beside, came))
    text = jnp.concatenate([text, text_beside], axis=0)
    pair_sum = (here + came[:near_rows].astype(jnp.float32)).astype(jnp.bfloat16)
    other = came[near_rows : near_rows + 1, : facts.shape[1]]
    facts = jnp.concatenate(
        [jnp.where(c_at == 0, facts, other), jnp.where(c_at == 0, other, facts)], axis=1
    )
    tail = jnp.pad(facts, ((0, CHUNK - 1), (0, width - facts.shape[1])))
    by_z = pair_sum.reshape(4, own_rows, width)
    terms = lax.all_to_all(
        jnp.stack(
            [
                jnp.concatenate(
                    [lax.dynamic_index_in_dim(by_z, (z_at - j + 4) % 4, 0, False), tail], axis=0
                )
                for j in range(4)
            ]
        ),
        "z",
        split_axis=0,
        concat_axis=0,
    )
    branch = jnp.sum(terms[:, :own_rows].astype(jnp.float32), axis=0)
    facts = terms[:, own_rows, : facts.shape[1]].astype(jnp.int32)
    facts = facts.reshape(4, 2, 8, 2, fact_count).transpose(2, 0, 3, 1, 4)
    facts = facts.reshape(8, 16, 2, fact_count // 2)
    facts = facts[:, :, 0] * 128 + facts[:, :, 1]
    vision = (patches.astype(jnp.float32) + branch).astype(jnp.bfloat16)
    merged_in = layer_norm(vision, merge_gain, merge_bias).reshape(-1, 4 * width)

    text, merged_in = lax.optimization_barrier((text, merged_in))
    text = jnp.concatenate(
        [
            text,
            lax.ppermute(text, "z", [(0, 1), (1, 2), (2, 3)]),
            lax.ppermute(text, "z", [(0, 2), (1, 3)]),
        ],
        axis=0,
    )
    yh_at, x_at = lax.axis_index("yh"), lax.axis_index("x")
    step = jnp.array([0, 0, 3, 3, 1, 1, 2, 2], jnp.int32)
    order = (yh_at ^ (jnp.arange(8, dtype=jnp.int32) % 2)) * 4 + (x_at + step) % 4
    member = jnp.arange(8, dtype=jnp.int32)
    slot_of = jnp.sum(
        jnp.where(member[:, None] == order[None, :], member[None, :], 0), axis=1, dtype=jnp.int32
    )
    columns = [
        gather_by_ring(merged_in[at : at + CHUNK]).reshape(-1, 4 * width) for at in (0, CHUNK)
    ]
    spread_rows = []
    for column_in in columns:
        merged = jnp.dot(column_in, merge_weight, preferred_element_type=jnp.float32).astype(
            jnp.bfloat16
        )
        by_member = merged.reshape(DP_COUNT, CHUNK, -1)
        spread_rows.append(
            jnp.concatenate(
                [lax.dynamic_index_in_dim(by_member, slot_of[d], 0, False) for d in range(8)],
                axis=0,
            )
        )
    text, spread_rows[1] = lax.optimization_barrier((text, spread_rows[1]))
    wholes = [gather_by_ring(rows) for rows in spread_rows]
    gains = attn_gain.reshape(DP_COUNT, 1, -1)
    image_query, image_kv = project(order, wholes, gains, query_weight, kv_weight)
    text = [half.reshape(6, SEQ, -1) for half in (text, swap(text, "c"))]

    sizes = jnp.swapaxes(facts[:, :, :4], 0, 1)
    offsets = jnp.swapaxes(facts[:, :, 4:8], 0, 1)
    starts = jnp.sum(facts[0, :, 8:], axis=0, dtype=jnp.int32)
    positions = row_positions(sizes.reshape(128, 4), offsets.reshape(128, 4), CAPACITY).reshape(
        16, 256
    )
    before = jnp.arange(256)[None, :] < jnp.arange(256)[:, None]
    own_owner = lax.dynamic_index_in_dim(positions, ctx_index, 0, False) // SEQ
    own_rank = jnp.sum(
        ((own_owner[None, :] == own_owner[:, None]) & before).astype(jnp.int32),
        axis=1,
        dtype=jnp.int32,
    )
    own_slot = (own_owner * CAPACITY + own_rank).reshape(8, 2, CHUNK).swapaxes(0, 1).reshape(-1)
    spread_out = (jnp.arange(512, dtype=jnp.int32)[:, None] == own_slot[None, :]).astype(
        jnp.bfloat16
    )
    mine = positions // SEQ == ctx_index
    rank = jnp.sum((mine[:, None, :] & before[None]).astype(jnp.int32), axis=2, dtype=jnp.int32)
    slot_here = mine[:, :, None] & (
        rank[:, :, None] == jnp.arange(CAPACITY, dtype=jnp.int32)[None, None, :]
    )
    slot_place = jnp.sum(
        jnp.where(slot_here, positions[:, :, None] - ctx_index * SEQ + 1, 0),
        axis=1,
        dtype=jnp.int32,
    ).reshape(-1) - 1
    bring_in = jnp.arange(SEQ, dtype=jnp.int32)[:, None] == slot_place[None, :]

    sent = jnp.dot(spread_out, image_query, preferred_element_type=jnp.float32).astype(jnp.bfloat16)
    last = lax.all_to_all(
        jnp.concatenate(
            [
                jnp.broadcast_to(image_kv[None], (CTX_COUNT,) + image_kv.shape),
                sent.reshape(CTX_COUNT, CAPACITY, -1),
            ],
            axis=1,
        ),
        CTX,
        split_axis=0,
        concat_axis=0,
    )

    window_start = jnp.maximum(ctx_index - REACH, 0) * SEQ
    low_rows = (
        jnp.sum(
            jnp.where(
                doc_ids[:, None] == jnp.arange(4, dtype=jnp.int32)[None, :], starts[None, :], 0
            ),
            axis=1,
            dtype=jnp.int32,
        )
        - window_start
    )
    low_rows = jnp.maximum(low_rows, 0)
    edges = low_rows.reshape(-1, QUERY_BLOCK)
    info = jnp.concatenate(
        [
            jnp.stack([window_start, ctx_index * SEQ - window_start]).astype(jnp.int32),
            jnp.stack([edges[:, 0], edges[:, -1]], axis=1).reshape(-1),
        ]
    )
    within_device = starts_within(sizes)
    shard = window_start // SEQ + jnp.arange(REACH + 1, dtype=jnp.int32)
    text_at = (
        ((shard % 2) ^ c_at) * 6
        + jnp.clip(z_at - shard // 4, 0, 2) * 2
        + ((shard // 2 % 2) ^ yl_at)
    )
    image_src = (
        jnp.arange(CTX_COUNT * DP_COUNT, dtype=jnp.int32).reshape(CTX_COUNT, DP_COUNT, 1) * CAPACITY
        + within_device
    )
    targets = (offsets - window_start).reshape(-1)
    inside = (targets >= 0) & (targets < WINDOW)
    tables = (
        info,
        image_src.reshape(-1),
        jnp.where(inside, targets, 0),
        jnp.where(inside, sizes.reshape(-1), 0),
        text_at.astype(jnp.int32),
    )
    return attention(
        tables, text_query, bring_in.astype(jnp.bfloat16), low_rows[None, :], last, text
    )


def solution(mesh):
    fine = Mesh(mesh.devices.reshape(2, 4, 4, 2, 2), DP + CTX)
    every = DP + CTX
    return jax.shard_map(
        body,
        mesh=fine,
        in_specs=(
            P(every, None),
            P(),
            P(),
            P(every, None),
            P(every, None),
            P(),
            P(),
            P(None, DP),
            P(),
            P(None, DP),
            P(None, None, DP),
            P(CTX, DP),
            P(None, CTX, DP),
            P(CTX),
            P(every, None),
            P(every, None),
        ),
        out_specs=P(CTX, DP),
        check_vma=False,
    )
```

```python
import math

import jax
import jax.numpy as jnp
import numpy as np
from jax import lax
from jax.experimental import pallas as pl
from jax.experimental.pallas import tpu as pltpu
from jax.sharding import Mesh
from jax.sharding import PartitionSpec as P

HEAD_DIM = 128
MOST = 16
SEQ = 640
REACH = 8
WINDOW = SEQ * (REACH + 1)
KEY_BLOCK = 640
QUERY_BLOCK = 640
GROUP = 4
IMAGES = 512
PLACE_UNROLL = 8
CAPACITY = 32
CHUNK = 16
UNITS = 24
CTX_COUNT = 16
DP_COUNT = 8

MASKED_SCORE = -1e30
LOWEST_PEAK = -1e29
EPSILON = 1e-06
DP = ("yh", "x")
CTX = ("z", "yl", "c")


def layer_norm(rows_in, norm_gain, norm_bias):
    values = rows_in.astype(jnp.float32)
    center = values - jnp.mean(values, axis=-1, keepdims=True)
    spread = jnp.mean(center * center, axis=-1, keepdims=True)
    return (center * lax.rsqrt(spread + EPSILON) * norm_gain + norm_bias).astype(jnp.bfloat16)


def quick_gelu(values):
    return values * jax.nn.sigmoid(1.702 * values)


def starts_within(sizes):
    count = sizes.shape[-1]
    earlier = jnp.arange(count)[None, :] < jnp.arange(count)[:, None]
    return jnp.sum(jnp.where(earlier, sizes[..., None, :], 0), axis=-1, dtype=jnp.int32)


def row_positions(size_table, offset_table, row_count):
    image_starts = starts_within(size_table)
    image_ends = image_starts + size_table
    within = jnp.arange(row_count, dtype=jnp.int32)[None, :, None]
    inside = (within >= image_starts[:, None, :]) & (within < image_ends[:, None, :])
    placed = offset_table[:, None, :] - image_starts[:, None, :] + within
    return jnp.sum(jnp.where(inside, placed, 0), axis=2, dtype=jnp.int32)


def gather_by_exchange(block, axes, count):
    return lax.all_to_all(
        jnp.broadcast_to(block[None], (count,) + block.shape), axes, split_axis=0, concat_axis=0
    )


def swap(rows, axis):
    return lax.ppermute(rows, axis, [(0, 1), (1, 0)])


def turn(rows, axis, by):
    return lax.ppermute(rows, axis, [(i, (i + by) % 4) for i in range(4)])


def gather_by_ring(block):
    pair = jnp.stack([block, swap(block, "yh")])
    left, right = turn(pair, "x", 1), turn(pair, "x", -1)
    across = jnp.stack([turn(left[0], "x", 1), turn(right[1], "x", -1)])
    return jnp.concatenate([pair, left, right, across], axis=0)


def attention_kernel(
    info,
    image_src,
    image_dst,
    image_len,
    blocks_at,
    text_query_ref,
    bring_ref,
    low_ref,
    last_ref,
    text_near_ref,
    text_far_ref,
    out_ref,
    text_held,
    key_wide,
    value_wide,
    image_key,
    image_value,
    image_query,
    sems,
):
    query_offset = info[1]
    near = text_near_ref.shape[0]
    copies = []
    for shard in range(REACH + 1):
        at = blocks_at[shard]
        target = text_held.at[pl.ds(shard * SEQ, SEQ), :]

        @pl.when(at < near)
        def _(at=at, target=target, shard=shard):
            pltpu.make_async_copy(text_near_ref.at[at], target, sems.at[shard]).start()

        @pl.when(at >= near)
        def _(at=at, target=target, shard=shard):
            pltpu.make_async_copy(text_far_ref.at[at - near], target, sems.at[shard]).start()

        copies.append(pltpu.make_async_copy(text_near_ref.at[0], target, sems.at[shard]))

    def widen_image(source, unused):
        for device in range(DP_COUNT):
            base = source * (DP_COUNT * CAPACITY) + device * CAPACITY
            held = last_ref[source, device * CHUNK : (device + 1) * CHUNK, :].astype(jnp.float32)
            for part in range(2):
                rows = pl.ds(pl.multiple_of(base + part * CHUNK, CHUNK), CHUNK)
                side = part * 2 * HEAD_DIM
                image_key[rows, :] = held[:, side : side + HEAD_DIM]
                image_value[rows, :] = held[:, side + HEAD_DIM : side + 2 * HEAD_DIM]
        rows = pl.ds(pl.multiple_of(source * CAPACITY, CAPACITY), CAPACITY)
        image_query[rows, :] = last_ref[source, DP_COUNT * CHUNK :, :]
        return unused

    lax.fori_loop(0, CTX_COUNT, widen_image, 0)
    for shard in range(REACH + 1):
        copies[shard].wait()

    def widen_text(step, unused):
        rows = pl.ds(pl.multiple_of(step * 320, 320), 320)
        key_wide[rows, :] = text_held[rows, :HEAD_DIM].astype(jnp.float32)
        value_wide[rows, :] = text_held[rows, HEAD_DIM:].astype(jnp.float32)
        return unused

    lax.fori_loop(info[2] // SEQ * 2, (query_offset // SEQ + 1) * 2, widen_text, 0)
    row_in = lax.broadcasted_iota(jnp.int32, (MOST, HEAD_DIM), 0)

    def place(step, unused):
        for lane in range(PLACE_UNROLL):
            image = step * PLACE_UNROLL + lane
            target = image_dst[image]
            origin = image_src[image]
            taken = row_in < image_len[image]
            rows = pl.ds(target, MOST)
            pltpu.store(key_wide.at[rows, :], image_key[pl.ds(origin, MOST), :], mask=taken)
            pltpu.store(value_wide.at[rows, :], image_value[pl.ds(origin, MOST), :], mask=taken)
        return unused

    lax.fori_loop(0, IMAGES // PLACE_UNROLL, place, 0)

    ones = jnp.ones((CHUNK, KEY_BLOCK), jnp.bfloat16)
    across = GROUP * QUERY_BLOCK
    to_power = math.log2(math.e) / math.sqrt(HEAD_DIM)
    column_at = lax.broadcasted_iota(jnp.int32, (1, QUERY_BLOCK), 1)

    def query_step(block, unused):
        rows = pl.ds(pl.multiple_of(block * QUERY_BLOCK, QUERY_BLOCK), QUERY_BLOCK)
        first = query_offset + block * QUERY_BLOCK
        bring = bring_ref[rows, :]
        is_image = jnp.max(bring.astype(jnp.float32), axis=-1, keepdims=True) > 0.5
        placed = jnp.where(
            is_image,
            jnp.dot(bring, image_query[...], preferred_element_type=jnp.float32),
            text_query_ref[rows, :].astype(jnp.float32),
        )
        queries = jnp.concatenate(
            [placed[:, h * HEAD_DIM : (h + 1) * HEAD_DIM].T for h in range(GROUP)], axis=1
        ).astype(jnp.bfloat16)
        lows = jnp.concatenate([low_ref[:, rows]] * GROUP, axis=1)
        highs = jnp.concatenate([column_at + first] * GROUP, axis=1)
        low_first = info[2 + 2 * block]
        low_last = info[3 + 2 * block]
        begin = low_first // KEY_BLOCK
        end = (first + QUERY_BLOCK - 1) // KEY_BLOCK + 1
        clear_begin = jnp.minimum((low_last + KEY_BLOCK - 1) // KEY_BLOCK, end)
        clear_end = jnp.maximum((first + 1) // KEY_BLOCK, clear_begin)

        def key_step(at, running, masked):
            peak, gathered = running
            keys_at = pl.ds(pl.multiple_of(at * KEY_BLOCK, KEY_BLOCK), KEY_BLOCK)
            scores = jnp.dot(
                key_wide[keys_at, :].astype(jnp.bfloat16),
                queries,
                preferred_element_type=jnp.float32,
            )
            values = jnp.concatenate(
                [value_wide[keys_at, :].T.astype(jnp.bfloat16), ones], axis=0
            )
            if masked:
                place_at = at * KEY_BLOCK + lax.broadcasted_iota(jnp.int32, (KEY_BLOCK, 1), 0)
                scores = jnp.where((place_at >= lows) & (place_at <= highs), scores, MASKED_SCORE)
            new_peak = jnp.maximum(peak, jnp.max(scores, axis=0, keepdims=True))
            weights = jnp.exp2((scores - new_peak) * to_power).astype(jnp.bfloat16)
            rescale = jnp.exp2((peak - new_peak) * to_power)
            gathered = gathered * rescale + jnp.dot(
                values, weights, preferred_element_type=jnp.float32
            )
            return new_peak, gathered

        running = (
            jnp.full((1, across), LOWEST_PEAK, jnp.float32),
            jnp.zeros((HEAD_DIM + CHUNK, across), jnp.float32),
        )
        running = lax.fori_loop(begin, clear_begin, lambda a, r: key_step(a, r, True), running)
        running = lax.fori_loop(clear_begin, clear_end, lambda a, r: key_step(a, r, False), running)
        peak, gathered = lax.fori_loop(clear_end, end, lambda a, r: key_step(a, r, True), running)
        context = gathered[:HEAD_DIM] / gathered[HEAD_DIM : HEAD_DIM + 1]
        for h in range(GROUP):
            out_ref[rows, h * HEAD_DIM : (h + 1) * HEAD_DIM] = context[
                :, h * QUERY_BLOCK : (h + 1) * QUERY_BLOCK
            ].T.astype(jnp.bfloat16)
        return unused

    lax.fori_loop(0, SEQ // QUERY_BLOCK, query_step, 0)


def attention(tables, text_query, bring_in, low_rows, last, text):
    smem = pl.BlockSpec(memory_space=pltpu.SMEM)
    vmem = pl.BlockSpec(memory_space=pltpu.VMEM)
    image_rows = CTX_COUNT * DP_COUNT * CAPACITY
    return pl.pallas_call(
        attention_kernel,
        out_shape=jax.ShapeDtypeStruct(text_query.shape, jnp.bfloat16),
        in_specs=[smem] * 5 + [vmem] * 4 + [pl.BlockSpec(memory_space=pl.ANY)] * 2,
        out_specs=vmem,
        scratch_shapes=[
            pltpu.VMEM((WINDOW, 2 * HEAD_DIM), jnp.bfloat16),
            pltpu.VMEM((WINDOW + MOST, HEAD_DIM), jnp.float32),
            pltpu.VMEM((WINDOW + MOST, HEAD_DIM), jnp.float32),
            pltpu.VMEM((image_rows + MOST, HEAD_DIM), jnp.float32),
            pltpu.VMEM((image_rows + MOST, HEAD_DIM), jnp.float32),
            pltpu.VMEM((CTX_COUNT * CAPACITY, GROUP * HEAD_DIM), jnp.bfloat16),
            pltpu.SemaphoreType.DMA((REACH + 1,)),
        ],
        compiler_params=pltpu.CompilerParams(vmem_limit_bytes=48 * 1024 * 1024),
        cost_estimate=pl.CostEstimate(
            flops=8_000_000_000, bytes_accessed=8_000_000, transcendentals=13_000_000
        ),
    )(*tables, text_query, bring_in, low_rows, last, *text)


def project_kernel(
    order_ref,
    first_ref,
    second_ref,
    gain_ref,
    query_weight_ref,
    kv_weight_ref,
    query_ref,
    kv_ref,
    query_sum,
    kv_sum,
    squares,
):
    step = pl.program_id(0)

    @pl.when(step == 0)
    def _():
        query_sum[...] = jnp.zeros_like(query_sum)
        kv_sum[...] = jnp.zeros_like(kv_sum)
        squares[...] = jnp.zeros_like(squares)

    values = jnp.concatenate([first_ref[0], second_ref[0]], axis=0).astype(jnp.float32)
    squares[...] += jnp.sum(values * values, axis=-1, keepdims=True)
    gained = (values * gain_ref[0]).astype(jnp.bfloat16)
    query_sum[...] += jnp.dot(gained, query_weight_ref[...], preferred_element_type=jnp.float32)
    kv_sum[:, :HEAD_DIM] += jnp.dot(gained, kv_weight_ref[0], preferred_element_type=jnp.float32)
    kv_sum[:, HEAD_DIM:] += jnp.dot(gained, kv_weight_ref[1], preferred_element_type=jnp.float32)

    @pl.when(step == DP_COUNT - 1)
    def _():
        scale = lax.rsqrt(squares[...] / (DP_COUNT * first_ref.shape[2]) + EPSILON)
        query_ref[...] = (query_sum[...] * scale).astype(jnp.bfloat16)
        kv = (kv_sum[...] * scale).astype(jnp.bfloat16)
        half = first_ref.shape[1]
        kv_ref[:, : 2 * HEAD_DIM] = kv[:half]
        kv_ref[:, 2 * HEAD_DIM :] = kv[half:]


def project(order, wholes, gain, query_weight, kv_weight):
    count, rows, part = wholes[0].shape
    query_width, kv_width = query_weight.shape[1], kv_weight.shape[2]
    rows_spec = pl.BlockSpec((1, rows, part), lambda k, order: (k, 0, 0))
    return pl.pallas_call(
        project_kernel,
        grid_spec=pltpu.PrefetchScalarGridSpec(
            num_scalar_prefetch=1,
            grid=(count,),
            in_specs=[
                rows_spec,
                rows_spec,
                pl.BlockSpec((1, 1, part), lambda k, order: (order[k], 0, 0)),
                pl.BlockSpec((part, query_width), lambda k, order: (order[k], 0)),
                pl.BlockSpec((2, part, kv_width), lambda k, order: (0, order[k], 0)),
            ],
            out_specs=(
                pl.BlockSpec((2 * rows, query_width), lambda k, order: (0, 0)),
                pl.BlockSpec((rows, 4 * kv_width), lambda k, order: (0, 0)),
            ),
            scratch_shapes=[
                pltpu.VMEM((2 * rows, query_width), jnp.float32),
                pltpu.VMEM((2 * rows, 2 * kv_width), jnp.float32),
                pltpu.VMEM((2 * rows, 1), jnp.float32),
            ],
        ),
        out_shape=(
            jax.ShapeDtypeStruct((2 * rows, query_width), jnp.bfloat16),
            jax.ShapeDtypeStruct((rows, 4 * kv_width), jnp.bfloat16),
        ),
        compiler_params=pltpu.CompilerParams(vmem_limit_bytes=20 * 1024 * 1024),
        cost_estimate=pl.CostEstimate(
            flops=4 * rows * count * part * (query_width + 2 * kv_width),
            bytes_accessed=2 * count * part * (query_width + 2 * kv_width + 2 * rows),
            transcendentals=0,
        ),
    )(order, *wholes, gain, query_weight, kv_weight)


def body(
    patches,
    vision_gain,
    vision_bias,
    up_weight,
    down_weight,
    merge_gain,
    merge_bias,
    merge_weight,
    attn_gain,
    query_weight,
    kv_weight,
    text_query,
    text_kv,
    doc_ids,
    image_sizes,
    image_offsets,
):
    z_at, yl_at, c_at = lax.axis_index("z"), lax.axis_index("yl"), lax.axis_index("c")
    ctx_index = lax.axis_index(CTX)
    width = patches.shape[1]
    own_rows = patches.shape[0]
    units_own = up_weight.shape[0]

    below = jnp.sum(
        (doc_ids[:, None] < jnp.arange(4, dtype=jnp.int32)[None, :]).astype(jnp.int32),
        axis=0,
        dtype=jnp.int32,
    )
    facts = jnp.concatenate([image_sizes, image_offsets, below[None, :]], axis=1)
    facts = jnp.concatenate([facts // 128, facts % 128], axis=1).astype(jnp.bfloat16)
    fact_count = facts.shape[1]
    block = jnp.concatenate(
        [
            jnp.pad(up_weight, ((0, UNITS - units_own), (0, 0))),
            down_weight,
            jnp.pad(facts, ((0, UNITS - units_own - 1), (0, width - fact_count))),
        ],
        axis=0,
    )
    block = jnp.broadcast_to(block[None], (16,) + block.shape)
    block, patches = lax.optimization_barrier((block, patches))
    units = lax.all_to_all(block, DP + ("yl",), split_axis=0, concat_axis=0)
    text = jnp.concatenate([text_kv[0], text_kv[1]], axis=1)
    text, units = lax.optimization_barrier((text, units))
    text_beside = swap(text, "yl")
    normed = layer_norm(patches, vision_gain, vision_bias)
    column = jnp.concatenate(
        [normed]
        + [
            lax.ppermute(normed, "z", [(i, (i + step) % 4) for i in range(4)])
            for step in (1, 2, 3)
        ],
        axis=0,
    )
    near_rows = column.shape[0]
    near = jnp.concatenate([column, swap(column, "c")], axis=0)
    ups = units[:, :UNITS].reshape(-1, width)
    downs = units[:, UNITS:].reshape(-1, width)
    facts = units[:, UNITS + units_own, :fact_count].reshape(1, -1)
    hidden = quick_gelu(
        lax.dot_general(near, ups, (((1,), (1,)), ((), ())), preferred_element_type=jnp.float32)
    ).astype(jnp.bfloat16)
    away = jnp.dot(hidden[near_rows:], downs, preferred_element_type=jnp.float32).astype(
        jnp.bfloat16
    )
    here = jnp.dot(hidden[:near_rows], downs, preferred_element_type=jnp.float32)
    came = swap(
        jnp.concatenate(
            [away, jnp.pad(facts, ((0, CHUNK - 1), (0, width - facts.shape[1])))], axis=0
        ),
        "c",
    )
    text_beside, came = lax.optimization_barrier((text_beside, came))
    text = jnp.concatenate([text, text_beside], axis=0)
    pair_sum = (here + came[:near_rows].astype(jnp.float32)).astype(jnp.bfloat16)
    other = came[near_rows : near_rows + 1, : facts.shape[1]]
    facts = jnp.concatenate(
        [jnp.where(c_at == 0, facts, other), jnp.where(c_at == 0, other, facts)], axis=1
    )
    tail = jnp.pad(facts, ((0, CHUNK - 1), (0, width - facts.shape[1])))
    by_z = pair_sum.reshape(4, own_rows, width)
    terms = lax.all_to_all(
        jnp.stack(
            [
                jnp.concatenate(
                    [lax.dynamic_index_in_dim(by_z, (z_at - j + 4) % 4, 0, False), tail], axis=0
                )
                for j in range(4)
            ]
        ),
        "z",
        split_axis=0,
        concat_axis=0,
    )
    branch = jnp.sum(terms[:, :own_rows].astype(jnp.float32), axis=0)
    facts = terms[:, own_rows, : facts.shape[1]].astype(jnp.int32)
    facts = facts.reshape(4, 2, 8, 2, fact_count).transpose(2, 0, 3, 1, 4)
    facts = facts.reshape(8, 16, 2, fact_count // 2)
    facts = facts[:, :, 0] * 128 + facts[:, :, 1]
    vision = (patches.astype(jnp.float32) + branch).astype(jnp.bfloat16)
    merged_in = layer_norm(vision, merge_gain, merge_bias).reshape(-1, 4 * width)

    text, merged_in = lax.optimization_barrier((text, merged_in))
    text = jnp.concatenate(
        [
            text,
            lax.ppermute(text, "z", [(0, 1), (1, 2), (2, 3)]),
            lax.ppermute(text, "z", [(0, 2), (1, 3)]),
        ],
        axis=0,
    )
    yh_at, x_at = lax.axis_index("yh"), lax.axis_index("x")
    step = jnp.array([0, 0, 3, 3, 1, 1, 2, 2], jnp.int32)
    order = (yh_at ^ (jnp.arange(8, dtype=jnp.int32) % 2)) * 4 + (x_at + step) % 4
    member = jnp.arange(8, dtype=jnp.int32)
    slot_of = jnp.sum(
        jnp.where(member[:, None] == order[None, :], member[None, :], 0), axis=1, dtype=jnp.int32
    )
    columns = [
        gather_by_ring(merged_in[at : at + CHUNK]).reshape(-1, 4 * width) for at in (0, CHUNK)
    ]
    spread_rows = []
    for column_in in columns:
        merged = jnp.dot(column_in, merge_weight, preferred_element_type=jnp.float32).astype(
            jnp.bfloat16
        )
        by_member = merged.reshape(DP_COUNT, CHUNK, -1)
        spread_rows.append(
            jnp.concatenate(
                [lax.dynamic_index_in_dim(by_member, slot_of[d], 0, False) for d in range(8)],
                axis=0,
            )
        )
    text, spread_rows[1] = lax.optimization_barrier((text, spread_rows[1]))
    wholes = [gather_by_ring(rows) for rows in spread_rows]
    gains = attn_gain.reshape(DP_COUNT, 1, -1)
    image_query, image_kv = project(order, wholes, gains, query_weight, kv_weight)
    text = [half.reshape(6, SEQ, -1) for half in (text, swap(text, "c"))]

    sizes = jnp.swapaxes(facts[:, :, :4], 0, 1)
    offsets = jnp.swapaxes(facts[:, :, 4:8], 0, 1)
    starts = jnp.sum(facts[0, :, 8:], axis=0, dtype=jnp.int32)
    positions = row_positions(sizes.reshape(128, 4), offsets.reshape(128, 4), CAPACITY).reshape(
        16, 256
    )
    before = jnp.arange(256)[None, :] < jnp.arange(256)[:, None]
    own_owner = lax.dynamic_index_in_dim(positions, ctx_index, 0, False) // SEQ
    own_rank = jnp.sum(
        ((own_owner[None, :] == own_owner[:, None]) & before).astype(jnp.int32),
        axis=1,
        dtype=jnp.int32,
    )
    own_slot = (own_owner * CAPACITY + own_rank).reshape(8, 2, CHUNK).swapaxes(0, 1).reshape(-1)
    spread_out = (jnp.arange(512, dtype=jnp.int32)[:, None] == own_slot[None, :]).astype(
        jnp.bfloat16
    )
    mine = positions // SEQ == ctx_index
    rank = jnp.sum((mine[:, None, :] & before[None]).astype(jnp.int32), axis=2, dtype=jnp.int32)
    slot_here = mine[:, :, None] & (
        rank[:, :, None] == jnp.arange(CAPACITY, dtype=jnp.int32)[None, None, :]
    )
    slot_place = jnp.sum(
        jnp.where(slot_here, positions[:, :, None] - ctx_index * SEQ + 1, 0),
        axis=1,
        dtype=jnp.int32,
    ).reshape(-1) - 1
    bring_in = jnp.arange(SEQ, dtype=jnp.int32)[:, None] == slot_place[None, :]

    sent = jnp.dot(spread_out, image_query, preferred_element_type=jnp.float32).astype(jnp.bfloat16)
    last = lax.all_to_all(
        jnp.concatenate(
            [
                jnp.broadcast_to(image_kv[None], (CTX_COUNT,) + image_kv.shape),
                sent.reshape(CTX_COUNT, CAPACITY, -1),
            ],
            axis=1,
        ),
        CTX,
        split_axis=0,
        concat_axis=0,
    )

    window_start = jnp.maximum(ctx_index - REACH, 0) * SEQ
    low_rows = (
        jnp.sum(
            jnp.where(
                doc_ids[:, None] == jnp.arange(4, dtype=jnp.int32)[None, :], starts[None, :], 0
            ),
            axis=1,
            dtype=jnp.int32,
        )
        - window_start
    )
    low_rows = jnp.maximum(low_rows, 0)
    edges = low_rows.reshape(-1, QUERY_BLOCK)
    info = jnp.concatenate(
        [
            jnp.stack([window_start, ctx_index * SEQ - window_start]).astype(jnp.int32),
            jnp.stack([edges[:, 0], edges[:, -1]], axis=1).reshape(-1),
        ]
    )
    within_device = starts_within(sizes)
    shard = window_start // SEQ + jnp.arange(REACH + 1, dtype=jnp.int32)
    text_at = (
        ((shard % 2) ^ c_at) * 6
        + jnp.clip(z_at - shard // 4, 0, 2) * 2
        + ((shard // 2 % 2) ^ yl_at)
    )
    image_src = (
        jnp.arange(CTX_COUNT * DP_COUNT, dtype=jnp.int32).reshape(CTX_COUNT, DP_COUNT, 1) * CAPACITY
        + within_device
    )
    targets = (offsets - window_start).reshape(-1)
    inside = (targets >= 0) & (targets < WINDOW)
    tables = (
        info,
        image_src.reshape(-1),
        jnp.where(inside, targets, 0),
        jnp.where(inside, sizes.reshape(-1), 0),
        text_at.astype(jnp.int32),
    )
    return attention(
        tables, text_query, bring_in.astype(jnp.bfloat16), low_rows[None, :], last, text
    )


def solution(mesh):
    fine = Mesh(mesh.devices.reshape(2, 4, 4, 2, 2), DP + CTX)
    every = DP + CTX
    return jax.shard_map(
        body,
        mesh=fine,
        in_specs=(
            P(every, None),
            P(),
            P(),
            P(every, None),
            P(every, None),
            P(),
            P(),
            P(None, DP),
            P(),
            P(None, DP),
            P(None, None, DP),
            P(CTX, DP),
            P(None, CTX, DP),
            P(CTX),
            P(every, None),
            P(every, None),
        ),
        out_specs=P(CTX, DP),
        check_vma=False,
    )
```
